32 devices in a mesh: wide: 8 (over y, x, core), narrow: 4 (over z).
Axes of the slice: x: 2, y: 2, z: 4, core: 2. Of those that a mesh axis runs over, the one named last changes fastest.
Arguments:
- tokens: bfloat16 [128, 157, 768], P(('wide', 'narrow')), may hold values from -6 to 6
- out_grad: bfloat16 [128, 157, 768], P(('wide', 'narrow')), may hold values from -6 to 6
- first_gain: bfloat16 [768], P('wide'), may hold values from 0.25 to 2.7, as said below
- first_shift: bfloat16 [768], P('wide'), may hold values from -3 to 3
- qkv_weight: bfloat16 [768, 2304], P('wide'), may hold values from -0.21875 to 0.21875
- query_bias: bfloat16 [768], P('wide'), may hold values from -3 to 3
- value_bias: bfloat16 [768], P('wide'), may hold values from -3 to 3
- proj_weight: bfloat16 [768, 768], P('wide'), may hold values from -1.75 to 1.75
- proj_bias: bfloat16 [768], P('wide'), may hold values from -3 to 3
- second_gain: bfloat16 [768], P('wide'), may hold values from 0.25 to 2.7, as said below
- second_shift: bfloat16 [768], P('wide'), may hold values from -3 to 3
- expand_weight: bfloat16 [768, 3072], P('wide'), may hold values from -0.21875 to 0.21875
- expand_bias: bfloat16 [3072], P('wide'), may hold values from -3 to 3
- shrink_weight: bfloat16 [3072, 768], P('wide'), may hold values from -0.109375 to 0.109375
- shrink_bias: bfloat16 [768], P('wide'), may hold values from -3 to 3
Outputs:
- block_out: bfloat16 [128, 157, 768], P(('wide', 'narrow'))
- tokens_grad: float32 [128, 157, 768], P(('wide', 'narrow'))
- grad_first_gain: float32 [768], P('wide')
- grad_first_shift: float32 [768], P('wide')
- grad_qkv_weight: float32 [768, 2304], P('wide')
- grad_query_bias: float32 [768], P('wide')
- grad_value_bias: float32 [768], P('wide')
- grad_proj_weight: float32 [768, 768], P('wide')
- grad_proj_bias: float32 [768], P('wide')
- grad_second_gain: float32 [768], P('wide')
- grad_second_shift: float32 [768], P('wide')
- grad_expand_weight: float32 [768, 3072], P('wide')
- grad_expand_bias: float32 [3072], P('wide')
- grad_shrink_weight: float32 [3072, 768], P('wide')
- grad_shrink_bias: float32 [768], P('wide')
- grad_sq_norm: float32 [], replicated
The draws below stay inside these ranges and needn't reach their ends.
Inputs may be any that keep to these rules, and one draw needn't show every extreme that they name: `first_gain`: positive per-feature gains. `second_gain`: positive per-feature gains.
All inputs are finite; a program needn't handle non-finite values.
Results may differ from the reference program's by a relative error of at most 0.018.
Values may be sent and summed in bfloat16 or wider, within the bound.
No kernel may reach another device: no remote copies, remote signals or barrier semaphores. Data moves between devices by JAX's collectives and lax.ppermute only.
A program may use at most 192 MiB of HBM per device.

```python
import jax
import jax.numpy as jnp
from jax import lax

D = 768
HEADS = 12
FF = 3072
SEQ = 157
CLIPS = 128


def rising_gain(key, start, noise_low, noise_high):
    position = jnp.arange(D).astype(jnp.float32) / (D - 1)
    noise = jax.random.uniform(key, (D,), jnp.float32, noise_low, noise_high)
    return (start + position) * noise


def draw_first_gain(key, part):
    key = jax.random.fold_in(key, 11)
    return rising_gain(key, 0.5, 0.8, 1.2).astype(jnp.bfloat16)


def draw_second_gain(key, part):
    key = jax.random.fold_in(key, 23)
    return rising_gain(key, 0.5, 0.8, 1.2).astype(jnp.bfloat16)


def level_of(stream_key, shape, pieces, low, largest):
    factor_of = 1.0
    for dim, blocks in pieces:
        draws = jax.random.uniform(jax.random.fold_in(jax.random.fold_in(stream_key, 6), dim), (blocks,), jnp.float32, low / len(pieces), largest / len(pieces))
        factor_of = factor_of * jnp.repeat(jnp.exp(draws), shape[dim] // blocks).reshape((-1,) + (1,) * (len(shape) - 1 - dim))
    return factor_of


def centred(own_key, shape, scale, limit, pieces=(), held_as=jnp.bfloat16):
    values = scale * jax.random.normal(own_key, shape, jnp.float32)
    if pieces:
        values = values * level_of(own_key, shape, pieces, -0.22, 0.18)
    return jnp.clip(values, -limit, limit).astype(held_as)


def setup_inputs(seed: int = 0) -> dict:
    arg_keys = jax.random.split(jax.random.key(seed), 16)
    tokens = centred(arg_keys[0], (CLIPS, SEQ, D), 1.0, 6.0, ((0, 32),))
    out_grad = centred(arg_keys[1], (CLIPS, SEQ, D), 1.0, 6.0, ((0, 32),))
    first_gain = draw_first_gain(jax.random.fold_in(arg_keys[15], 71), 0)
    first_shift = centred(arg_keys[3], (D,), 0.5, 3.0, ((0, 8),))
    qkv_weight = centred(arg_keys[4], (D, 3 * D), D ** -0.5, 0.21875, ((0, 8),))
    query_bias = centred(arg_keys[5], (D,), 0.5, 3.0, ((0, 8),))
    value_bias = centred(arg_keys[6], (D,), 0.5, 3.0, ((0, 8),))
    proj_weight = centred(arg_keys[7], (D, D), (max(D // 64, 8)) ** -0.5, 1.75, ((0, 8),))
    proj_bias = centred(arg_keys[8], (D,), 0.5, 3.0, ((0, 8),))
    second_gain = draw_second_gain(jax.random.fold_in(arg_keys[15], 71), 0)
    second_shift = centred(arg_keys[10], (D,), 0.5, 3.0, ((0, 8),))
    expand_weight = centred(arg_keys[11], (D, FF), D ** -0.5, 0.21875, ((0, 8),))
    expand_bias = centred(arg_keys[12], (FF,), 0.5, 3.0, ((0, 8),))
    shrink_weight = centred(arg_keys[13], (FF, D), FF ** -0.5, 0.109375, ((0, 8),))
    shrink_bias = centred(arg_keys[14], (D,), 0.5, 3.0, ((0, 8),))
    return {"tokens": tokens, "out_grad": out_grad, "first_gain": first_gain, "first_shift": first_shift, "qkv_weight": qkv_weight, "query_bias": query_bias, "value_bias": value_bias, "proj_weight": proj_weight, "proj_bias": proj_bias, "second_gain": second_gain, "second_shift": second_shift, "expand_weight": expand_weight, "expand_bias": expand_bias, "shrink_weight": shrink_weight, "shrink_bias": shrink_bias}


EPS = 1e-06
HIGH = lax.Precision.HIGHEST

@jax.custom_vjp
def low(v):
    return lax.optimization_barrier(v.astype(jnp.bfloat16)).astype(jnp.float32)

@jax.custom_vjp
def low_back(v):
    return v

def low_keep(v):
    return (low(v), None)

def low_pass(kept, grad):
    return (grad,)

def back_keep(v):
    return (v, None)

def back_low(kept, grad):
    return (low(grad),)
low.defvjp(low_keep, low_pass)
low_back.defvjp(back_keep, back_low)

def layer_norm(values, gain, shift):
    mean_row = lax.optimization_barrier(jnp.mean(values, axis=-1, keepdims=True))
    centered = values - mean_row
    spread = lax.optimization_barrier(jnp.mean(centered * centered, axis=-1, keepdims=True))
    return centered * lax.rsqrt(spread + EPS) * gain + shift

def gelu_exact(values):
    return jax.nn.gelu(values, approximate=False)

def forward(inputs, params):
    gain_one, shift_one, attn_weight, qbias_full, vbias_full, out_weight, out_shift, gain_two, shift_two, up_weight, up_shift, down_weight, down_shift = params
    clips, length, width = inputs.shape
    head_dim = width // HEADS
    normed_one = low(layer_norm(inputs, gain_one, shift_one))
    bias_row = jnp.concatenate([qbias_full, jnp.zeros((width,), jnp.float32), vbias_full])
    mixed = low(low_back(jnp.einsum('csd,de->cse', normed_one, attn_weight, precision=HIGH) + bias_row))
    queries = mixed[:, :, :width].reshape(clips, length, HEADS, head_dim)
    keys = mixed[:, :, width:2 * width].reshape(clips, length, HEADS, head_dim)
    values = mixed[:, :, 2 * width:].reshape(clips, length, HEADS, head_dim)
    scores = low_back(jnp.einsum('cqhe,ckhe->chqk', queries, keys, precision=HIGH) * head_dim ** (-0.5))
    probs = low(jax.nn.softmax(scores, axis=-1))
    attended = jnp.einsum('chqk,ckhe->cqhe', probs, values, precision=HIGH).reshape(clips, length, width)
    attended = low(low_back(attended))
    attn_out = low_back(jnp.einsum('csd,de->cse', attended, out_weight, precision=HIGH) + out_shift)
    middle = inputs + attn_out
    normed_two = low(layer_norm(middle, gain_two, shift_two))
    hidden_pre = low_back(jnp.einsum('csd,df->csf', normed_two, up_weight, precision=HIGH) + up_shift)
    hidden_low = low(gelu_exact(hidden_pre))
    branch = low_back(jnp.einsum('csf,fd->csd', hidden_low, down_weight, precision=HIGH) + down_shift)
    return middle + branch

def add_pair(first, second):
    return first + second

def reference(tokens, out_grad, first_gain, first_shift, qkv_weight, query_bias, value_bias, proj_weight, proj_bias, second_gain, second_shift, expand_weight, expand_bias, shrink_weight, shrink_bias):
    params = tuple((item.astype(jnp.float32) for item in (first_gain, first_shift, qkv_weight, query_bias, value_bias, proj_weight, proj_bias, second_gain, second_shift, expand_weight, expand_bias, shrink_weight, shrink_bias)))
    group = min(16, CLIPS)
    blocks = CLIPS // group
    tok_blocks = tokens.astype(jnp.float32).reshape(blocks, group, SEQ, D)
    grad_blocks = out_grad.astype(jnp.float32).reshape(blocks, group, SEQ, D)

    def step(totals, pair):
        tok_block, grad_block = pair
        result, pullback = jax.vjp(forward, tok_block, params)
        grad_tokens, grad_params = pullback(grad_block)
        totals = jax.tree.map(add_pair, totals, grad_params)
        return (totals, (result.astype(jnp.bfloat16), grad_tokens))
    zeros_start = jax.tree.map(jnp.zeros_like, params)
    totals, (outputs, grads) = lax.scan(step, zeros_start, (tok_blocks, grad_blocks))
    g_gain_one, g_shift_one, g_attn, g_qbias, g_vbias, g_out, g_out_shift, g_gain_two, g_shift_two, g_up, g_up_shift, g_down, g_down_shift = totals
    squares = jnp.zeros((), jnp.float32)
    for item in totals:
        squares = squares + jnp.sum(item * item)
    return (outputs.reshape(CLIPS, SEQ, D), grads.reshape(CLIPS, SEQ, D), g_gain_one, g_shift_one, g_attn, g_qbias, g_vbias, g_out, g_out_shift, g_gain_two, g_shift_two, g_up, g_up_shift, g_down, g_down_shift, squares)
```

```python
import functools

import jax
import jax.numpy as jnp
from jax import lax
from jax.experimental import pallas as pl
from jax.experimental.pallas import tpu as pltpu
from jax.sharding import PartitionSpec as P

HEADS = 12
EPS = 1e-06
BLOCKS = 8
HALF = BLOCKS // 2
SMALL = 128
MIB = 1024 * 1024

f32 = jnp.float32
bf16 = jnp.bfloat16

ANY = pl.BlockSpec(memory_space=pl.ANY)
HBM = pl.BlockSpec(memory_space=pltpu.HBM)
FULL = pl.BlockSpec(memory_space=pltpu.VMEM)
SCALAR = pl.BlockSpec(memory_space=pltpu.SMEM)


def nn(a, b):
    return lax.dot_general(a, b, (((1,), (0,)), ((), ())), preferred_element_type=f32)


def nt(a, b):
    return lax.dot_general(a, b, (((1,), (1,)), ((), ())), preferred_element_type=f32)


def tn(a, b):
    return lax.dot_general(a, b, (((0,), (0,)), ((), ())), preferred_element_type=f32)


def normalise(values):
    mean_row = jnp.mean(values, axis=-1, keepdims=True)
    centered = values - mean_row
    spread = jnp.mean(centered * centered, axis=-1, keepdims=True)
    inverse = lax.rsqrt(spread + EPS)
    return centered * inverse, inverse


def norm_back(grad, normed, inverse):
    first = jnp.mean(grad, axis=-1, keepdims=True)
    second = jnp.mean(grad * normed, axis=-1, keepdims=True)
    return inverse * (grad - first - normed * second)


def gelu_both(values):
    cdf = 0.5 * (1.0 + lax.erf(values * (0.5**0.5)))
    density = 0.3989422804014327 * jnp.exp(-0.5 * values * values)
    return values * cdf, cdf + values * density


def sems(count):
    return pltpu.SemaphoreType.DMA((count,))


def start_all(pairs, sem, first=0):
    copies = [pltpu.make_async_copy(a, b, sem.at[first + k]) for k, (a, b) in enumerate(pairs)]
    for copy in copies:
        copy.start()
    return copies


def wait_all(copies):
    for copy in copies:
        copy.wait()


def rows_in_order(idx, pieces, target, columns=None):
    for i, piece in enumerate(pieces):
        count = piece.shape[0]
        rows = pl.ds(pl.multiple_of(idx[i] * count, 16), count)
        for source, to, size in columns or [(0, 0, piece.shape[1])]:
            target[rows, to : to + size] = piece[:, source : source + size]


def columns_by_place(idx, pieces, target, tile, places):
    for i, piece in enumerate(pieces):
        count = piece.shape[0]
        rows = pl.ds(pl.multiple_of(idx[i] * count, 16), count)
        for k, place in enumerate(places):
            source = pl.ds(pl.multiple_of(idx[place] * tile, 128), tile)
            target[rows, k * tile : (k + 1) * tile] = piece[:, source]


def rows_by_place(idx, target, value):
    part = value.shape[0] // BLOCKS
    for b in range(BLOCKS):
        to = pl.multiple_of(idx[BLOCKS + b] * part, 16)
        target[pl.ds(to, part)] = value[b * part : (b + 1) * part]


def beside(one, two):
    return jnp.concatenate([one[...], two[...]], axis=1)


def below(one, two):
    return jnp.concatenate([one[...], two[...]], axis=0)


def lanes_of(head_dim):
    return lax.broadcasted_iota(jnp.int32, (1, 2 * head_dim), 1) < head_dim


def stack_pair(pair, left):
    zero = jnp.zeros_like(pair)
    return jnp.concatenate([jnp.where(left, pair, zero), jnp.where(left, zero, pair)], axis=0)


def merge_pair(stacked, left):
    half = stacked.shape[0] // 2
    return jnp.where(left, stacked[:half], stacked[half:])


KERNELS = {
    "attention_forward": (0.01, 28),
    "proj_forward": (0.01, 16),
    "expand_first": (10, 16),
    "expand_second": (25, 16),
    "shrink_weight_grad": (5, 16),
    "hidden_back": (14, 16),
    "middle_back": (45, 28),
    "expand_weight_grad": (14, 16),
    "heads_back": (20, 16),
    "attention_weight_grad": (20, 16),
    "last_weight_grad": (10, 12),
    "input_sums": (10, 20),
    "shrink_forward": (8, 16),
    "input_back": (8, 12),
    "combine": (0.5, 12),
}
SCALE = 1.0


class Far:
    def __init__(self, array):
        self.array = array

    def operand(self):
        return pltpu.with_memory_space_constraint(self.array, pltpu.HBM)

    def result(self):
        return pltpu.HBM(self.array.shape, self.array.dtype)


TOKEN = jax.ShapeDtypeStruct((8, 128), f32)


def call(kernel, name, out_shape, scratch, inputs, after=()):
    given, skip, many = len(inputs), len(after), len(out_shape)
    specs = [HBM if isinstance(a, Far) else SCALAR if a.dtype == jnp.int32 else FULL for a in inputs]
    outs = [HBM if isinstance(o, Far) else FULL for o in out_shape] + [FULL]
    micros, mib = KERNELS[name]

    def run(*refs):
        token = refs[given + skip + many]
        token[...] = jnp.zeros(token.shape, f32)
        kernel(*refs[:given], *refs[given + skip : given + skip + many], *refs[given + skip + many + 1 :])

    return pl.pallas_call(
        run,
        out_shape=[o.result() if isinstance(o, Far) else o for o in out_shape] + [TOKEN],
        in_specs=specs + [FULL if a.shape == TOKEN.shape else ANY for a in after],
        out_specs=outs,
        scratch_shapes=scratch,
        compiler_params=pltpu.CompilerParams(vmem_limit_bytes=mib * MIB),
        cost_estimate=pl.CostEstimate(
            flops=int(micros * SCALE * 1e9), bytes_accessed=0, transcendentals=0
        ),
        name=name,
    )(*[a.operand() if isinstance(a, Far) else a for a in inputs], *after)


def combine(sums, after=()):
    arrays = [a for terms in sums for a in terms]

    def kernel(*refs):
        at = 0
        for terms, out in zip(sums, refs[len(arrays) :]):
            total = refs[at][...].astype(f32)
            for k in range(1, len(terms)):
                total = total + refs[at + k][...].astype(f32)
            out[...] = total.astype(out.dtype)
            at += len(terms)

    shapes = [jax.ShapeDtypeStruct(terms[0].shape, terms[0].dtype) for terms in sums]
    return call(kernel, "combine", shapes, [], arrays, after)


def tie(values, after):
    def nothing(*refs):
        pass

    n = len(values)
    return pl.pallas_call(
        nothing,
        out_shape=[jax.ShapeDtypeStruct(v.shape, v.dtype) for v in values],
        in_specs=[ANY] * n + [FULL if a.shape == TOKEN.shape else ANY for a in after],
        out_specs=[ANY] * n,
        input_output_aliases={i: i for i in range(n)},
        compiler_params=pltpu.CompilerParams(vmem_limit_bytes=MIB),
        name="tie",
    )(*values, *after)


def turn(idx, value, target, k, send_o, keep_o):
    rows_by_place(idx, target, value.T)
    half = target.shape[0] // 2
    send_o[k * half : (k + 1) * half] = target[:half]
    keep_o[k * half : (k + 1) * half] = target[half:]


def attention_forward(clips, rows, seq, idx, x_ref, *refs):
    pieces, others = refs[:BLOCKS], refs[BLOCKS : 2 * BLOCKS]
    attended, send_o, keep_o, mixed_o, probs_o, small_o, up_shift_o = refs[2 * BLOCKS : 2 * BLOCKS + 7]
    weights_o, near_proj_o, proj_o, weights, small_block, mixed, probs_all, turned, sem = refs[2 * BLOCKS + 7 :]
    width = x_ref.shape[1]
    pair = 2 * (width // HEADS)
    rows_in_order(idx, pieces, weights)
    rows_in_order(idx, others, small_block, [(width, 0, SMALL)])
    rows_in_order(idx, others, near_proj_o, [(0, 0, width)])
    gone = start_all([(weights, weights_o), (near_proj_o, proj_o)], sem, 3)
    normed, inverse = normalise(x_ref[...].astype(f32))
    small = small_block[...].astype(f32).T
    small_o[...] = small[:16]
    up = [small[8 + k : 9 + k] for k in range(4)]
    part = width // BLOCKS
    for s in range(BLOCKS):
        up_shift_o[s] = jnp.concatenate([u[:, part * s : part * (s + 1)] for u in up], axis=1)
    n1 = (normed * small[0:1] + small[1:2]).astype(bf16)
    for t in range(3):
        acc = nn(n1, weights[:, width * t : width * (t + 1)])
        if t == 0:
            acc = acc + small[2:3]
        if t == 2:
            acc = acc + small[3:4]
        mixed[:, width * t : width * (t + 1)] = acc.astype(bf16)
    gone += start_all([(mixed, mixed_o)], sem)
    turn(idx, n1, turned, 0, send_o, keep_o)
    left = lanes_of(width // HEADS)
    valid = lax.broadcasted_iota(jnp.int32, (1, rows), 1) < seq
    scale = (width // HEADS) ** (-0.5)

    def heads(p, carry):
        lane = pl.multiple_of(p * pair, pair)
        for c in range(clips):
            here = pl.ds(c * rows, rows)
            q = mixed[here, pl.ds(lane, pair)]
            k = mixed[here, pl.ds(lane + width, pair)]
            v = mixed[here, pl.ds(lane + 2 * width, pair)]
            scores = nt(stack_pair(q, left), k) * scale
            scores = jnp.where(valid, scores, -1e30)
            peak = jnp.max(scores, axis=-1, keepdims=True)
            raised = jnp.exp(scores - peak)
            total = jnp.sum(raised, axis=-1, keepdims=True)
            probs = (raised * (1.0 / total)).astype(bf16)
            probs_all[p * clips + c] = probs
            attended[here, pl.ds(lane, pair)] = merge_pair(nn(probs, v), left).astype(bf16)
        return carry

    half = HEADS // 4
    for h in range(2):
        lax.fori_loop(h * half, (h + 1) * half, heads, 0)
        at = pl.ds(h * half * clips, half * clips)
        gone += start_all([(probs_all.at[at], probs_o.at[at])], sem, 1 + h)
    wait_all(gone)


def proj_forward(
    idx, x_ref, attended, small, weights, n1_send, n1_keep, middle_o, n2_o, send_o, keep_o, middle, turned, sem
):
    half = n1_send.shape[0]
    send_o[:half] = n1_send[...]
    keep_o[:half] = n1_keep[...]
    att = attended[...]
    value = x_ref[...].astype(f32) + (nn(att, weights[...]) + small[4:5])
    middle[...] = value
    gone = start_all([(middle, middle_o)], sem)
    turn(idx, att, turned.at[0], 1, send_o, keep_o)
    normed, inverse = normalise(value)
    n2 = (normed * small[5:6] + small[6:7]).astype(bf16)
    n2_o[...] = n2
    turn(idx, n2, turned.at[1], 2, send_o, keep_o)
    wait_all(gone)


def expand_tiles(start, idx, n2_ref, shift_ref, weights, hidden_o, slope_o, hidden_far, pre, sem, at):
    width = n2_ref.shape[1]
    step = 256
    gone = []

    def multiply(t, c):
        cols = slice(c * step, (c + 1) * step)
        pre[t, :, cols] = nn(n2_ref[...], weights[t, :, cols])

    for c in range(width // step):
        multiply(0, c)
    for t in range(2):
        shift = jnp.concatenate([shift_ref[idx[2 * (start + t) + k]] for k in range(2)], axis=1)
        for c in range(width // step):
            cols = slice(c * step, (c + 1) * step)
            if t == 0:
                multiply(1, c)
            act, derivative = gelu_both(pre[t, :, cols] + shift[:, cols])
            hidden_o[t, :, cols] = act.astype(bf16)
            slope_o[t, :, cols] = derivative.astype(bf16)
        gone += start_all([(hidden_o.at[t], hidden_far.at[t])], sem, at + t)
    return gone


def expand_first(idx, n2_ref, shift_ref, *refs):
    pieces = refs[:BLOCKS]
    hidden_o, slope_o, two_o, hidden_far, up_far, one, pre, sem = refs[BLOCKS:]
    tile = n2_ref.shape[1] // 2
    for t in range(2):
        columns_by_place(idx, pieces, one.at[t], tile, (2 * t, 2 * t + 1))
    gone = start_all([(one, up_far.at[pl.ds(0, 2)])], sem)
    gone += expand_tiles(0, idx, n2_ref, shift_ref, one, hidden_o, slope_o, hidden_far, pre, sem, 2)
    for t in range(2):
        columns_by_place(idx, pieces, two_o.at[t], tile, (2 * t + 4, 2 * t + 5))
    gone += start_all([(two_o, up_far.at[pl.ds(2, 2)])], sem, 1)
    wait_all(gone)


def expand_second(idx, n2_ref, shift_ref, two, hidden_o, slope_o, hidden_far, pre, sem):
    wait_all(expand_tiles(2, idx, n2_ref, shift_ref, two, hidden_o, slope_o, hidden_far, pre, sem, 0))


def shrink_weight_grad(ogt, ogt_sibling, own, sibling, *outs):
    left = beside(ogt, ogt_sibling)
    for t in range(2):
        grad = nn(left, below(own.at[t], sibling.at[t])).astype(bf16)
        tile = grad.shape[1] // 2
        for k in range(2):
            outs[2 * t + k][...] = grad[:, k * tile : (k + 1) * tile]


def expand_weight_grad(idx, own_left, sibling_left, own, sibling, *outs):
    half = own_left.shape[0] // 3
    part = half // HALF
    at = pl.ds(2 * half, half)
    left = beside(own_left.at[at], sibling_left.at[at])
    for t in range(4):
        grad = nn(left, below(own.at[t], sibling.at[(t + 2) % 4])).astype(bf16)
        tile = grad.shape[1] // 2
        for k in range(2):
            to = pl.multiple_of(idx[2 * t + k] * tile, 128)
            for b in range(HALF):
                outs[b][:, pl.ds(to, tile)] = grad[b * part : (b + 1) * part, k * tile : (k + 1) * tile]


def rows_out(grad, outs, columns):
    part = grad.shape[0] // HALF
    for b in range(HALF):
        outs[b][:, columns] = grad[b * part : (b + 1) * part].astype(bf16)


def attention_weight_grad(own_left, sibling_left, own_low, sibling_low, own_mixed, sibling_mixed, *outs):
    width = own_low.shape[1]
    half = width // 2
    for k, right, columns in (
        (1, below(own_low, sibling_low), slice(0, width)),
        (0, below(own_mixed, sibling_mixed), slice(width, None)),
    ):
        at = pl.ds(k * half, half)
        rows_out(nn(beside(own_left.at[at], sibling_left.at[at]), right), outs, columns)


def last_weight_grad(own_left, sibling_left, own_mixed, sibling_mixed, *outs):
    at = pl.ds(0, own_left.shape[0] // 3)
    left = beside(own_left.at[at], sibling_left.at[at])
    rows_out(nn(left, below(own_mixed, sibling_mixed)), outs, slice(None))


def hidden_back(idx, og_ref, slope_one, slope_two, *refs):
    down_pieces, (grad_pre, sums_o, down_far, sem) = refs[:BLOCKS], refs[BLOCKS:]
    tile = down_pieces[0].shape[0]
    pairs = [(piece, down_far.at[i // 2, pl.ds(i % 2 * tile, tile)]) for i, piece in enumerate(down_pieces)]
    gone = start_all(pairs, sem)
    for t in range(grad_pre.shape[0]):
        down = below(down_pieces[2 * t], down_pieces[2 * t + 1])
        slope = (slope_one if t < 2 else slope_two)[t % 2]
        gp = (nt(og_ref[...], down) * slope.astype(f32)).astype(bf16)
        grad_pre[t] = gp
        sums = jnp.sum(gp.astype(f32), axis=0, keepdims=True)
        for k in range(2):
            sums_o[idx[2 * t + k]] = sums[:, k * tile : (k + 1) * tile]
    wait_all(gone)


def middle_back(og_ref, small_ref, weights_ref, middle_ref, up_ref, grad_pre, *refs):
    grad_middle_o, low_o, grad_att_o, vectors_o, up, weights, middle, grad_middle, sem = refs
    up_here = [start_all([(up_ref.at[t], up.at[t])], sem, t) for t in range(4)]
    here = start_all([(middle_ref, middle), (weights_ref, weights)], sem, 4)
    gn2 = None
    for t in range(4):
        wait_all(up_here[t])
        more = nt(grad_pre[t], up[t])
        gn2 = more if gn2 is None else gn2 + more
    wait_all(here)
    normed, inverse = normalise(middle[...])
    og = og_ref[...].astype(f32)
    value = og + norm_back(gn2 * small_ref[5:6], normed, inverse)
    grad_middle[...] = value
    gone = start_all([(grad_middle, grad_middle_o)], sem, 6)
    low = value.astype(bf16)
    low_o[...] = low
    grad_att_o[...] = nt(low, weights[...]).astype(bf16)
    vectors_o[0:1] = jnp.sum(low.astype(f32), axis=0, keepdims=True)
    vectors_o[1:2] = jnp.sum(gn2 * normed, axis=0, keepdims=True)
    vectors_o[2:3] = jnp.sum(gn2, axis=0, keepdims=True)
    vectors_o[3:4] = jnp.sum(og, axis=0, keepdims=True)
    wait_all(gone)


def heads_back(half, clips, rows, grad_att, mixed_ref, probs_ref, grad_mixed_o, mixed, probs_all, sem):
    width = grad_att.shape[1]
    group = width // 2
    head_dim = width // HEADS
    pair = 2 * head_dim
    count = group // pair
    left = lanes_of(head_dim)
    scale = head_dim ** (-0.5)
    arrived = []
    for p in range(count):
        at = half * group + p * pair
        pairs = [
            (mixed_ref.at[:, pl.ds(k * width + at, pair)], mixed.at[:, pl.ds(k * group + p * pair, pair)])
            for k in range(3)
        ]
        source = pl.ds((half * count + p) * clips, clips)
        pairs.append((probs_ref.at[source], probs_all.at[pl.ds(p * clips, clips)]))
        arrived.append(start_all(pairs, sem, 4 * p))
    for p in range(count):
        wait_all(arrived[p])
        lanes = slice(p * pair, (p + 1) * pair)
        for c in range(clips):
            here = pl.ds(c * rows, rows)
            q, k, v = (mixed[here, t * group + p * pair : t * group + (p + 1) * pair] for t in range(3))
            low_probs = probs_all[p * clips + c]
            probs = low_probs.astype(f32)
            at = half * group + p * pair
            grad = stack_pair(grad_att[here, at : at + pair], left)
            grad_probs = nt(grad, v)
            inner = jnp.sum(probs * grad_probs, axis=-1, keepdims=True)
            grad_scores = (probs * (grad_probs - inner)).astype(bf16)
            gq = merge_pair(nn(grad_scores, k), left) * scale
            gk = tn(grad_scores, stack_pair(q, left)) * scale
            gv = tn(low_probs, grad)
            for t, value in enumerate((gq, gk, gv)):
                grad_mixed_o[here, t * group + p * pair : t * group + (p + 1) * pair] = value.astype(bf16)


def input_sums(first, second, x_ref, vectors_ref, sums_ref, weights_ref, gn1_o, vectors_o, weights, gn1_all, sem):
    width = x_ref.shape[1]
    group = width // 2
    part = width // BLOCKS
    here = []
    for g in range(2):
        pairs = []
        for k in range(3):
            source = weights_ref.at[:, pl.ds(k * width + g * group, group)]
            pairs.append((source, weights.at[g, :, pl.ds(k * group, group)]))
        here.append(start_all(pairs, sem, 1 + 3 * g))
    normed, inverse = normalise(x_ref[...].astype(f32))

    def sum_of(ref, k):
        return jnp.sum(ref[:, k * group : (k + 1) * group].astype(f32), axis=0, keepdims=True)

    vectors_o[2:3] = jnp.concatenate([sum_of(first, 0), sum_of(second, 0)], axis=1)
    vectors_o[3:4] = jnp.concatenate([sum_of(first, 2), sum_of(second, 2)], axis=1)
    vectors_o[4:8] = vectors_ref[0:4]
    for k in range(4):
        vectors_o[8 + k : 9 + k] = jnp.concatenate(
            [sums_ref[s][:, part * k : part * (k + 1)] for s in range(BLOCKS)], axis=1
        )
    vectors_o[12:] = jnp.zeros((4, width), f32)
    gn1 = None
    for g, grad in enumerate((first, second)):
        wait_all(here[g])
        more = nt(grad[...], weights[g])
        gn1 = more if gn1 is None else gn1 + more
    gn1_all[...] = gn1
    gone = start_all([(gn1_all, gn1_o)], sem)
    vectors_o[0:1] = jnp.sum(gn1 * normed, axis=0, keepdims=True)
    vectors_o[1:2] = jnp.sum(gn1, axis=0, keepdims=True)
    wait_all(gone)


def shrink_forward(start, clips, rows, seq, small_ref, hidden_ref, base_ref, down_ref, out_o, hidden, base, down, sem):
    here = []
    for t in range(2):
        here.append(start_all([(down_ref.at[start + t], down.at[t]), (hidden_ref.at[t], hidden.at[t])], sem, 2 * t))
    base_here = start_all([(base_ref, base)], sem, 4)
    total = None
    for t in range(2):
        wait_all(here[t])
        more = nn(hidden[t], down[t])
        total = more if total is None else total + more
    wait_all(base_here)
    total = total + base[...]
    if start == 0:
        out_o[...] = total + small_ref[7:8]
    else:
        for c in range(clips):
            out_o[:, c, :] = total[c * rows : c * rows + seq].astype(bf16)


def input_back(clips, rows, seq, gn1_ref, middle_ref, x_ref, small_ref, out_o):
    normed, inverse = normalise(x_ref[...].astype(f32))
    grad = middle_ref[...] + norm_back(gn1_ref[...] * small_ref[0:1], normed, inverse)
    for c in range(clips):
        out_o[:, c, :] = grad[c * rows : c * rows + seq]


def cores(values):
    return lax.ppermute(values, "wide", [(i, i ^ 1) for i in range(BLOCKS)])


def near(values):
    return lax.ppermute(values, "wide", [(i, i ^ (4 if i & 1 else 2)) for i in range(BLOCKS)])


def across(values):
    return lax.ppermute(values, "wide", [(i, i ^ 6) for i in range(BLOCKS)])


def cross(values):
    return lax.ppermute(values, "wide", [(i, i ^ (2 if i & 1 else 4)) for i in range(BLOCKS)])


class Scatter:
    def __init__(self, blocks, forward):
        self.far, self.other, self.first, self.own = blocks
        self.forward = forward
        if forward:
            self.came_far, self.came_other = cross(self.far), cross(self.other)
        else:
            self.send_first(self.first)
            self.came_far, self.came_other = across(self.far), cross(self.other)

    def pass_on(self):
        return [self.first, self.came_far]

    def send_first(self, first):
        self.came_first = near(first)

    def total(self):
        terms = [self.own, self.came_other, self.came_first]
        return terms if self.forward else terms + [self.came_far]


class Fold:
    def __init__(self, values):
        self.perms = [[(0, 1), (3, 2)], [(1, 2), (2, 1)], [(1, 0), (2, 3)]]
        self.send(values)

    def send(self, values):
        self.values = values
        self.came = lax.ppermute(values, "narrow", self.perms.pop(0))

    def terms(self):
        return [self.values, self.came]

    def result(self):
        place = lax.axis_index("narrow")
        return jnp.where((place == 1) | (place == 2), self.values, self.came)


class Gather:
    def __init__(self, own):
        self.own, self.first, self.other = own, near(own), cross(own)

    def forward(self, after):
        (self.first,) = tie([self.first], after)
        self.far = cross(self.first)

    def parts(self, after=()):
        mine = [self.far, self.other, self.first]
        if after:
            mine = list(tie(mine, after))
        mine.append(self.own)
        return [cores(m) for m in mine] + mine


class Everywhere:
    def __init__(self, value):
        self.hops = [("wide", b, BLOCKS) for b in (1, 2, 4)] + [("narrow", b, 4) for b in (1, 2)]
        self.send(value)

    def send(self, value):
        self.value = value
        if self.hops:
            axis, bit, count = self.hops.pop(0)
            self.came = lax.ppermute(value, axis, [(i, i ^ bit) for i in range(count)])

    def terms(self):
        return [self.value, self.came]


def spread(whole):
    return list(jnp.split(whole, BLOCKS, axis=0))


def reduce_plain(whole):
    return lax.psum(lax.psum_scatter(whole, "wide", scatter_dimension=0, tiled=True), "narrow")


def body(
    fast,
    tokens,
    out_grad,
    first_gain,
    first_shift,
    qkv_weight,
    query_bias,
    value_bias,
    proj_weight,
    proj_bias,
    second_gain,
    second_shift,
    expand_weight,
    expand_bias,
    shrink_weight,
    shrink_bias,
):
    clips, seq, width = tokens.shape
    rows = -(-seq // 16) * 16
    flat = clips * rows
    part = width // BLOCKS
    hidden = 4 * width
    tile = hidden // BLOCKS
    tiles = hidden // width
    group = width // 2
    pairs = HEADS // 2 * clips
    first_cols = width + 3 * group
    second_cols = 3 * group
    own = first_gain.shape[0]
    gather_plain = functools.partial(lax.all_gather, axis_name="wide", axis=0, tiled=True)

    def shape(*dims, dtype=bf16):
        return jax.ShapeDtypeStruct(dims, dtype)

    def vmem(*dims, dtype=bf16):
        return pltpu.VMEM(dims, dtype)

    if fast:
        me = lax.axis_index("wide")
        odd = me % 2
        relative = [
            jnp.where(odd == 1, b, a) for a, b in zip((7, 3, 5, 1, 6, 4, 2, 0), (7, 5, 3, 1, 6, 2, 4, 0))
        ]
        order = jnp.stack(relative) ^ me
        where = jnp.sum(
            jnp.where(order[None, :] == jnp.arange(BLOCKS)[:, None], jnp.arange(BLOCKS)[None, :], 0),
            axis=1,
        )
        idx = jnp.concatenate([order, where]).astype(jnp.int32)
    else:
        idx = jnp.concatenate([jnp.arange(BLOCKS), jnp.arange(BLOCKS)]).astype(jnp.int32)

    vectors = [
        first_gain,
        first_shift,
        query_bias,
        value_bias,
        proj_bias,
        second_gain,
        second_shift,
        shrink_bias,
    ]
    block = jnp.concatenate([jnp.stack(vectors), expand_bias.reshape(4, own)], axis=0).T
    block = jnp.pad(block, ((0, 0), (0, SMALL - block.shape[1])))
    packed = jnp.concatenate([proj_weight, block], axis=1)
    pad = ((0, 0), (0, rows - seq), (0, 0))
    x = jnp.pad(tokens, pad).reshape(flat, width)
    og = jnp.pad(out_grad, pad).reshape(flat, width)
    ogt = og.T

    after = []
    if fast:
        qkv, proj = Gather(qkv_weight), Gather(packed)
        up, down = Gather(expand_weight), Gather(shrink_weight)
        qkv.forward([x, ogt, idx])
        proj.forward([x, ogt, idx])
        qkv_parts, proj_parts = qkv.parts(), proj.parts()
    else:
        qkv_parts = spread(gather_plain(qkv_weight))
        up_parts = spread(gather_plain(expand_weight))
        down_parts = spread(gather_plain(shrink_weight))
        whole = gather_plain(packed)
        bias = whole[:, width + 8 : width + 12].reshape(width // own, own, 4)
        bias = bias.transpose(0, 2, 1).reshape(BLOCKS, 4, part).transpose(0, 2, 1).reshape(width, 4)
        proj_parts = spread(whole.at[:, width + 8 : width + 12].set(bias))

    def sibling(array):
        return cores(array) if fast else jnp.zeros_like(array)

    ogt_sibling = sibling(ogt)
    attended, n1_send, n1_keep, mixed, probs, small, up_shift, w_qkv, near_proj, w_proj, token = call(
        functools.partial(attention_forward, clips, rows, seq),
        "attention_forward",
        (
            shape(flat, width),
            shape(width // 2, flat),
            shape(width // 2, flat),
            Far(shape(flat, 3 * width)),
            Far(shape(pairs, 2 * rows, rows)),
            shape(16, width, dtype=f32),
            shape(BLOCKS, 1, tile, dtype=f32),
            Far(shape(width, 3 * width)),
            shape(width, width),
            Far(shape(width, width)),
        ),
        [vmem(width, 3 * width), vmem(width, SMALL), vmem(flat, 3 * width), vmem(pairs, 2 * rows, rows), vmem(width, flat), sems(5)],
        [idx, x, *qkv_parts, *proj_parts],
    )
    if fast:
        up.forward([token])
    middle, n2, turned_send, turned_keep, token = call(
        proj_forward,
        "proj_forward",
        (Far(shape(flat, width, dtype=f32)), shape(flat, width), *([shape(3 * width // 2, flat)] * 2)),
        [vmem(flat, width, dtype=f32), vmem(2, width, flat), sems(1)],
        [idx, x, attended, small, near_proj, n1_send, n1_keep],
    )
    turned_sibling = sibling(turned_send)
    after = []
    if fast:
        up_parts = up.parts([token])
        down.forward([token])
        after = [down.first]

    two_tiles = (shape(2, flat, width), shape(2, flat, width))
    hidden_one, slope_one, up_two, hidden_one_far, up_far, token = call(
        expand_first,
        "expand_first",
        (
            *two_tiles,
            shape(2, width, width),
            Far(shape(2, flat, width)),
            Far(shape(4, width, width)),
        ),
        [vmem(2, width, width), vmem(2, flat, width, dtype=f32), sems(4)],
        [idx, n2, up_shift, *up_parts],
        after,
    )
    hidden_sibling = sibling(hidden_one)
    hidden_two, slope_two, hidden_two_far, token = call(
        expand_second,
        "expand_second",
        (*two_tiles, Far(shape(2, flat, width))),
        [vmem(2, flat, width, dtype=f32), sems(2)],
        [idx, n2, up_shift, up_two],
        [token, turned_sibling],
    )

    def shrink_grad(own_hidden, sibling_hidden):
        return call(
            shrink_weight_grad,
            "shrink_weight_grad",
            [shape(width, tile)] * HALF,
            [],
            [ogt, ogt_sibling, own_hidden, sibling_hidden],
        )

    *down_blocks, token = shrink_grad(hidden_two, hidden_sibling)
    if fast:
        down_sum = Scatter(down_blocks, True)
        down_parts = down.parts([token])
    grad_pre, sums, down_far, token = call(
        hidden_back,
        "hidden_back",
        [shape(tiles, flat, width), shape(BLOCKS, 1, tile, dtype=f32), Far(shape(tiles, width, width))],
        [sems(BLOCKS)],
        [idx, og, slope_one, slope_two, *down_parts],
    )
    grad_pre_sibling = sibling(grad_pre)
    if fast:
        first, token = combine([down_sum.pass_on()], [token])
        down_sum.send_first(first)
    grad_middle, low, grad_att, sums_two, token = call(
        middle_back,
        "middle_back",
        (Far(shape(flat, width, dtype=f32)), shape(flat, width), shape(flat, width), shape(8, width, dtype=f32)),
        [
            vmem(tiles, width, width),
            vmem(width, width),
            vmem(flat, width, dtype=f32),
            vmem(flat, width, dtype=f32),
            sems(7),
        ],
        [og, small, Far(w_proj), Far(middle), Far(up_far), grad_pre],
        [token],
    )
    low_sibling = sibling(low)

    def expand_grad(left, left_sibling, after=()):
        return call(
            expand_weight_grad,
            "expand_weight_grad",
            [shape(part, hidden)] * HALF,
            [],
            [idx, left, left_sibling, grad_pre, grad_pre_sibling],
            after,
        )

    if fast:
        total, token = combine([down_sum.total()], [token])
        down_fold = Fold(total)
    *up_blocks, token = expand_grad(turned_keep, turned_sibling, [token])
    if fast:
        up_sum = Scatter(up_blocks, True)

    def heads(half, after):
        return call(
            functools.partial(heads_back, half, clips, rows),
            "heads_back",
            [shape(flat, 3 * group)],
            [vmem(flat, 3 * group), vmem(pairs // 2, 2 * rows, rows), sems(12)],
            [grad_att, Far(mixed), Far(probs)],
            after,
        )

    first_mixed, token = heads(0, [token])
    first_sibling = sibling(first_mixed)
    if fast:
        first, total, token = combine([up_sum.pass_on(), down_fold.terms()], [token])
        up_sum.send_first(first)
        down_fold.send(total)
    second_mixed, token = heads(1, [token])
    second_sibling = sibling(second_mixed)

    def attention_grad(left, left_sibling, after=()):
        return call(
            attention_weight_grad,
            "attention_weight_grad",
            [shape(part, first_cols)] * HALF,
            [],
            [left, left_sibling, low, low_sibling, first_mixed, first_sibling],
            after,
        )

    if fast:
        total, token = combine([up_sum.total()], [token])
        up_fold = Fold(total)
    *first_blocks, token = attention_grad(turned_keep, turned_sibling, [token])
    if fast:
        first_sum = Scatter(first_blocks, False)
        total, token = combine([down_fold.terms()], [token])
        down_fold.send(total)

    def last_grad(left, left_sibling, after=()):
        return call(
            last_weight_grad,
            "last_weight_grad",
            [shape(part, second_cols)] * HALF,
            [],
            [left, left_sibling, second_mixed, second_sibling],
            after,
        )

    *second_blocks, token = last_grad(turned_keep, turned_sibling, [token])
    if fast:
        second_sum = Scatter(second_blocks, False)
        total, token = combine([up_fold.terms()], [token])
        up_fold.send(total)
    gn1, vectors, token = call(
        input_sums,
        "input_sums",
        (Far(shape(flat, width, dtype=f32)), shape(16, width, dtype=f32)),
        [vmem(2, width, 3 * group), vmem(flat, width, dtype=f32), sems(7)],
        [first_mixed, second_mixed, x, sums_two, sums, Far(w_qkv)],
        [token],
    )
    if fast:
        every = Everywhere(vectors)
        total, token = combine([first_sum.total()], [token])
        first_fold = Fold(total)

    def shrink(start, hidden, base, out, after):
        return call(
            functools.partial(shrink_forward, start, clips, rows, seq),
            "shrink_forward",
            [out],
            [vmem(2, flat, width), vmem(flat, width, dtype=f32), vmem(2, width, width), sems(5)],
            [small, Far(hidden), Far(base), Far(down_far)],
            after,
        )

    partial_out, token = shrink(0, hidden_one_far, middle, shape(flat, width, dtype=f32), [token])
    if fast:
        vectors, total, more, token = combine([every.terms(), up_fold.terms(), second_sum.total()], [token])
        every.send(vectors)
        up_fold.send(total)
        second_fold = Fold(more)
    block_out, token = shrink(2, hidden_two_far, partial_out, shape(seq, clips, width), [token])
    if fast:
        vectors, total, token = combine([every.terms(), first_fold.terms()], [token])
        every.send(vectors)
        first_fold.send(total)
    tokens_grad, token = call(
        functools.partial(input_back, clips, rows, seq),
        "input_back",
        [shape(seq, clips, width, dtype=f32)],
        [],
        [gn1, grad_middle, x, small],
        [token],
    )

    if fast:
        vectors, total, token = combine([every.terms(), second_fold.terms()], [token])
        every.send(vectors)
        second_fold.send(total)
        vectors, total, token = combine([every.terms(), first_fold.terms()], [token])
        every.send(vectors)
        first_fold.send(total)
        vectors, total, token = combine([every.terms(), second_fold.terms()], [token])
        second_fold.send(total)
        folds = (down_fold, up_fold, first_fold, second_fold)
        whole_sums = [f.values for f in folds]
        grad_down, grad_up, grad_first, grad_second = (f.result().astype(f32) for f in folds)
        grad_down = grad_down.T
        index = me * own
    else:
        none = jnp.zeros_like(turned_send)
        halves = (
            (shrink_grad(hidden_one, hidden_sibling)[:-1], down_blocks),
            (expand_grad(turned_send, none)[:-1], up_blocks),
            (attention_grad(turned_send, none)[:-1], first_blocks),
            (last_grad(turned_send, none)[:-1], second_blocks),
        )
        whole_down = jnp.concatenate([b.T for half in halves[0] for b in half], axis=0)
        grad_down = reduce_plain(whole_down).astype(f32)
        grad_up, grad_first, grad_second = (
            reduce_plain(jnp.concatenate([b for half in pair for b in half], axis=0)).astype(f32)
            for pair in halves[1:]
        )
        whole_sums = [grad_down, grad_up, grad_first, grad_second]
        vectors = lax.psum(vectors, ("wide", "narrow"))
        index = lax.axis_index("wide") * own
    up_bias = vectors[8:12].reshape(4, BLOCKS, part).transpose(1, 0, 2).reshape(-1)
    up_bias = lax.dynamic_slice(up_bias, (4 * index,), (4 * own,))
    small_grads = lax.dynamic_slice(vectors[:8], (0, index), (8, own))

    local = jnp.sum(small_grads * small_grads) + jnp.sum(up_bias * up_bias)
    for values in whole_sums:
        local = local + jnp.sum(jnp.square(values.astype(f32)))
    if fast:
        for bit in (1, 2, 4):
            local = local + lax.ppermute(local, "wide", [(i, i ^ bit) for i in range(BLOCKS)])
        place = lax.axis_index("narrow")
        came = lax.ppermute(local, "narrow", [(1, 0), (2, 3)])
        grad_sq_norm = jnp.where((place == 1) | (place == 2), local, came)
    else:
        grad_sq_norm = lax.psum(local, "wide")
    grad_qkv = jnp.concatenate(
        [
            g[:, at + k * group : at + (k + 1) * group]
            for k in range(3)
            for g, at in ((grad_first, width), (grad_second, 0))
        ],
        axis=1,
    )
    return (
        block_out.transpose(1, 0, 2),
        tokens_grad.transpose(1, 0, 2),
        small_grads[0],
        small_grads[1],
        grad_qkv,
        small_grads[2],
        small_grads[3],
        grad_first[:, :width],
        small_grads[4],
        small_grads[5],
        small_grads[6],
        grad_up,
        up_bias,
        grad_down,
        small_grads[7],
        grad_sq_norm,
    )


def solution(mesh):
    fast = mesh.shape["wide"] == BLOCKS and mesh.shape["narrow"] == 4
    clips = P(("wide", "narrow"), None, None)
    vector = P("wide")
    matrix = P("wide", None)
    return jax.shard_map(
        functools.partial(body, fast),
        mesh=mesh,
        in_specs=(
            clips,
            clips,
            vector,
            vector,
            matrix,
            vector,
            vector,
            matrix,
            vector,
            vector,
            vector,
            matrix,
            vector,
            matrix,
            vector,
        ),
        out_specs=(
            clips,
            clips,
            vector,
            vector,
            matrix,
            vector,
            vector,
            matrix,
            vector,
            vector,
            vector,
            matrix,
            vector,
            matrix,
            vector,
            P(),
        ),
        check_vma=False,
    )
```

```python
import functools

import jax
import jax.numpy as jnp
from jax import lax
from jax.experimental import pallas as pl
from jax.experimental.pallas import tpu as pltpu
from jax.sharding import PartitionSpec as P

HEADS = 12
EPS = 1e-06
BLOCKS = 8
HALF = BLOCKS // 2
SMALL = 128
MIB = 1024 * 1024

f32 = jnp.float32
bf16 = jnp.bfloat16

ANY = pl.BlockSpec(memory_space=pl.ANY)
HBM = pl.BlockSpec(memory_space=pltpu.HBM)
FULL = pl.BlockSpec(memory_space=pltpu.VMEM)
SCALAR = pl.BlockSpec(memory_space=pltpu.SMEM)


def nn(a, b):
    return lax.dot_general(a, b, (((1,), (0,)), ((), ())), preferred_element_type=f32)


def nt(a, b):
    return lax.dot_general(a, b, (((1,), (1,)), ((), ())), preferred_element_type=f32)


def tn(a, b):
    return lax.dot_general(a, b, (((0,), (0,)), ((), ())), preferred_element_type=f32)


def normalise(values):
    mean_row = jnp.mean(values, axis=-1, keepdims=True)
    centered = values - mean_row
    spread = jnp.mean(centered * centered, axis=-1, keepdims=True)
    inverse = lax.rsqrt(spread + EPS)
    return centered * inverse, inverse


def norm_back(grad, normed, inverse):
    first = jnp.mean(grad, axis=-1, keepdims=True)
    second = jnp.mean(grad * normed, axis=-1, keepdims=True)
    return inverse * (grad - first - normed * second)


def gelu_both(values):
    cdf = 0.5 * (1.0 + lax.erf(values * (0.5**0.5)))
    density = 0.3989422804014327 * jnp.exp(-0.5 * values * values)
    return values * cdf, cdf + values * density


def sems(count):
    return pltpu.SemaphoreType.DMA((count,))


def start_all(pairs, sem, first=0):
    copies = [pltpu.make_async_copy(a, b, sem.at[first + k]) for k, (a, b) in enumerate(pairs)]
    for copy in copies:
        copy.start()
    return copies


def wait_all(copies):
    for copy in copies:
        copy.wait()


def rows_in_order(idx, pieces, target, columns=None):
    for i, piece in enumerate(pieces):
        count = piece.shape[0]
        rows = pl.ds(pl.multiple_of(idx[i] * count, 16), count)
        for source, to, size in columns or [(0, 0, piece.shape[1])]:
            target[rows, to : to + size] = piece[:, source : source + size]


def columns_by_place(idx, pieces, target, tile, places):
    for i, piece in enumerate(pieces):
        count = piece.shape[0]
        rows = pl.ds(pl.multiple_of(idx[i] * count, 16), count)
        for k, place in enumerate(places):
            source = pl.ds(pl.multiple_of(idx[place] * tile, 128), tile)
            target[rows, k * tile : (k + 1) * tile] = piece[:, source]


def rows_by_place(idx, target, value):
    part = value.shape[0] // BLOCKS
    for b in range(BLOCKS):
        to = pl.multiple_of(idx[BLOCKS + b] * part, 16)
        target[pl.ds(to, part)] = value[b * part : (b + 1) * part]


def beside(one, two):
    return jnp.concatenate([one[...], two[...]], axis=1)


def below(one, two):
    return jnp.concatenate([one[...], two[...]], axis=0)


def lanes_of(head_dim):
    return lax.broadcasted_iota(jnp.int32, (1, 2 * head_dim), 1) < head_dim


def stack_pair(pair, left):
    zero = jnp.zeros_like(pair)
    return jnp.concatenate([jnp.where(left, pair, zero), jnp.where(left, zero, pair)], axis=0)


def merge_pair(stacked, left):
    half = stacked.shape[0] // 2
    return jnp.where(left, stacked[:half], stacked[half:])


KERNELS = {
    "pack": (1, 8),
    "turn_rows": (1, 8),
    "norm_input": (0.01, 12),
    "attention_forward": (0.01, 28),
    "left_operands": (8, 16),
    "proj_forward": (0.01, 16),
    "expand_first": (0.01, 24),
    "expand_second": (25, 20),
    "shrink_weight_grad": (5, 16),
    "hidden_back": (14, 20),
    "middle_back": (45, 28),
    "expand_weight_grad": (14, 16),
    "heads_back": (20, 16),
    "attention_weight_grad": (20, 16),
    "last_weight_grad": (10, 12),
    "input_sums": (10, 20),
    "shrink_forward": (8, 16),
    "input_back": (8, 12),
    "combine": (0.5, 12),
    "cut_half": (0.5, 12),
    "join_halves": (0.5, 12),
    "finish_down": (1, 12),
    "finish_up": (1, 12),
    "finish_attention": (1, 12),
}
SCALE = 1.0


class Far:
    def __init__(self, array):
        self.array = array

    def operand(self):
        return pltpu.with_memory_space_constraint(self.array, pltpu.HBM)

    def result(self):
        return pltpu.HBM(self.array.shape, self.array.dtype)


TOKEN = jax.ShapeDtypeStruct((8, 128), f32)


def call(kernel, name, out_shape, scratch, inputs, after=()):
    given, skip, many = len(inputs), len(after), len(out_shape)
    specs = [HBM if isinstance(a, Far) else SCALAR if a.dtype == jnp.int32 else FULL for a in inputs]
    outs = [HBM if isinstance(o, Far) else FULL for o in out_shape] + [FULL]
    micros, mib = KERNELS[name]

    def run(*refs):
        token = refs[given + skip + many]
        token[...] = jnp.zeros(token.shape, f32)
        kernel(*refs[:given], *refs[given + skip : given + skip + many], *refs[given + skip + many + 1 :])

    return pl.pallas_call(
        run,
        out_shape=[o.result() if isinstance(o, Far) else o for o in out_shape] + [TOKEN],
        in_specs=specs + [FULL if a.shape == TOKEN.shape else ANY for a in after],
        out_specs=outs,
        scratch_shapes=scratch,
        compiler_params=pltpu.CompilerParams(vmem_limit_bytes=mib * MIB),
        cost_estimate=pl.CostEstimate(
            flops=int(micros * SCALE * 1e9), bytes_accessed=0, transcendentals=0
        ),
        name=name,
    )(*[a.operand() if isinstance(a, Far) else a for a in inputs], *after)


def combine(sums, after=()):
    arrays = [a for terms in sums for a in terms]

    def kernel(*refs):
        at = 0
        for terms, out in zip(sums, refs[len(arrays) :]):
            total = refs[at][...].astype(f32)
            for k in range(1, len(terms)):
                total = total + refs[at + k][...].astype(f32)
            out[...] = total.astype(out.dtype)
            at += len(terms)

    shapes = [jax.ShapeDtypeStruct(terms[0].shape, terms[0].dtype) for terms in sums]
    return call(kernel, "combine", shapes, [], arrays, after)


def side_by_side(sums, after=()):
    arrays = [a for some in sums for terms in some for a in terms]

    def kernel(*refs):
        refs = list(refs)
        outs = refs[len(arrays) :]
        for some, out in zip(sums, outs):
            at = 0
            for terms in some:
                values = [refs.pop(0)[...].astype(f32) for _ in terms]
                total = values[0]
                for value in values[1:]:
                    total = total + value
                out[:, at : at + total.shape[1]] = total.astype(out.dtype)
                at += total.shape[1]

    shapes = [
        jax.ShapeDtypeStruct((some[0][0].shape[0], sum(terms[0].shape[1] for terms in some)), bf16) for some in sums
    ]
    return call(kernel, "combine", shapes, [], arrays, after)


def tie(values, after):
    def nothing(*refs):
        pass

    n = len(values)
    return pl.pallas_call(
        nothing,
        out_shape=[jax.ShapeDtypeStruct(v.shape, v.dtype) for v in values],
        in_specs=[ANY] * n + [FULL if a.shape == TOKEN.shape else ANY for a in after],
        out_specs=[ANY] * n,
        input_output_aliases={i: i for i in range(n)},
        compiler_params=pltpu.CompilerParams(vmem_limit_bytes=MIB),
        name="tie",
    )(*values, *after)


def pack(qkv_ref, proj_ref, down_ref, vectors_ref, out_o, down_o, sem):
    cols, width = qkv_ref.shape[1], proj_ref.shape[1]
    pairs = [(qkv_ref, out_o.at[:, pl.ds(0, cols)]), (proj_ref, out_o.at[:, pl.ds(cols, width)])]
    here = start_all(pairs + [(down_ref, down_o)], sem)
    out_o[:, cols + width :] = vectors_ref[...].astype(f32).T.astype(bf16)
    wait_all(here)


def norm_input(x_ref, normed_o):
    normed_o[...] = normalise(x_ref[...].astype(f32))[0]


def turn_rows(source, out_o):
    out_o[...] = source[...].T


def attention_forward(clips, rows, seq, idx, normed, *refs):
    pieces = refs[:BLOCKS]
    attended, n1_o, mixed_o, probs_o, small_o, up_shift_o = refs[BLOCKS : BLOCKS + 6]
    weights_o, proj_o, weights, small_block, mixed, probs_all, sem = refs[BLOCKS + 6 :]
    width = normed.shape[1]
    pair = 2 * (width // HEADS)
    rows_in_order(idx, pieces, weights, [(0, 0, 3 * width)])
    rows_in_order(idx, pieces, small_block, [(4 * width, 0, SMALL)])
    rows_in_order(idx, pieces, proj_o, [(3 * width, 0, width)])
    gone = start_all([(weights, weights_o)], sem, 3)
    small = small_block[...].astype(f32).T
    small_o[...] = small[:16]
    up = [small[8 + k : 9 + k] for k in range(4)]
    part = width // BLOCKS
    for s in range(BLOCKS):
        up_shift_o[s] = jnp.concatenate([u[:, part * s : part * (s + 1)] for u in up], axis=1)
    n1 = (normed[...] * small[0:1] + small[1:2]).astype(bf16)
    for t in range(3):
        acc = nn(n1, weights[:, width * t : width * (t + 1)])
        if t == 0:
            acc = acc + small[2:3]
        if t == 2:
            acc = acc + small[3:4]
        mixed[:, width * t : width * (t + 1)] = acc.astype(bf16)
    gone += start_all([(mixed, mixed_o)], sem)
    n1_o[...] = n1
    left = lanes_of(width // HEADS)
    valid = lax.broadcasted_iota(jnp.int32, (1, rows), 1) < seq
    scale = (width // HEADS) ** (-0.5)

    def probs_copy(p):
        at = pl.ds(p * clips, clips)
        return pltpu.make_async_copy(probs_all.at[at], probs_o.at[at], sem.at[4 + p])

    def heads(p, carry):
        lane = pl.multiple_of(p * pair, pair)
        for c in range(clips):
            here = pl.ds(c * rows, rows)
            q = mixed[here, pl.ds(lane, pair)]
            k = mixed[here, pl.ds(lane + width, pair)]
            v = mixed[here, pl.ds(lane + 2 * width, pair)]
            scores = nt(stack_pair(q, left), k) * scale
            scores = jnp.where(valid, scores, -1e30)
            peak = jnp.max(scores, axis=-1, keepdims=True)
            raised = jnp.exp(scores - peak)
            total = jnp.sum(raised, axis=-1, keepdims=True)
            probs = (raised * (1.0 / total)).astype(bf16)
            probs_all[p * clips + c] = probs
            attended[here, pl.ds(lane, pair)] = merge_pair(nn(probs, v), left).astype(bf16)
        probs_copy(p).start()
        return carry

    lax.fori_loop(0, HEADS // 2, heads, 0, unroll=2)

    def gone_heads(p, carry):
        probs_copy(p).wait()
        return carry

    lax.fori_loop(0, HEADS // 2, gone_heads, 0)
    wait_all(gone)


def proj_forward(x_ref, attended, small, weights, middle_far, n2_o, middle, sem):
    value = x_ref[...].astype(f32) + (nn(attended[...], weights[...]) + small[4:5])
    middle[...] = value
    gone = start_all([(middle, middle_far)], sem)
    normed, inverse = normalise(value)
    n2_o[...] = (normed * small[5:6] + small[6:7]).astype(bf16)
    wait_all(gone)


def left_operands(idx, n1, attended, n2, send_o, keep_o, turned):
    width = n1.shape[1]
    half, part = width // 2, width // BLOCKS
    for k, source in enumerate((n1, attended, n2)):
        turned[k] = source[...].T
        for p in range(BLOCKS):
            to = k * half + p % HALF * part
            rows = pl.ds(pl.multiple_of(idx[p] * part, 16), part)
            (send_o if p < HALF else keep_o)[to : to + part] = turned[k, rows]


def expand_tiles(start, idx, n2_ref, shift_ref, weights, hidden_o, slope_far, hidden_far, pre, slope, sem):
    width = n2_ref.shape[1]
    step = 256
    gone = []

    def multiply(t, c):
        cols = slice(c * step, (c + 1) * step)
        pre[t, :, cols] = nn(n2_ref[...], weights[t, :, cols])

    for c in range(width // step):
        multiply(0, c)
    for t in range(2):
        shift = jnp.concatenate([shift_ref[idx[2 * (start + t) + k]] for k in range(2)], axis=1)
        for c in range(width // step):
            cols = slice(c * step, (c + 1) * step)
            if t == 0:
                multiply(1, c)
            act, derivative = gelu_both(pre[t, :, cols] + shift[:, cols])
            hidden_o[t, :, cols] = act.astype(bf16)
            slope[t, :, cols] = derivative.astype(bf16)
        gone += start_all([(hidden_o.at[t], hidden_far.at[t]), (slope.at[t], slope_far.at[t])], sem, 2 * t)
    return gone


def expand_first(idx, n2_ref, shift_ref, *refs):
    pieces = refs[:BLOCKS]
    hidden_o, two_o, slope_far, hidden_far, up_far, one, pre, slope, sem = refs[BLOCKS:]
    tile = n2_ref.shape[1] // 2
    for t in range(2):
        columns_by_place(idx, pieces, one.at[t], tile, (2 * t, 2 * t + 1))
    gone = start_all([(one, up_far.at[pl.ds(0, 2)])], sem, 4)
    gone += expand_tiles(0, idx, n2_ref, shift_ref, one, hidden_o, slope_far, hidden_far, pre, slope, sem)
    for t in range(2):
        columns_by_place(idx, pieces, two_o.at[t], tile, (2 * t + 4, 2 * t + 5))
    gone += start_all([(two_o, up_far.at[pl.ds(2, 2)])], sem, 5)
    wait_all(gone)


def expand_second(*refs):
    wait_all(expand_tiles(2, *refs))


def shrink_weight_grad(ogt, ogt_sibling, own, sibling, *outs):
    left = beside(ogt, ogt_sibling)
    for t in range(2):
        grad = nn(left, below(own.at[t], sibling.at[t])).astype(bf16)
        tile = grad.shape[1] // 2
        for k in range(2):
            outs[2 * t + k][...] = grad[:, k * tile : (k + 1) * tile]


def expand_weight_grad(idx, own_left, sibling_left, own, sibling, *outs):
    half = own_left.shape[0] // 3
    part = half // HALF
    at = pl.ds(2 * half, half)
    left = beside(own_left.at[at], sibling_left.at[at])
    for t in range(4):
        grad = nn(left, below(own.at[t], sibling.at[(t + 2) % 4])).astype(bf16)
        tile = grad.shape[1] // 2
        for k in range(2):
            to = pl.multiple_of(idx[2 * t + k] * tile, 128)
            for b in range(HALF):
                outs[b][:, pl.ds(to, tile)] = grad[b * part : (b + 1) * part, k * tile : (k + 1) * tile]


def rows_out(grad, outs, columns):
    part = grad.shape[0] // HALF
    for b in range(HALF):
        outs[b][:, columns] = grad[b * part : (b + 1) * part].astype(bf16)


def attention_weight_grad(own_left, sibling_left, own_low, sibling_low, own_mixed, sibling_mixed, *outs):
    width = own_low.shape[1]
    half = width // 2
    for k, right, columns in (
        (1, below(own_low, sibling_low), slice(0, width)),
        (0, below(own_mixed, sibling_mixed), slice(width, None)),
    ):
        at = pl.ds(k * half, half)
        rows_out(nn(beside(own_left.at[at], sibling_left.at[at]), right), outs, columns)


def last_weight_grad(own_left, sibling_left, own_mixed, sibling_mixed, *outs):
    at = pl.ds(0, own_left.shape[0] // 3)
    left = beside(own_left.at[at], sibling_left.at[at])
    rows_out(nn(left, below(own_mixed, sibling_mixed)), outs, slice(None))


def hidden_back(idx, og_ref, slope_one, slope_two, *refs):
    down_pieces, (grad_pre, sums_o, down_far, slope, sem) = refs[:BLOCKS], refs[BLOCKS:]
    tile = down_pieces[0].shape[0]
    here = [
        start_all([((slope_one if t < 2 else slope_two).at[t % 2], slope.at[t])], sem, BLOCKS + t)
        for t in range(4)
    ]
    pairs = [(piece, down_far.at[i // 2, pl.ds(i % 2 * tile, tile)]) for i, piece in enumerate(down_pieces)]
    gone = start_all(pairs, sem)
    for t in range(grad_pre.shape[0]):
        down = below(down_pieces[2 * t], down_pieces[2 * t + 1])
        grad_hidden = nt(og_ref[...], down)
        wait_all(here[t])
        gp = (grad_hidden * slope[t].astype(f32)).astype(bf16)
        grad_pre[t] = gp
        sums = jnp.sum(gp.astype(f32), axis=0, keepdims=True)
        for k in range(2):
            sums_o[idx[2 * t + k]] = sums[:, k * tile : (k + 1) * tile]
    wait_all(gone)


def middle_back(og_ref, small_ref, weights, middle_ref, up_ref, grad_pre, *refs):
    grad_middle_o, low_o, grad_att_o, vectors_o, up, middle, sem = refs

    def up_copy(t):
        return pltpu.make_async_copy(up_ref.at[t], up.at[t], sem.at[t])

    for t in range(4):
        up_copy(t).start()
    here = start_all([(middle_ref, middle)], sem, 4)
    grad_middle_o[...] = jnp.zeros(grad_middle_o.shape, f32)

    def step(t, carry):
        up_copy(t).wait()
        grad_middle_o[...] += nt(grad_pre[t], up[t])
        return carry

    lax.fori_loop(0, 4, step, 0)
    wait_all(here)
    gn2 = grad_middle_o[...]
    normed, inverse = normalise(middle[...])
    og = og_ref[...].astype(f32)
    value = og + norm_back(gn2 * small_ref[5:6], normed, inverse)
    grad_middle_o[...] = value
    low = value.astype(bf16)
    low_o[...] = low
    grad_att_o[...] = nt(low, weights[...]).astype(bf16)
    vectors_o[0:1] = jnp.sum(low.astype(f32), axis=0, keepdims=True)
    vectors_o[1:2] = jnp.sum(gn2 * normed, axis=0, keepdims=True)
    vectors_o[2:3] = jnp.sum(gn2, axis=0, keepdims=True)
    vectors_o[3:4] = jnp.sum(og, axis=0, keepdims=True)


def heads_back(half, clips, rows, grad_att, mixed_ref, probs_ref, grad_mixed_o, mixed, probs_all, sem):
    width = grad_att.shape[1]
    group = width // 2
    head_dim = width // HEADS
    pair = 2 * head_dim
    count = group // pair
    left = lanes_of(head_dim)
    scale = head_dim ** (-0.5)
    arrived = []
    for p in range(count):
        at = half * group + p * pair
        pairs = [
            (mixed_ref.at[:, pl.ds(k * width + at, pair)], mixed.at[:, pl.ds(k * group + p * pair, pair)])
            for k in range(3)
        ]
        source = pl.ds((half * count + p) * clips, clips)
        pairs.append((probs_ref.at[source], probs_all.at[pl.ds(p * clips, clips)]))
        arrived.append(start_all(pairs, sem, 4 * p))
    for p in range(count):
        wait_all(arrived[p])
        lanes = slice(p * pair, (p + 1) * pair)
        for c in range(clips):
            here = pl.ds(c * rows, rows)
            q, k, v = (mixed[here, t * group + p * pair : t * group + (p + 1) * pair] for t in range(3))
            low_probs = probs_all[p * clips + c]
            probs = low_probs.astype(f32)
            at = half * group + p * pair
            grad = stack_pair(grad_att[here, at : at + pair], left)
            grad_probs = nt(grad, v)
            inner = jnp.sum(probs * grad_probs, axis=-1, keepdims=True)
            grad_scores = (probs * (grad_probs - inner)).astype(bf16)
            gq = merge_pair(nn(grad_scores, k), left) * scale
            gk = tn(grad_scores, stack_pair(q, left)) * scale
            gv = tn(low_probs, grad)
            for t, value in enumerate((gq, gk, gv)):
                grad_mixed_o[here, t * group + p * pair : t * group + (p + 1) * pair] = value.astype(bf16)


def input_sums(first, second, x_ref, vectors_ref, sums_ref, weights_ref, gn1_o, vectors_o, weights, gn1_all, sem):
    width = x_ref.shape[1]
    group = width // 2
    part = width // BLOCKS
    here = []
    for g in range(2):
        pairs = []
        for k in range(3):
            source = weights_ref.at[:, pl.ds(k * width + g * group, group)]
            pairs.append((source, weights.at[g, :, pl.ds(k * group, group)]))
        here.append(start_all(pairs, sem, 1 + 3 * g))
    normed, inverse = normalise(x_ref[...].astype(f32))

    def sum_of(ref, k):
        return jnp.sum(ref[:, k * group : (k + 1) * group].astype(f32), axis=0, keepdims=True)

    vectors_o[2:3] = jnp.concatenate([sum_of(first, 0), sum_of(second, 0)], axis=1)
    vectors_o[3:4] = jnp.concatenate([sum_of(first, 2), sum_of(second, 2)], axis=1)
    vectors_o[4:8] = vectors_ref[0:4]
    for k in range(4):
        vectors_o[8 + k : 9 + k] = jnp.concatenate(
            [sums_ref[s][:, part * k : part * (k + 1)] for s in range(BLOCKS)], axis=1
        )
    vectors_o[12:] = jnp.zeros((4, width), f32)
    gn1 = None
    for g, grad in enumerate((first, second)):
        wait_all(here[g])
        more = nt(grad[...], weights[g])
        gn1 = more if gn1 is None else gn1 + more
    gn1_all[...] = gn1
    gone = start_all([(gn1_all, gn1_o)], sem)
    vectors_o[0:1] = jnp.sum(gn1 * normed, axis=0, keepdims=True)
    vectors_o[1:2] = jnp.sum(gn1, axis=0, keepdims=True)
    wait_all(gone)


def shrink_forward(start, clips, rows, seq, small_ref, hidden_ref, base_ref, down_ref, out_o, hidden, base, down, sem):
    here = []
    for t in range(2):
        here.append(start_all([(down_ref.at[start + t], down.at[t]), (hidden_ref.at[t], hidden.at[t])], sem, 2 * t))
    base_here = start_all([(base_ref, base)], sem, 4)
    total = None
    for t in range(2):
        wait_all(here[t])
        more = nn(hidden[t], down[t])
        total = more if total is None else total + more
    wait_all(base_here)
    total = total + base[...]
    if start == 0:
        out_o[...] = total + small_ref[7:8]
    else:
        for c in range(clips):
            out_o[:, c, :] = total[c * rows : c * rows + seq].astype(bf16)


def input_back(clips, rows, seq, gn1_ref, middle_ref, x_ref, small_ref, out_o):
    normed, inverse = normalise(x_ref[...].astype(f32))
    grad = middle_ref[...] + norm_back(gn1_ref[...] * small_ref[0:1], normed, inverse)
    for c in range(clips):
        out_o[:, c, :] = grad[c * rows : c * rows + seq]


def half_of(ref, axis, place):
    size = ref.shape[axis] // 2
    at = pl.ds(pl.multiple_of(place * size, 128), size)
    return ref.at[at] if axis == 0 else ref.at[:, at]


def cut_half(axis, bit, counts, idx, *refs):
    terms, (send_o, keep_o, whole) = list(refs[:-3]), refs[-3:]
    at = 0
    for count in counts:
        some = [terms.pop(0) for _ in range(count)]
        total = some[0][...].astype(f32)
        for term in some[1:]:
            total = total + term[...].astype(f32)
        size = total.shape[axis]
        (whole.at[at : at + size] if axis == 0 else whole.at[:, at : at + size])[...] = total.astype(bf16)
        at += size
    send_o[...] = half_of(whole, axis, 1 - idx[bit])[...]
    keep_o[...] = half_of(whole, axis, idx[bit])[...]


def join_halves(axis, bit, idx, own, other, out_o):
    half_of(out_o, axis, idx[bit])[...] = own[...].astype(out_o.dtype)
    half_of(out_o, axis, 1 - idx[bit])[...] = other[...].astype(out_o.dtype)


def squares_of(ref, sums_o):
    sums_o[...] = jnp.broadcast_to(jnp.sum(ref[...] * ref[...]), sums_o.shape)


def finish_down(idx, own, other, out_o, sums_o, whole):
    join_halves(0, 2 * BLOCKS, idx, own, other, whole)
    out_o[...] = whole[...].T
    squares_of(whole, sums_o)


def finish_up(idx, own, other, out_o, sums_o):
    join_halves(1, 2 * BLOCKS, idx, own, other, out_o)
    squares_of(out_o, sums_o)


def finish_attention(idx, own, other, vectors, sums, qkv_o, proj_o, sums_o, whole):
    join_halves(1, 2 * BLOCKS, idx, own, other, whole)
    width = proj_o.shape[1]
    group = width // 2
    proj_o[...] = whole[:, :width]
    for k in range(3):
        for g in range(2):
            at = width + (3 * g + k) * group
            to = k * width + g * group
            qkv_o[:, to : to + group] = whole[:, at : at + group]
    squares_of(whole, sums_o)
    sums_o[...] += sums[...] + jnp.sum(vectors[...] * vectors[...])


def cores(values):
    return lax.ppermute(values, "wide", [(i, i ^ 1) for i in range(BLOCKS)])


def near(values):
    return lax.ppermute(values, "wide", [(i, i ^ (4 if i & 1 else 2)) for i in range(BLOCKS)])


def across(values):
    return lax.ppermute(values, "wide", [(i, i ^ 6) for i in range(BLOCKS)])


def cross(values):
    return lax.ppermute(values, "wide", [(i, i ^ (2 if i & 1 else 4)) for i in range(BLOCKS)])


class Scatter:
    def __init__(self, blocks):
        self.parts = []
        self.more(blocks)

    def more(self, blocks):
        far, other, first, own = blocks
        self.parts.append((cross(far), other, first, own))

    def pass_on(self, after):
        sums = [[[first, came] for came, _, first, _ in self.parts]]
        sums += [[[part[k]] for part in self.parts] for k in (1, 3)]
        if len(self.parts) == 1:
            first, token = combine([sums[0][0]], after)
            (other,) = tie([self.parts[0][1]], [token])
            self.own = self.parts[0][3]
        else:
            first, other, self.own, token = side_by_side(sums, after)
        self.came_first, self.came_other = near(first), cross(other)
        return token

    def total(self):
        return [self.own, self.came_other, self.came_first]


class Halves:
    def __init__(self, idx, axis):
        self.idx, self.axis, self.steps = idx, axis, 0

    def send(self, values, bit):
        self.came = lax.ppermute(values, "narrow", [(i, i ^ bit) for i in range(4)])

    def cut(self, sums, bit, after):
        whole = list(sums[0][0].shape)
        whole[self.axis] = sum(terms[0].shape[self.axis] for terms in sums)
        shape = list(whole)
        shape[self.axis] //= 2
        out = jax.ShapeDtypeStruct(tuple(shape), bf16)
        send, self.keep, token = call(
            functools.partial(cut_half, self.axis, 2 * BLOCKS + bit - 1, [len(terms) for terms in sums]),
            "cut_half",
            [out, out],
            [pltpu.VMEM(tuple(whole), bf16)],
            [self.idx, *(term for terms in sums for term in terms)],
            after,
        )
        self.send(send, bit)
        return token

    def one(self, sums, after):
        return self.cut(sums, 1, after)

    def two(self, after):
        return self.cut([[self.keep, self.came]], 2, after)

    def three(self, after):
        self.keep, token = combine([[self.keep, self.came]], after)
        self.send(self.keep, 2)
        return token

    def four(self, after):
        shape = list(self.keep.shape)
        shape[self.axis] *= 2
        self.keep, token = call(
            functools.partial(join_halves, self.axis, 2 * BLOCKS + 1),
            "join_halves",
            [jax.ShapeDtypeStruct(tuple(shape), bf16)],
            [],
            [self.idx, self.keep, self.came],
            after,
        )
        self.send(self.keep, 1)
        return token


class Gather:
    def __init__(self, own):
        self.own, self.first, self.other = own, near(own), cross(own)

    def direct(self):
        self.far = across(self.own)

    def forward(self, after):
        self.first, self.other = tie([self.first, self.other], after)
        self.far = cross(self.first)

    def parts(self, after=()):
        mine = [self.far, self.other, self.first]
        if after:
            mine = list(tie(mine, after))
        mine.append(self.own)
        return [cores(m) for m in mine] + mine

    def parts_early(self):
        early = [cores(m) for m in (self.other, self.first, self.own)]
        (far,) = tie([self.far], early)
        return [cores(far)] + early + [far, self.other, self.first, self.own]


class Everywhere:
    def __init__(self, value):
        self.hops = [("wide", b, BLOCKS) for b in (1, 2, 4)] + [("narrow", b, 4) for b in (1, 2)]
        self.send(value)

    def send(self, value):
        self.value = value
        if self.hops:
            axis, bit, count = self.hops.pop(0)
            self.came = lax.ppermute(value, axis, [(i, i ^ bit) for i in range(count)])

    def terms(self):
        return [self.value, self.came]


def spread(whole):
    return list(jnp.split(whole, BLOCKS, axis=0))


def reduce_plain(whole):
    return lax.psum(lax.psum_scatter(whole, "wide", scatter_dimension=0, tiled=True), "narrow")


def body(
    fast,
    tokens,
    out_grad,
    first_gain,
    first_shift,
    qkv_weight,
    query_bias,
    value_bias,
    proj_weight,
    proj_bias,
    second_gain,
    second_shift,
    expand_weight,
    expand_bias,
    shrink_weight,
    shrink_bias,
):
    clips, seq, width = tokens.shape
    rows = -(-seq // 16) * 16
    flat = clips * rows
    part = width // BLOCKS
    hidden = 4 * width
    tile = hidden // BLOCKS
    tiles = hidden // width
    group = width // 2
    pairs = HEADS // 2 * clips
    first_cols = width + 3 * group
    second_cols = 3 * group
    own = first_gain.shape[0]
    gather_plain = functools.partial(lax.all_gather, axis_name="wide", axis=0, tiled=True)

    def shape(*dims, dtype=bf16):
        return jax.ShapeDtypeStruct(dims, dtype)

    def vmem(*dims, dtype=bf16):
        return pltpu.VMEM(dims, dtype)

    if fast:
        me = lax.axis_index("wide")
        odd = me % 2
        relative = [
            jnp.where(odd == 1, b, a) for a, b in zip((7, 3, 5, 1, 6, 4, 2, 0), (7, 5, 3, 1, 6, 2, 4, 0))
        ]
        order = jnp.stack(relative) ^ me
        where = jnp.sum(
            jnp.where(order[None, :] == jnp.arange(BLOCKS)[:, None], jnp.arange(BLOCKS)[None, :], 0),
            axis=1,
        )
        line = lax.axis_index("narrow")
        idx = jnp.concatenate([order, where, jnp.stack([line % 2, line // 2])]).astype(jnp.int32)
    else:
        idx = jnp.concatenate([jnp.arange(BLOCKS), jnp.arange(BLOCKS)]).astype(jnp.int32)

    vectors = [
        first_gain,
        first_shift,
        query_bias,
        value_bias,
        proj_bias,
        second_gain,
        second_shift,
        shrink_bias,
    ]
    block = jnp.concatenate([jnp.stack(vectors), expand_bias.reshape(4, own)], axis=0)
    block = jnp.pad(block, ((0, SMALL - block.shape[0]), (0, 0)))
    packed, down_own, token = call(
        pack,
        "pack",
        [shape(own, 4 * width + SMALL), shape(*shrink_weight.shape)],
        [sems(3)],
        [Far(qkv_weight), Far(proj_weight), Far(shrink_weight), block],
    )
    pad = ((0, 0), (0, rows - seq), (0, 0))
    x = jnp.pad(tokens, pad).reshape(flat, width)
    og = jnp.pad(out_grad, pad).reshape(flat, width)
    ogt, token = call(turn_rows, "turn_rows", [shape(width, flat)], [], [og])

    after = []
    if fast:
        attn = Gather(packed)
        up = Gather(expand_weight)
        attn.forward([x, ogt, idx])
        attn_parts = attn.parts_early()
    else:
        up_parts = spread(gather_plain(expand_weight))
        down_parts = spread(gather_plain(shrink_weight))
        whole = gather_plain(packed)
        bias = whole[:, 4 * width + 8 : 4 * width + 12].reshape(width // own, own, 4)
        bias = bias.transpose(0, 2, 1).reshape(BLOCKS, 4, part).transpose(0, 2, 1).reshape(width, 4)
        attn_parts = spread(whole.at[:, 4 * width + 8 : 4 * width + 12].set(bias))

    def sibling(array):
        return cores(array) if fast else jnp.zeros_like(array)

    ogt_sibling = sibling(ogt)
    normed, token = call(norm_input, "norm_input", [shape(flat, width, dtype=f32)], [], [x])
    attended, n1, mixed, probs, small, up_shift, w_qkv, w_proj, token = call(
        functools.partial(attention_forward, clips, rows, seq),
        "attention_forward",
        (
            shape(flat, width),
            shape(flat, width),
            Far(shape(flat, 3 * width)),
            Far(shape(pairs, 2 * rows, rows)),
            shape(16, width, dtype=f32),
            shape(BLOCKS, 1, tile, dtype=f32),
            Far(shape(width, 3 * width)),
            shape(width, width),
        ),
        [vmem(width, 3 * width), vmem(width, SMALL), vmem(flat, 3 * width), vmem(pairs, 2 * rows, rows), sems(4 + HEADS // 2)],
        [idx, normed, *attn_parts],
    )
    if fast:
        up.forward([token])
    middle, n2, token = call(
        proj_forward,
        "proj_forward",
        (Far(shape(flat, width, dtype=f32)), shape(flat, width)),
        [vmem(flat, width, dtype=f32), sems(1)],
        [x, attended, small, w_proj],
    )
    if fast:
        up_parts = up.parts([token])
        (down_own,) = tie([down_own], [up.far])
        down = Gather(down_own)
    turned_send, turned_keep, token = call(
        left_operands,
        "left_operands",
        [shape(3 * width // 2, flat)] * 2,
        [vmem(3, width, flat)],
        [idx, n1, attended, n2],
        [token],
    )
    turned_sibling = sibling(turned_send)

    two_tiles = shape(2, flat, width)
    expand_scratch = [vmem(2, flat, width, dtype=f32), vmem(2, flat, width), sems(6)]
    hidden_one, up_two, slope_one, hidden_one_far, up_far, token = call(
        expand_first,
        "expand_first",
        (two_tiles, shape(2, width, width), Far(two_tiles), Far(two_tiles), Far(shape(tiles, width, width))),
        [vmem(2, width, width)] + expand_scratch,
        [idx, n2, up_shift, *up_parts],
        [token],
    )
    hidden_sibling = sibling(hidden_one)
    if fast:
        down.forward([token])
    hidden_two, slope_two, hidden_two_far, token = call(
        expand_second,
        "expand_second",
        (two_tiles, Far(two_tiles), Far(two_tiles)),
        expand_scratch,
        [idx, n2, up_shift, up_two],
        [token],
    )

    def shrink_grad(own_hidden, sibling_hidden):
        return call(
            shrink_weight_grad,
            "shrink_weight_grad",
            [shape(width, tile)] * HALF,
            [],
            [ogt, ogt_sibling, own_hidden, sibling_hidden],
        )

    *down_blocks, token = shrink_grad(hidden_two, hidden_sibling)
    if fast:
        down_sum = Scatter(down_blocks)
        down_parts = down.parts([token])
    grad_pre, sums, down_far, token = call(
        hidden_back,
        "hidden_back",
        [shape(tiles, flat, width), shape(BLOCKS, 1, tile, dtype=f32), Far(shape(tiles, width, width))],
        [vmem(tiles, flat, width), sems(BLOCKS + 4)],
        [idx, og, Far(slope_one), Far(slope_two), *down_parts],
        [turned_sibling],
    )
    grad_pre_sibling = sibling(grad_pre)
    if fast:
        token = down_sum.pass_on([token])
    grad_middle, low, grad_att, sums_two, token = call(
        middle_back,
        "middle_back",
        (shape(flat, width, dtype=f32), shape(flat, width), shape(flat, width), shape(8, width, dtype=f32)),
        [vmem(tiles, width, width), vmem(flat, width, dtype=f32), sems(5)],
        [og, small, w_proj, Far(middle), Far(up_far), grad_pre],
        [token],
    )
    low_sibling = sibling(low)

    def expand_grad(left, left_sibling, after=()):
        return call(
            expand_weight_grad,
            "expand_weight_grad",
            [shape(part, hidden)] * HALF,
            [],
            [idx, left, left_sibling, grad_pre, grad_pre_sibling],
            after,
        )

    *up_blocks, token = expand_grad(turned_keep, turned_sibling, [token])
    if fast:
        up_sum = Scatter(up_blocks)
        down_fold = Halves(idx, 0)
        token = down_fold.one([down_sum.total()], [token])

    def heads(half, after):
        return call(
            functools.partial(heads_back, half, clips, rows),
            "heads_back",
            [shape(flat, 3 * group)],
            [vmem(flat, 3 * group), vmem(pairs // 2, 2 * rows, rows), sems(12)],
            [grad_att, Far(mixed), Far(probs)],
            after,
        )

    first_mixed, token = heads(0, [token, low_sibling])
    first_sibling = sibling(first_mixed)
    if fast:
        token = up_sum.pass_on([token])
        token = down_fold.two([token])
    second_mixed, token = heads(1, [token])
    second_sibling = sibling(second_mixed)
    if fast:
        token = down_fold.three([token])

    def attention_grad(left, left_sibling, after=()):
        return call(
            attention_weight_grad,
            "attention_weight_grad",
            [shape(part, first_cols)] * HALF,
            [],
            [left, left_sibling, low, low_sibling, first_mixed, first_sibling],
            after,
        )

    *first_blocks, token = attention_grad(turned_keep, turned_sibling, [token])
    if fast:
        attn_sum = Scatter(first_blocks)

    def last_grad(left, left_sibling, after=()):
        return call(
            last_weight_grad,
            "last_weight_grad",
            [shape(part, second_cols)] * HALF,
            [],
            [left, left_sibling, second_mixed, second_sibling],
            after,
        )

    *second_blocks, token = last_grad(turned_keep, turned_sibling, [token])
    if fast:
        attn_sum.more(second_blocks)
        up_fold = Halves(idx, 1)
        token = up_fold.one([up_sum.total()], [token])
        token = down_fold.four([token])
    gn1, vectors, token = call(
        input_sums,
        "input_sums",
        (Far(shape(flat, width, dtype=f32)), shape(16, width, dtype=f32)),
        [vmem(2, width, 3 * group), vmem(flat, width, dtype=f32), sems(7)],
        [first_mixed, second_mixed, x, sums_two, sums, Far(w_qkv)],
        [token],
    )
    if fast:
        token = attn_sum.pass_on([token])
        token = up_fold.two([token])
        every = Everywhere(vectors)

    def shrink(start, hidden, base, out, after):
        return call(
            functools.partial(shrink_forward, start, clips, rows, seq),
            "shrink_forward",
            [out],
            [vmem(2, flat, width), vmem(flat, width, dtype=f32), vmem(2, width, width), sems(5)],
            [small, Far(hidden), Far(base), Far(down_far)],
            after,
        )

    partial_out, token = shrink(0, hidden_one_far, middle, shape(flat, width, dtype=f32), [token])
    if fast:
        vectors, token = combine([every.terms()], [token])
        every.send(vectors)
        token = up_fold.three([token])
    block_out, token = shrink(2, hidden_two_far, partial_out, shape(seq, clips, width), [token])
    if fast:
        fold = Halves(idx, 1)
        token = fold.one([attn_sum.total()], [token])
        token = up_fold.four([token])
        vectors, token = combine([every.terms()], [token])
        every.send(vectors)
        grad_down, sums_down, token = call(
            finish_down,
            "finish_down",
            [shape(tile, width, dtype=f32), TOKEN],
            [vmem(width, tile, dtype=f32)],
            [idx, down_fold.keep, down_fold.came],
            [token],
        )
    tokens_grad, token = call(
        functools.partial(input_back, clips, rows, seq),
        "input_back",
        [shape(seq, clips, width, dtype=f32)],
        [],
        [gn1, grad_middle, x, small],
        [token],
    )

    if fast:
        token = fold.two([token])
        vectors, token = combine([every.terms()], [token])
        every.send(vectors)
        grad_up, sums_up, token = call(
            finish_up,
            "finish_up",
            [shape(part, hidden, dtype=f32), TOKEN],
            [],
            [idx, up_fold.keep, up_fold.came],
            [token],
        )
        token = fold.three([token])
        vectors, token = combine([every.terms()], [token])
        every.send(vectors)
        token = fold.four([token])
        vectors, token = combine([every.terms()], [token])
        index = me * own
    else:
        none = jnp.zeros_like(turned_send)
        halves = (
            (shrink_grad(hidden_one, hidden_sibling)[:-1], down_blocks),
            (expand_grad(turned_send, none)[:-1], up_blocks),
            (attention_grad(turned_send, none)[:-1], first_blocks),
            (last_grad(turned_send, none)[:-1], second_blocks),
        )
        whole_down = jnp.concatenate([b.T for half in halves[0] for b in half], axis=0)
        grad_down = reduce_plain(whole_down).astype(f32)
        grad_up, grad_first, grad_second = (
            reduce_plain(jnp.concatenate([b for half in pair for b in half], axis=0)).astype(f32)
            for pair in halves[1:]
        )
        vectors = lax.psum(vectors, ("wide", "narrow"))
        index = lax.axis_index("wide") * own
    up_bias = vectors[8:12].reshape(4, BLOCKS, part).transpose(1, 0, 2).reshape(-1)
    up_bias = lax.dynamic_slice(up_bias, (4 * index,), (4 * own,))
    small_grads = lax.dynamic_slice(vectors[:8], (0, index), (8, own))
    if fast:
        own_vectors = jnp.concatenate([small_grads.reshape(-1), up_bias]).reshape(-1, 128)
        own_vectors = jnp.pad(own_vectors, ((0, 16 - own_vectors.shape[0]), (0, 0)))
        grad_qkv, grad_proj, squares, token = call(
            finish_attention,
            "finish_attention",
            [shape(part, 3 * width, dtype=f32), shape(part, width, dtype=f32), TOKEN],
            [vmem(part, hidden, dtype=f32)],
            [idx, fold.keep, fold.came, own_vectors, sums_down + sums_up],
        )
        for perms in ((1,), (2, 4, 6)):
            came = [lax.ppermute(squares, "wide", [(i, i ^ b) for i in range(BLOCKS)]) for b in perms]
            squares = squares + came[0] if len(came) == 1 else (squares + came[0]) + (came[1] + came[2])
        grad_sq_norm = squares[0, 0]
    else:
        grad_proj = grad_first[:, :width]
        grad_qkv = jnp.concatenate(
            [
                g[:, at + k * group : at + (k + 1) * group]
                for k in range(3)
                for g, at in ((grad_first, width), (grad_second, 0))
            ],
            axis=1,
        )
        local = sum(jnp.sum(g * g) for g in (small_grads, up_bias, grad_down, grad_up, grad_first, grad_second))
        grad_sq_norm = lax.psum(local, "wide")
    return (
        block_out.transpose(1, 0, 2),
        tokens_grad.transpose(1, 0, 2),
        small_grads[0],
        small_grads[1],
        grad_qkv,
        small_grads[2],
        small_grads[3],
        grad_proj,
        small_grads[4],
        small_grads[5],
        small_grads[6],
        grad_up,
        up_bias,
        grad_down,
        small_grads[7],
        grad_sq_norm,
    )


def solution(mesh):
    fast = mesh.shape["wide"] == BLOCKS and mesh.shape["narrow"] == 4
    clips = P(("wide", "narrow"), None, None)
    vector = P("wide")
    matrix = P("wide", None)
    return jax.shard_map(
        functools.partial(body, fast),
        mesh=mesh,
        in_specs=(
            clips,
            clips,
            vector,
            vector,
            matrix,
            vector,
            vector,
            matrix,
            vector,
            vector,
            vector,
            matrix,
            vector,
            matrix,
            vector,
        ),
        out_specs=(
            clips,
            clips,
            vector,
            vector,
            matrix,
            vector,
            vector,
            matrix,
            vector,
            vector,
            vector,
            matrix,
            vector,
            matrix,
            vector,
            P(),
        ),
        check_vma=False,
    )
```

```python
import functools

import jax
import jax.numpy as jnp
from jax import lax
from jax.experimental import pallas as pl
from jax.experimental.pallas import tpu as pltpu
from jax.sharding import PartitionSpec as P

HEADS = 12
EPS = 1e-06
BLOCKS = 8
HALF = BLOCKS // 2
SMALL = 128
MIB = 1024 * 1024

f32 = jnp.float32
bf16 = jnp.bfloat16

ANY = pl.BlockSpec(memory_space=pl.ANY)
HBM = pl.BlockSpec(memory_space=pltpu.HBM)
FULL = pl.BlockSpec(memory_space=pltpu.VMEM)
SCALAR = pl.BlockSpec(memory_space=pltpu.SMEM)


def nn(a, b):
    return lax.dot_general(a, b, (((1,), (0,)), ((), ())), preferred_element_type=f32)


def nt(a, b):
    return lax.dot_general(a, b, (((1,), (1,)), ((), ())), preferred_element_type=f32)


def tn(a, b):
    return lax.dot_general(a, b, (((0,), (0,)), ((), ())), preferred_element_type=f32)


def normalise(values):
    mean_row = jnp.mean(values, axis=-1, keepdims=True)
    centered = values - mean_row
    spread = jnp.mean(centered * centered, axis=-1, keepdims=True)
    inverse = lax.rsqrt(spread + EPS)
    return centered * inverse, inverse


def norm_back(grad, normed, inverse):
    first = jnp.mean(grad, axis=-1, keepdims=True)
    second = jnp.mean(grad * normed, axis=-1, keepdims=True)
    return inverse * (grad - first - normed * second)


def gelu_both(values):
    cdf = 0.5 * (1.0 + lax.erf(values * (0.5**0.5)))
    density = 0.3989422804014327 * jnp.exp(-0.5 * values * values)
    return values * cdf, cdf + values * density


def sems(count):
    return pltpu.SemaphoreType.DMA((count,))


def start_all(pairs, sem, first=0):
    copies = [pltpu.make_async_copy(a, b, sem.at[first + k]) for k, (a, b) in enumerate(pairs)]
    for copy in copies:
        copy.start()
    return copies


def wait_all(copies):
    for copy in copies:
        copy.wait()


def rows_in_order(idx, pieces, target, columns=None):
    for i, piece in enumerate(pieces):
        count = piece.shape[0]
        rows = pl.ds(pl.multiple_of(idx[i] * count, 16), count)
        for source, to, size in columns or [(0, 0, piece.shape[1])]:
            target[rows, to : to + size] = piece[:, source : source + size]


def columns_by_place(idx, pieces, target, tile, places):
    for i, piece in enumerate(pieces):
        count = piece.shape[0]
        rows = pl.ds(pl.multiple_of(idx[i] * count, 16), count)
        for k, place in enumerate(places):
            source = pl.ds(pl.multiple_of(idx[place] * tile, 128), tile)
            target[rows, k * tile : (k + 1) * tile] = piece[:, source]


def rows_by_place(idx, target, value):
    part = value.shape[0] // BLOCKS
    for b in range(BLOCKS):
        to = pl.multiple_of(idx[BLOCKS + b] * part, 16)
        target[pl.ds(to, part)] = value[b * part : (b + 1) * part]


def beside(one, two):
    return jnp.concatenate([one[...], two[...]], axis=1)


def below(one, two):
    return jnp.concatenate([one[...], two[...]], axis=0)


def lanes_of(head_dim):
    return lax.broadcasted_iota(jnp.int32, (1, 2 * head_dim), 1) < head_dim


def stack_pair(pair, left):
    zero = jnp.zeros_like(pair)
    return jnp.concatenate([jnp.where(left, pair, zero), jnp.where(left, zero, pair)], axis=0)


def merge_pair(stacked, left):
    half = stacked.shape[0] // 2
    return jnp.where(left, stacked[:half], stacked[half:])


KERNELS = {
    "pack": (1, 8),
    "turn_rows": (1, 8),
    "norm_input": (0.01, 12),
    "attention_forward": (0.01, 28),
    "left_operands": (8, 16),
    "proj_forward": (0.01, 16),
    "expand_first": (0.01, 24),
    "expand_second": (25, 20),
    "shrink_weight_grad": (5, 16),
    "hidden_back": (14, 20),
    "middle_back": (45, 28),
    "expand_weight_grad": (14, 16),
    "heads_back": (20, 16),
    "attention_weight_grad": (20, 16),
    "last_weight_grad": (10, 12),
    "input_sums": (10, 20),
    "shrink_forward": (8, 16),
    "input_back": (8, 12),
    "combine": (0.5, 12),
    "cut_half": (0.5, 12),
    "join_halves": (0.5, 12),
    "finish_down": (1, 12),
    "finish_up": (1, 12),
    "finish_attention": (1, 12),
}
SCALE = 1.0


class Far:
    def __init__(self, array):
        self.array = array

    def operand(self):
        return pltpu.with_memory_space_constraint(self.array, pltpu.HBM)

    def result(self):
        return pltpu.HBM(self.array.shape, self.array.dtype)


TOKEN = jax.ShapeDtypeStruct((8, 128), f32)


def call(kernel, name, out_shape, scratch, inputs, after=()):
    given, skip, many = len(inputs), len(after), len(out_shape)
    specs = [HBM if isinstance(a, Far) else SCALAR if a.dtype == jnp.int32 else FULL for a in inputs]
    outs = [HBM if isinstance(o, Far) else FULL for o in out_shape] + [FULL]
    micros, mib = KERNELS[name]

    def run(*refs):
        token = refs[given + skip + many]
        token[...] = jnp.zeros(token.shape, f32)
        kernel(*refs[:given], *refs[given + skip : given + skip + many], *refs[given + skip + many + 1 :])

    return pl.pallas_call(
        run,
        out_shape=[o.result() if isinstance(o, Far) else o for o in out_shape] + [TOKEN],
        in_specs=specs + [FULL if a.shape == TOKEN.shape else ANY for a in after],
        out_specs=outs,
        scratch_shapes=scratch,
        compiler_params=pltpu.CompilerParams(vmem_limit_bytes=mib * MIB),
        cost_estimate=pl.CostEstimate(
            flops=int(micros * SCALE * 1e9), bytes_accessed=0, transcendentals=0
        ),
        name=name,
    )(*[a.operand() if isinstance(a, Far) else a for a in inputs], *after)


def combine(sums, after=()):
    arrays = [a for terms in sums for a in terms]

    def kernel(*refs):
        at = 0
        for terms, out in zip(sums, refs[len(arrays) :]):
            total = refs[at][...].astype(f32)
            for k in range(1, len(terms)):
                total = total + refs[at + k][...].astype(f32)
            out[...] = total.astype(out.dtype)
            at += len(terms)

    shapes = [jax.ShapeDtypeStruct(terms[0].shape, terms[0].dtype) for terms in sums]
    return call(kernel, "combine", shapes, [], arrays, after)


def side_by_side(sums, after=()):
    arrays = [a for some in sums for terms in some for a in terms]

    def kernel(*refs):
        refs = list(refs)
        outs = refs[len(arrays) :]
        for some, out in zip(sums, outs):
            at = 0
            for terms in some:
                values = [refs.pop(0)[...].astype(f32) for _ in terms]
                total = values[0]
                for value in values[1:]:
                    total = total + value
                out[:, at : at + total.shape[1]] = total.astype(out.dtype)
                at += total.shape[1]

    shapes = [
        jax.ShapeDtypeStruct((some[0][0].shape[0], sum(terms[0].shape[1] for terms in some)), bf16) for some in sums
    ]
    return call(kernel, "combine", shapes, [], arrays, after)


def tie(values, after):
    def nothing(*refs):
        pass

    n = len(values)
    return pl.pallas_call(
        nothing,
        out_shape=[jax.ShapeDtypeStruct(v.shape, v.dtype) for v in values],
        in_specs=[ANY] * n + [FULL if a.shape == TOKEN.shape else ANY for a in after],
        out_specs=[ANY] * n,
        input_output_aliases={i: i for i in range(n)},
        compiler_params=pltpu.CompilerParams(vmem_limit_bytes=MIB),
        name="tie",
    )(*values, *after)


def pack(qkv_ref, proj_ref, down_ref, vectors_ref, out_o, down_o, sem):
    cols, width = qkv_ref.shape[1], proj_ref.shape[1]
    pairs = [(qkv_ref, out_o.at[:, pl.ds(0, cols)]), (proj_ref, out_o.at[:, pl.ds(cols, width)])]
    here = start_all(pairs + [(down_ref, down_o)], sem)
    out_o[:, cols + width :] = vectors_ref[...].astype(f32).T.astype(bf16)
    wait_all(here)


def norm_input(x_ref, normed_o):
    normed_o[...] = normalise(x_ref[...].astype(f32))[0]


def turn_rows(source, out_o):
    out_o[...] = source[...].T


def attention_forward(clips, rows, seq, idx, normed, *refs):
    pieces = refs[:BLOCKS]
    attended, n1_o, mixed_o, probs_o, small_o, up_shift_o = refs[BLOCKS : BLOCKS + 6]
    weights_o, proj_o, weights, small_block, mixed, probs_all, sem = refs[BLOCKS + 6 :]
    width = normed.shape[1]
    pair = 2 * (width // HEADS)
    rows_in_order(idx, pieces, weights, [(0, 0, 3 * width)])
    rows_in_order(idx, pieces, small_block, [(4 * width, 0, SMALL)])
    rows_in_order(idx, pieces, proj_o, [(3 * width, 0, width)])
    gone = start_all([(weights, weights_o)], sem, 3)
    small = small_block[...].astype(f32).T
    small_o[...] = small[:16]
    up = [small[8 + k : 9 + k] for k in range(4)]
    part = width // BLOCKS
    for s in range(BLOCKS):
        up_shift_o[s] = jnp.concatenate([u[:, part * s : part * (s + 1)] for u in up], axis=1)
    n1 = (normed[...] * small[0:1] + small[1:2]).astype(bf16)
    for t in range(3):
        acc = nn(n1, weights[:, width * t : width * (t + 1)])
        if t == 0:
            acc = acc + small[2:3]
        if t == 2:
            acc = acc + small[3:4]
        mixed[:, width * t : width * (t + 1)] = acc.astype(bf16)
    gone += start_all([(mixed, mixed_o)], sem)
    n1_o[...] = n1
    left = lanes_of(width // HEADS)
    valid = lax.broadcasted_iota(jnp.int32, (1, rows), 1) < seq
    scale = (width // HEADS) ** (-0.5)

    def probs_copy(p):
        at = pl.ds(p * clips, clips)
        return pltpu.make_async_copy(probs_all.at[at], probs_o.at[at], sem.at[4 + p])

    def heads(p, carry):
        lane = pl.multiple_of(p * pair, pair)
        for c in range(clips):
            here = pl.ds(c * rows, rows)
            q = mixed[here, pl.ds(lane, pair)]
            k = mixed[here, pl.ds(lane + width, pair)]
            v = mixed[here, pl.ds(lane + 2 * width, pair)]
            scores = nt(stack_pair(q, left), k) * scale
            scores = jnp.where(valid, scores, -1e30)
            peak = jnp.max(scores, axis=-1, keepdims=True)
            raised = jnp.exp(scores - peak)
            total = jnp.sum(raised, axis=-1, keepdims=True)
            probs = (raised * (1.0 / total)).astype(bf16)
            probs_all[p * clips + c] = probs
            attended[here, pl.ds(lane, pair)] = merge_pair(nn(probs, v), left).astype(bf16)
        probs_copy(p).start()
        return carry

    lax.fori_loop(0, HEADS // 2, heads, 0, unroll=2)

    def gone_heads(p, carry):
        probs_copy(p).wait()
        return carry

    lax.fori_loop(0, HEADS // 2, gone_heads, 0)
    wait_all(gone)


def proj_forward(x_ref, attended, small, weights, middle_far, n2_o, middle, sem):
    value = x_ref[...].astype(f32) + (nn(attended[...], weights[...]) + small[4:5])
    middle[...] = value
    gone = start_all([(middle, middle_far)], sem)
    normed, inverse = normalise(value)
    n2_o[...] = (normed * small[5:6] + small[6:7]).astype(bf16)
    wait_all(gone)


def left_operands(idx, n1, attended, n2, send_o, keep_o, turned):
    width = n1.shape[1]
    half, part = width // 2, width // BLOCKS
    for k, source in enumerate((n1, attended, n2)):
        turned[k] = source[...].T
        for p in range(BLOCKS):
            to = k * half + p % HALF * part
            rows = pl.ds(pl.multiple_of(idx[p] * part, 16), part)
            (send_o if p < HALF else keep_o)[to : to + part] = turned[k, rows]


def expand_tiles(start, idx, n2_ref, shift_ref, weights, hidden_o, slope_far, hidden_far, pre, slope, sem):
    width = n2_ref.shape[1]
    step = 256
    gone = []

    def multiply(t, c):
        cols = slice(c * step, (c + 1) * step)
        pre[t, :, cols] = nn(n2_ref[...], weights[t, :, cols])

    for c in range(width // step):
        multiply(0, c)
    for t in range(2):
        shift = jnp.concatenate([shift_ref[idx[2 * (start + t) + k]] for k in range(2)], axis=1)
        for c in range(width // step):
            cols = slice(c * step, (c + 1) * step)
            if t == 0:
                multiply(1, c)
            act, derivative = gelu_both(pre[t, :, cols] + shift[:, cols])
            hidden_o[t, :, cols] = act.astype(bf16)
            slope[t, :, cols] = derivative.astype(bf16)
        gone += start_all([(hidden_o.at[t], hidden_far.at[t]), (slope.at[t], slope_far.at[t])], sem, 2 * t)
    return gone


def expand_first(idx, n2_ref, shift_ref, *refs):
    pieces = refs[:BLOCKS]
    hidden_o, two_o, slope_far, hidden_far, up_far, one, pre, slope, sem = refs[BLOCKS:]
    tile = n2_ref.shape[1] // 2
    for t in range(2):
        columns_by_place(idx, pieces, one.at[t], tile, (2 * t, 2 * t + 1))
    gone = start_all([(one, up_far.at[pl.ds(0, 2)])], sem, 4)
    gone += expand_tiles(0, idx, n2_ref, shift_ref, one, hidden_o, slope_far, hidden_far, pre, slope, sem)
    for t in range(2):
        columns_by_place(idx, pieces, two_o.at[t], tile, (2 * t + 4, 2 * t + 5))
    gone += start_all([(two_o, up_far.at[pl.ds(2, 2)])], sem, 5)
    wait_all(gone)


def expand_second(*refs):
    wait_all(expand_tiles(2, *refs))


def shrink_weight_grad(ogt, ogt_sibling, own, sibling, *outs):
    left = beside(ogt, ogt_sibling)
    for t in range(2):
        grad = nn(left, below(own.at[t], sibling.at[t])).astype(bf16)
        tile = grad.shape[1] // 2
        for k in range(2):
            outs[2 * t + k][...] = grad[:, k * tile : (k + 1) * tile]


def expand_weight_grad(idx, own_left, sibling_left, own, sibling, *outs):
    half = own_left.shape[0] // 3
    part = half // HALF
    at = pl.ds(2 * half, half)
    left = beside(own_left.at[at], sibling_left.at[at])
    for t in range(4):
        grad = nn(left, below(own.at[t], sibling.at[(t + 2) % 4])).astype(bf16)
        tile = grad.shape[1] // 2
        for k in range(2):
            to = pl.multiple_of(idx[2 * t + k] * tile, 128)
            for b in range(HALF):
                outs[b][:, pl.ds(to, tile)] = grad[b * part : (b + 1) * part, k * tile : (k + 1) * tile]


def rows_out(grad, outs, columns):
    part = grad.shape[0] // HALF
    for b in range(HALF):
        outs[b][:, columns] = grad[b * part : (b + 1) * part].astype(bf16)


def attention_weight_grad(own_left, sibling_left, own_low, sibling_low, own_mixed, sibling_mixed, *outs):
    width = own_low.shape[1]
    half = width // 2
    for k, right, columns in (
        (1, below(own_low, sibling_low), slice(0, width)),
        (0, below(own_mixed, sibling_mixed), slice(width, None)),
    ):
        at = pl.ds(k * half, half)
        rows_out(nn(beside(own_left.at[at], sibling_left.at[at]), right), outs, columns)


def last_weight_grad(own_left, sibling_left, own_mixed, sibling_mixed, *outs):
    at = pl.ds(0, own_left.shape[0] // 3)
    left = beside(own_left.at[at], sibling_left.at[at])
    rows_out(nn(left, below(own_mixed, sibling_mixed)), outs, slice(None))


def hidden_back(idx, og_ref, slope_one, slope_two, *refs):
    down_pieces, (grad_pre, sums_o, down_far, slope, sem) = refs[:BLOCKS], refs[BLOCKS:]
    tile = down_pieces[0].shape[0]
    here = [
        start_all([((slope_one if t < 2 else slope_two).at[t % 2], slope.at[t])], sem, BLOCKS + t)
        for t in range(4)
    ]
    pairs = [(piece, down_far.at[i // 2, pl.ds(i % 2 * tile, tile)]) for i, piece in enumerate(down_pieces)]
    gone = start_all(pairs, sem)
    for t in range(grad_pre.shape[0]):
        down = below(down_pieces[2 * t], down_pieces[2 * t + 1])
        grad_hidden = nt(og_ref[...], down)
        wait_all(here[t])
        gp = (grad_hidden * slope[t].astype(f32)).astype(bf16)
        grad_pre[t] = gp
        sums = jnp.sum(gp.astype(f32), axis=0, keepdims=True)
        for k in range(2):
            sums_o[idx[2 * t + k]] = sums[:, k * tile : (k + 1) * tile]
    wait_all(gone)


def middle_back(og_ref, small_ref, weights, middle_ref, up_ref, grad_pre, *refs):
    grad_middle_o, low_o, grad_att_o, vectors_o, up, middle, sem = refs

    def up_copy(t):
        return pltpu.make_async_copy(up_ref.at[t], up.at[t], sem.at[t])

    for t in range(4):
        up_copy(t).start()
    here = start_all([(middle_ref, middle)], sem, 4)
    grad_middle_o[...] = jnp.zeros(grad_middle_o.shape, f32)

    def step(t, carry):
        up_copy(t).wait()
        grad_middle_o[...] += nt(grad_pre[t], up[t])
        return carry

    lax.fori_loop(0, 4, step, 0)
    wait_all(here)
    gn2 = grad_middle_o[...]
    normed, inverse = normalise(middle[...])
    og = og_ref[...].astype(f32)
    value = og + norm_back(gn2 * small_ref[5:6], normed, inverse)
    grad_middle_o[...] = value
    low = value.astype(bf16)
    low_o[...] = low
    grad_att_o[...] = nt(low, weights[...]).astype(bf16)
    vectors_o[0:1] = jnp.sum(low.astype(f32), axis=0, keepdims=True)
    vectors_o[1:2] = jnp.sum(gn2 * normed, axis=0, keepdims=True)
    vectors_o[2:3] = jnp.sum(gn2, axis=0, keepdims=True)
    vectors_o[3:4] = jnp.sum(og, axis=0, keepdims=True)


def heads_back(half, clips, rows, grad_att, mixed_ref, probs_ref, grad_mixed_o, mixed, probs_all, sem):
    width = grad_att.shape[1]
    group = width // 2
    head_dim = width // HEADS
    pair = 2 * head_dim
    count = group // pair
    left = lanes_of(head_dim)
    scale = head_dim ** (-0.5)
    arrived = []
    for p in range(count):
        at = half * group + p * pair
        pairs = [
            (mixed_ref.at[:, pl.ds(k * width + at, pair)], mixed.at[:, pl.ds(k * group + p * pair, pair)])
            for k in range(3)
        ]
        source = pl.ds((half * count + p) * clips, clips)
        pairs.append((probs_ref.at[source], probs_all.at[pl.ds(p * clips, clips)]))
        arrived.append(start_all(pairs, sem, 4 * p))
    for p in range(count):
        wait_all(arrived[p])
        lanes = slice(p * pair, (p + 1) * pair)
        for c in range(clips):
            here = pl.ds(c * rows, rows)
            q, k, v = (mixed[here, t * group + p * pair : t * group + (p + 1) * pair] for t in range(3))
            low_probs = probs_all[p * clips + c]
            probs = low_probs.astype(f32)
            at = half * group + p * pair
            grad = stack_pair(grad_att[here, at : at + pair], left)
            grad_probs = nt(grad, v)
            inner = jnp.sum(probs * grad_probs, axis=-1, keepdims=True)
            grad_scores = (probs * (grad_probs - inner)).astype(bf16)
            gq = merge_pair(nn(grad_scores, k), left) * scale
            gk = tn(grad_scores, stack_pair(q, left)) * scale
            gv = tn(low_probs, grad)
            for t, value in enumerate((gq, gk, gv)):
                grad_mixed_o[here, t * group + p * pair : t * group + (p + 1) * pair] = value.astype(bf16)


def input_sums(first, second, x_ref, vectors_ref, sums_ref, weights_ref, gn1_o, vectors_o, weights, gn1_all, sem):
    width = x_ref.shape[1]
    group = width // 2
    part = width // BLOCKS
    here = []
    for g in range(2):
        pairs = []
        for k in range(3):
            source = weights_ref.at[:, pl.ds(k * width + g * group, group)]
            pairs.append((source, weights.at[g, :, pl.ds(k * group, group)]))
        here.append(start_all(pairs, sem, 1 + 3 * g))
    normed, inverse = normalise(x_ref[...].astype(f32))

    def sum_of(ref, k):
        return jnp.sum(ref[:, k * group : (k + 1) * group].astype(f32), axis=0, keepdims=True)

    vectors_o[2:3] = jnp.concatenate([sum_of(first, 0), sum_of(second, 0)], axis=1)
    vectors_o[3:4] = jnp.concatenate([sum_of(first, 2), sum_of(second, 2)], axis=1)
    vectors_o[4:8] = vectors_ref[0:4]
    for k in range(4):
        vectors_o[8 + k : 9 + k] = jnp.concatenate(
            [sums_ref[s][:, part * k : part * (k + 1)] for s in range(BLOCKS)], axis=1
        )
    vectors_o[12:] = jnp.zeros((4, width), f32)
    gn1 = None
    for g, grad in enumerate((first, second)):
        wait_all(here[g])
        more = nt(grad[...], weights[g])
        gn1 = more if gn1 is None else gn1 + more
    gn1_all[...] = gn1
    gone = start_all([(gn1_all, gn1_o)], sem)
    vectors_o[0:1] = jnp.sum(gn1 * normed, axis=0, keepdims=True)
    vectors_o[1:2] = jnp.sum(gn1, axis=0, keepdims=True)
    wait_all(gone)


def shrink_forward(start, clips, rows, seq, small_ref, hidden_ref, base_ref, down_ref, out_o, hidden, base, down, sem):
    here = []
    for t in range(2):
        here.append(start_all([(down_ref.at[start + t], down.at[t]), (hidden_ref.at[t], hidden.at[t])], sem, 2 * t))
    base_here = start_all([(base_ref, base)], sem, 4)
    total = None
    for t in range(2):
        wait_all(here[t])
        more = nn(hidden[t], down[t])
        total = more if total is None else total + more
    wait_all(base_here)
    total = total + base[...]
    if start == 0:
        out_o[...] = total + small_ref[7:8]
    else:
        for c in range(clips):
            out_o[:, c, :] = total[c * rows : c * rows + seq].astype(bf16)


def input_back(clips, rows, seq, gn1_ref, middle_ref, x_ref, small_ref, out_o):
    normed, inverse = normalise(x_ref[...].astype(f32))
    grad = middle_ref[...] + norm_back(gn1_ref[...] * small_ref[0:1], normed, inverse)
    for c in range(clips):
        out_o[:, c, :] = grad[c * rows : c * rows + seq]


def half_of(ref, axis, place):
    size = ref.shape[axis] // 2
    at = pl.ds(pl.multiple_of(place * size, 128), size)
    return ref.at[at] if axis == 0 else ref.at[:, at]


def cut_half(axis, bit, counts, idx, *refs):
    terms, (send_o, keep_o, whole) = list(refs[:-3]), refs[-3:]
    at = 0
    for count in counts:
        some = [terms.pop(0) for _ in range(count)]
        total = some[0][...].astype(f32)
        for term in some[1:]:
            total = total + term[...].astype(f32)
        size = total.shape[axis]
        (whole.at[at : at + size] if axis == 0 else whole.at[:, at : at + size])[...] = total.astype(bf16)
        at += size
    send_o[...] = half_of(whole, axis, 1 - idx[bit])[...]
    keep_o[...] = half_of(whole, axis, idx[bit])[...]


def join_halves(axis, bit, idx, own, other, out_o):
    half_of(out_o, axis, idx[bit])[...] = own[...].astype(out_o.dtype)
    half_of(out_o, axis, 1 - idx[bit])[...] = other[...].astype(out_o.dtype)


def squares_of(ref, sums_o):
    sums_o[...] = jnp.broadcast_to(jnp.sum(ref[...] * ref[...]), sums_o.shape)


def finish_down(idx, own, other, out_o, sums_o, whole):
    join_halves(0, 2 * BLOCKS, idx, own, other, whole)
    out_o[...] = whole[...].T
    squares_of(whole, sums_o)


def finish_up(idx, own, other, out_o, sums_o):
    join_halves(1, 2 * BLOCKS, idx, own, other, out_o)
    squares_of(out_o, sums_o)


def finish_attention(idx, own, other, vectors, sums, qkv_o, proj_o, sums_o, whole):
    join_halves(1, 2 * BLOCKS, idx, own, other, whole)
    width = proj_o.shape[1]
    group = width // 2
    proj_o[...] = whole[:, :width]
    for k in range(3):
        for g in range(2):
            at = width + (3 * g + k) * group
            to = k * width + g * group
            qkv_o[:, to : to + group] = whole[:, at : at + group]
    squares_of(whole, sums_o)
    sums_o[...] += sums[...] + jnp.sum(vectors[...] * vectors[...])


def cores(values):
    return lax.ppermute(values, "wide", [(i, i ^ 1) for i in range(BLOCKS)])


def near(values):
    return lax.ppermute(values, "wide", [(i, i ^ (4 if i & 1 else 2)) for i in range(BLOCKS)])


def across(values):
    return lax.ppermute(values, "wide", [(i, i ^ 6) for i in range(BLOCKS)])


def cross(values):
    return lax.ppermute(values, "wide", [(i, i ^ (2 if i & 1 else 4)) for i in range(BLOCKS)])


class Scatter:
    def __init__(self, blocks):
        self.far, self.other, self.first, self.own = blocks
        self.came_far = cross(self.far)

    def pass_on(self, after):
        first, token = combine([[self.first, self.came_far]], after)
        (other,) = tie([self.other], [token])
        self.came_first, self.came_other = near(first), cross(other)
        return token

    def total(self):
        return [self.own, self.came_other, self.came_first]


class Halves:
    def __init__(self, idx, axis):
        self.idx, self.axis, self.steps = idx, axis, 0

    def send(self, values, bit):
        self.came = lax.ppermute(values, "narrow", [(i, i ^ bit) for i in range(4)])

    def cut(self, sums, bit, after):
        whole = list(sums[0][0].shape)
        whole[self.axis] = sum(terms[0].shape[self.axis] for terms in sums)
        shape = list(whole)
        shape[self.axis] //= 2
        out = jax.ShapeDtypeStruct(tuple(shape), bf16)
        send, self.keep, token = call(
            functools.partial(cut_half, self.axis, 2 * BLOCKS + bit - 1, [len(terms) for terms in sums]),
            "cut_half",
            [out, out],
            [pltpu.VMEM(tuple(whole), bf16)],
            [self.idx, *(term for terms in sums for term in terms)],
            after,
        )
        self.send(send, bit)
        return token

    def one(self, sums, after):
        return self.cut(sums, 1, after)

    def two(self, after):
        return self.cut([[self.keep, self.came]], 2, after)

    def three(self, after):
        self.keep, token = combine([[self.keep, self.came]], after)
        self.send(self.keep, 2)
        return token

    def four(self, after):
        shape = list(self.keep.shape)
        shape[self.axis] *= 2
        self.keep, token = call(
            functools.partial(join_halves, self.axis, 2 * BLOCKS + 1),
            "join_halves",
            [jax.ShapeDtypeStruct(tuple(shape), bf16)],
            [],
            [self.idx, self.keep, self.came],
            after,
        )
        self.send(self.keep, 1)
        return token


class Gather:
    def __init__(self, own):
        self.own, self.first, self.other = own, near(own), cross(own)

    def direct(self):
        self.far = across(self.own)

    def forward(self, after):
        self.first, self.other = tie([self.first, self.other], after)
        self.far = cross(self.first)

    def parts(self, after=()):
        mine = [self.far, self.other, self.first]
        if after:
            mine = list(tie(mine, after))
        mine.append(self.own)
        return [cores(m) for m in mine] + mine

    def early(self):
        self.ahead = [cores(m) for m in (self.other, self.first, self.own)]

    def late(self, after):
        (far,) = tie([self.far], self.ahead + after)
        return [cores(far)] + self.ahead + [far, self.other, self.first, self.own]

    def parts_early(self):
        early = [cores(m) for m in (self.other, self.first, self.own)]
        (far,) = tie([self.far], early)
        return [cores(far)] + early + [far, self.other, self.first, self.own]


class Everywhere:
    def __init__(self, value):
        self.hops = [("wide", b, BLOCKS) for b in (1, 2, 4)] + [("narrow", b, 4) for b in (1, 2)]
        self.send(value)

    def send(self, value):
        self.value = value
        if self.hops:
            axis, bit, count = self.hops.pop(0)
            self.came = lax.ppermute(value, axis, [(i, i ^ bit) for i in range(count)])

    def terms(self):
        return [self.value, self.came]


def spread(whole):
    return list(jnp.split(whole, BLOCKS, axis=0))


def reduce_plain(whole):
    return lax.psum(lax.psum_scatter(whole, "wide", scatter_dimension=0, tiled=True), "narrow")


def body(
    fast,
    tokens,
    out_grad,
    first_gain,
    first_shift,
    qkv_weight,
    query_bias,
    value_bias,
    proj_weight,
    proj_bias,
    second_gain,
    second_shift,
    expand_weight,
    expand_bias,
    shrink_weight,
    shrink_bias,
):
    clips, seq, width = tokens.shape
    rows = -(-seq // 16) * 16
    flat = clips * rows
    part = width // BLOCKS
    hidden = 4 * width
    tile = hidden // BLOCKS
    tiles = hidden // width
    group = width // 2
    pairs = HEADS // 2 * clips
    first_cols = width + 3 * group
    second_cols = 3 * group
    own = first_gain.shape[0]
    gather_plain = functools.partial(lax.all_gather, axis_name="wide", axis=0, tiled=True)

    def shape(*dims, dtype=bf16):
        return jax.ShapeDtypeStruct(dims, dtype)

    def vmem(*dims, dtype=bf16):
        return pltpu.VMEM(dims, dtype)

    if fast:
        me = lax.axis_index("wide")
        odd = me % 2
        relative = [
            jnp.where(odd == 1, b, a) for a, b in zip((7, 3, 5, 1, 6, 4, 2, 0), (7, 5, 3, 1, 6, 2, 4, 0))
        ]
        order = jnp.stack(relative) ^ me
        where = jnp.sum(
            jnp.where(order[None, :] == jnp.arange(BLOCKS)[:, None], jnp.arange(BLOCKS)[None, :], 0),
            axis=1,
        )
        line = lax.axis_index("narrow")
        idx = jnp.concatenate([order, where, jnp.stack([line % 2, line // 2])]).astype(jnp.int32)
    else:
        idx = jnp.concatenate([jnp.arange(BLOCKS), jnp.arange(BLOCKS)]).astype(jnp.int32)

    vectors = [
        first_gain,
        first_shift,
        query_bias,
        value_bias,
        proj_bias,
        second_gain,
        second_shift,
        shrink_bias,
    ]
    block = jnp.concatenate([jnp.stack(vectors), expand_bias.reshape(4, own)], axis=0)
    block = jnp.pad(block, ((0, SMALL - block.shape[0]), (0, 0)))
    packed, down_own, token = call(
        pack,
        "pack",
        [shape(own, 4 * width + SMALL), shape(*shrink_weight.shape)],
        [sems(3)],
        [Far(qkv_weight), Far(proj_weight), Far(shrink_weight), block],
    )
    pad = ((0, 0), (0, rows - seq), (0, 0))
    x = jnp.pad(tokens, pad).reshape(flat, width)
    og = jnp.pad(out_grad, pad).reshape(flat, width)
    ogt, token = call(turn_rows, "turn_rows", [shape(width, flat)], [], [og])

    after = []
    if fast:
        attn = Gather(packed)
        up = Gather(expand_weight)
        attn.forward([x, ogt, idx])
        attn_parts = attn.parts_early()
    else:
        up_parts = spread(gather_plain(expand_weight))
        down_parts = spread(gather_plain(shrink_weight))
        whole = gather_plain(packed)
        bias = whole[:, 4 * width + 8 : 4 * width + 12].reshape(width // own, own, 4)
        bias = bias.transpose(0, 2, 1).reshape(BLOCKS, 4, part).transpose(0, 2, 1).reshape(width, 4)
        attn_parts = spread(whole.at[:, 4 * width + 8 : 4 * width + 12].set(bias))

    def sibling(array):
        return cores(array) if fast else jnp.zeros_like(array)

    ogt_sibling = sibling(ogt)
    normed, token = call(norm_input, "norm_input", [shape(flat, width, dtype=f32)], [], [x])
    attended, n1, mixed, probs, small, up_shift, w_qkv, w_proj, token = call(
        functools.partial(attention_forward, clips, rows, seq),
        "attention_forward",
        (
            shape(flat, width),
            shape(flat, width),
            Far(shape(flat, 3 * width)),
            Far(shape(pairs, 2 * rows, rows)),
            shape(16, width, dtype=f32),
            shape(BLOCKS, 1, tile, dtype=f32),
            Far(shape(width, 3 * width)),
            shape(width, width),
        ),
        [vmem(width, 3 * width), vmem(width, SMALL), vmem(flat, 3 * width), vmem(pairs, 2 * rows, rows), sems(4 + HEADS // 2)],
        [idx, normed, *attn_parts],
    )
    if fast:
        up.forward([token])
        up.early()
    middle, n2, token = call(
        proj_forward,
        "proj_forward",
        (Far(shape(flat, width, dtype=f32)), shape(flat, width)),
        [vmem(flat, width, dtype=f32), sems(1)],
        [x, attended, small, w_proj],
    )
    if fast:
        up_parts = up.late([token])
        (down_own,) = tie([down_own], [token])
        down = Gather(down_own)
    turned_send, turned_keep, token = call(
        left_operands,
        "left_operands",
        [shape(3 * width // 2, flat)] * 2,
        [vmem(3, width, flat)],
        [idx, n1, attended, n2],
        [token],
    )
    turned_sibling = sibling(turned_send)

    two_tiles = shape(2, flat, width)
    expand_scratch = [vmem(2, flat, width, dtype=f32), vmem(2, flat, width), sems(6)]
    hidden_one, up_two, slope_one, hidden_one_far, up_far, token = call(
        expand_first,
        "expand_first",
        (two_tiles, shape(2, width, width), Far(two_tiles), Far(two_tiles), Far(shape(tiles, width, width))),
        [vmem(2, width, width)] + expand_scratch,
        [idx, n2, up_shift, *up_parts],
        [token],
    )
    hidden_sibling = sibling(hidden_one)
    if fast:
        down.forward([token])
    hidden_two, slope_two, hidden_two_far, token = call(
        expand_second,
        "expand_second",
        (two_tiles, Far(two_tiles), Far(two_tiles)),
        expand_scratch,
        [idx, n2, up_shift, up_two],
        [token],
    )

    def shrink_grad(own_hidden, sibling_hidden):
        return call(
            shrink_weight_grad,
            "shrink_weight_grad",
            [shape(width, tile)] * HALF,
            [],
            [ogt, ogt_sibling, own_hidden, sibling_hidden],
        )

    *down_blocks, token = shrink_grad(hidden_two, hidden_sibling)
    if fast:
        down_sum = Scatter(down_blocks)
        down_parts = down.parts([token])
    grad_pre, sums, down_far, token = call(
        hidden_back,
        "hidden_back",
        [shape(tiles, flat, width), shape(BLOCKS, 1, tile, dtype=f32), Far(shape(tiles, width, width))],
        [vmem(tiles, flat, width), sems(BLOCKS + 4)],
        [idx, og, Far(slope_one), Far(slope_two), *down_parts],
        [turned_sibling],
    )
    grad_pre_sibling = sibling(grad_pre)
    if fast:
        token = down_sum.pass_on([token])
    grad_middle, low, grad_att, sums_two, token = call(
        middle_back,
        "middle_back",
        (shape(flat, width, dtype=f32), shape(flat, width), shape(flat, width), shape(8, width, dtype=f32)),
        [vmem(tiles, width, width), vmem(flat, width, dtype=f32), sems(5)],
        [og, small, w_proj, Far(middle), Far(up_far), grad_pre],
        [token],
    )
    low_sibling = sibling(low)

    def expand_grad(left, left_sibling, after=()):
        return call(
            expand_weight_grad,
            "expand_weight_grad",
            [shape(part, hidden)] * HALF,
            [],
            [idx, left, left_sibling, grad_pre, grad_pre_sibling],
            after,
        )

    *up_blocks, token = expand_grad(turned_keep, turned_sibling, [token])
    if fast:
        up_sum = Scatter(up_blocks)
        down_fold = Halves(idx, 0)
        token = down_fold.one([down_sum.total()], [token])

    def heads(half, after):
        return call(
            functools.partial(heads_back, half, clips, rows),
            "heads_back",
            [shape(flat, 3 * group)],
            [vmem(flat, 3 * group), vmem(pairs // 2, 2 * rows, rows), sems(12)],
            [grad_att, Far(mixed), Far(probs)],
            after,
        )

    first_mixed, token = heads(0, [token, low_sibling])
    first_sibling = sibling(first_mixed)
    if fast:
        token = up_sum.pass_on([token])
        token = down_fold.two([token])
    second_mixed, token = heads(1, [token])
    second_sibling = sibling(second_mixed)
    if fast:
        token = down_fold.three([token])

    def attention_grad(left, left_sibling, after=()):
        return call(
            attention_weight_grad,
            "attention_weight_grad",
            [shape(part, first_cols)] * HALF,
            [],
            [left, left_sibling, low, low_sibling, first_mixed, first_sibling],
            after,
        )

    *first_blocks, token = attention_grad(turned_keep, turned_sibling, [token])

    def last_grad(left, left_sibling, after=()):
        return call(
            last_weight_grad,
            "last_weight_grad",
            [shape(part, second_cols)] * HALF,
            [],
            [left, left_sibling, second_mixed, second_sibling],
            after,
        )

    *second_blocks, token = last_grad(turned_keep, turned_sibling, [token])
    if fast:
        *attn_blocks, token = side_by_side([[[a], [b]] for a, b in zip(first_blocks, second_blocks)], [token])
        attn_sum = Scatter(attn_blocks)
        up_fold = Halves(idx, 1)
        token = up_fold.one([up_sum.total()], [token])
        token = down_fold.four([token])
    gn1, vectors, token = call(
        input_sums,
        "input_sums",
        (Far(shape(flat, width, dtype=f32)), shape(16, width, dtype=f32)),
        [vmem(2, width, 3 * group), vmem(flat, width, dtype=f32), sems(7)],
        [first_mixed, second_mixed, x, sums_two, sums, Far(w_qkv)],
        [token],
    )
    if fast:
        token = attn_sum.pass_on([token])
        token = up_fold.two([token])
        every = Everywhere(vectors)

    def shrink(start, hidden, base, out, after):
        return call(
            functools.partial(shrink_forward, start, clips, rows, seq),
            "shrink_forward",
            [out],
            [vmem(2, flat, width), vmem(flat, width, dtype=f32), vmem(2, width, width), sems(5)],
            [small, Far(hidden), Far(base), Far(down_far)],
            after,
        )

    partial_out, token = shrink(0, hidden_one_far, middle, shape(flat, width, dtype=f32), [token])
    if fast:
        vectors, token = combine([every.terms()], [token])
        every.send(vectors)
        token = up_fold.three([token])
        fold = Halves(idx, 1)
        token = fold.one([attn_sum.total()], [token])
    block_out, token = shrink(2, hidden_two_far, partial_out, shape(seq, clips, width), [token])
    if fast:
        token = fold.two([token])
        token = up_fold.four([token])
        vectors, token = combine([every.terms()], [token])
        every.send(vectors)
        grad_down, sums_down, token = call(
            finish_down,
            "finish_down",
            [shape(tile, width, dtype=f32), TOKEN],
            [vmem(width, tile, dtype=f32)],
            [idx, down_fold.keep, down_fold.came],
            [token],
        )
    tokens_grad, token = call(
        functools.partial(input_back, clips, rows, seq),
        "input_back",
        [shape(seq, clips, width, dtype=f32)],
        [],
        [gn1, grad_middle, x, small],
        [token],
    )

    if fast:
        token = fold.three([token])
        vectors, token = combine([every.terms()], [token])
        every.send(vectors)
        grad_up, sums_up, token = call(
            finish_up,
            "finish_up",
            [shape(part, hidden, dtype=f32), TOKEN],
            [],
            [idx, up_fold.keep, up_fold.came],
            [token],
        )
        vectors, token = combine([every.terms()], [token])
        every.send(vectors)
        token = fold.four([token])
        vectors, token = combine([every.terms()], [token])
        index = me * own
    else:
        none = jnp.zeros_like(turned_send)
        halves = (
            (shrink_grad(hidden_one, hidden_sibling)[:-1], down_blocks),
            (expand_grad(turned_send, none)[:-1], up_blocks),
            (attention_grad(turned_send, none)[:-1], first_blocks),
            (last_grad(turned_send, none)[:-1], second_blocks),
        )
        whole_down = jnp.concatenate([b.T for half in halves[0] for b in half], axis=0)
        grad_down = reduce_plain(whole_down).astype(f32)
        grad_up, grad_first, grad_second = (
            reduce_plain(jnp.concatenate([b for half in pair for b in half], axis=0)).astype(f32)
            for pair in halves[1:]
        )
        vectors = lax.psum(vectors, ("wide", "narrow"))
        index = lax.axis_index("wide") * own
    up_bias = vectors[8:12].reshape(4, BLOCKS, part).transpose(1, 0, 2).reshape(-1)
    up_bias = lax.dynamic_slice(up_bias, (4 * index,), (4 * own,))
    small_grads = lax.dynamic_slice(vectors[:8], (0, index), (8, own))
    if fast:
        own_vectors = jnp.concatenate([small_grads.reshape(-1), up_bias]).reshape(-1, 128)
        own_vectors = jnp.pad(own_vectors, ((0, 16 - own_vectors.shape[0]), (0, 0)))
        grad_qkv, grad_proj, squares, token = call(
            finish_attention,
            "finish_attention",
            [shape(part, 3 * width, dtype=f32), shape(part, width, dtype=f32), TOKEN],
            [vmem(part, hidden, dtype=f32)],
            [idx, fold.keep, fold.came, own_vectors, sums_down + sums_up],
        )
        for perms in ((1,), (2, 4, 6)):
            came = [lax.ppermute(squares, "wide", [(i, i ^ b) for i in range(BLOCKS)]) for b in perms]
            squares = squares + came[0] if len(came) == 1 else (squares + came[0]) + (came[1] + came[2])
        grad_sq_norm = squares[0, 0]
    else:
        grad_proj = grad_first[:, :width]
        grad_qkv = jnp.concatenate(
            [
                g[:, at + k * group : at + (k + 1) * group]
                for k in range(3)
                for g, at in ((grad_first, width), (grad_second, 0))
            ],
            axis=1,
        )
        local = sum(jnp.sum(g * g) for g in (small_grads, up_bias, grad_down, grad_up, grad_first, grad_second))
        grad_sq_norm = lax.psum(local, "wide")
    return (
        block_out.transpose(1, 0, 2),
        tokens_grad.transpose(1, 0, 2),
        small_grads[0],
        small_grads[1],
        grad_qkv,
        small_grads[2],
        small_grads[3],
        grad_proj,
        small_grads[4],
        small_grads[5],
        small_grads[6],
        grad_up,
        up_bias,
        grad_down,
        small_grads[7],
        grad_sq_norm,
    )


def solution(mesh):
    fast = mesh.shape["wide"] == BLOCKS and mesh.shape["narrow"] == 4
    clips = P(("wide", "narrow"), None, None)
    vector = P("wide")
    matrix = P("wide", None)
    return jax.shard_map(
        functools.partial(body, fast),
        mesh=mesh,
        in_specs=(
            clips,
            clips,
            vector,
            vector,
            matrix,
            vector,
            vector,
            matrix,
            vector,
            vector,
            vector,
            matrix,
            vector,
            matrix,
            vector,
        ),
        out_specs=(
            clips,
            clips,
            vector,
            vector,
            matrix,
            vector,
            vector,
            matrix,
            vector,
            vector,
            vector,
            matrix,
            vector,
            matrix,
            vector,
            P(),
        ),
        check_vma=False,
    )
```

```python
import functools

import jax
import jax.numpy as jnp
from jax import lax
from jax.experimental import pallas as pl
from jax.experimental.pallas import tpu as pltpu
from jax.sharding import PartitionSpec as P

HEADS = 12
EPS = 1e-06
BLOCKS = 8
HALF = BLOCKS // 2
SMALL = 128
MIB = 1024 * 1024

f32 = jnp.float32
bf16 = jnp.bfloat16

ANY = pl.BlockSpec(memory_space=pl.ANY)
HBM = pl.BlockSpec(memory_space=pltpu.HBM)
FULL = pl.BlockSpec(memory_space=pltpu.VMEM)
SCALAR = pl.BlockSpec(memory_space=pltpu.SMEM)


def nn(a, b):
    return lax.dot_general(a, b, (((1,), (0,)), ((), ())), preferred_element_type=f32)


def nt(a, b):
    return lax.dot_general(a, b, (((1,), (1,)), ((), ())), preferred_element_type=f32)


def tn(a, b):
    return lax.dot_general(a, b, (((0,), (0,)), ((), ())), preferred_element_type=f32)


def normalise(values):
    mean_row = jnp.mean(values, axis=-1, keepdims=True)
    centered = values - mean_row
    spread = jnp.mean(centered * centered, axis=-1, keepdims=True)
    inverse = lax.rsqrt(spread + EPS)
    return centered * inverse, inverse


def norm_back(grad, normed, inverse):
    first = jnp.mean(grad, axis=-1, keepdims=True)
    second = jnp.mean(grad * normed, axis=-1, keepdims=True)
    return inverse * (grad - first - normed * second)


def gelu_both(values):
    cdf = 0.5 * (1.0 + lax.erf(values * (0.5**0.5)))
    density = 0.3989422804014327 * jnp.exp(-0.5 * values * values)
    return values * cdf, cdf + values * density


def sems(count):
    return pltpu.SemaphoreType.DMA((count,))


def start_all(pairs, sem, first=0):
    copies = [pltpu.make_async_copy(a, b, sem.at[first + k]) for k, (a, b) in enumerate(pairs)]
    for copy in copies:
        copy.start()
    return copies


def wait_all(copies):
    for copy in copies:
        copy.wait()


def rows_in_order(idx, pieces, target, columns=None):
    for i, piece in enumerate(pieces):
        count = piece.shape[0]
        rows = pl.ds(pl.multiple_of(idx[i] * count, 16), count)
        for source, to, size in columns or [(0, 0, piece.shape[1])]:
            target[rows, to : to + size] = piece[:, source : source + size]


def columns_by_place(idx, pieces, target, tile, places):
    for i, piece in enumerate(pieces):
        count = piece.shape[0]
        rows = pl.ds(pl.multiple_of(idx[i] * count, 16), count)
        for k, place in enumerate(places):
            source = pl.ds(pl.multiple_of(idx[place] * tile, 128), tile)
            target[rows, k * tile : (k + 1) * tile] = piece[:, source]


def rows_by_place(idx, target, value):
    part = value.shape[0] // BLOCKS
    for b in range(BLOCKS):
        to = pl.multiple_of(idx[BLOCKS + b] * part, 16)
        target[pl.ds(to, part)] = value[b * part : (b + 1) * part]


def beside(one, two):
    return jnp.concatenate([one[...], two[...]], axis=1)


def below(one, two):
    return jnp.concatenate([one[...], two[...]], axis=0)


def lanes_of(head_dim):
    return lax.broadcasted_iota(jnp.int32, (1, 2 * head_dim), 1) < head_dim


def stack_pair(pair, left):
    zero = jnp.zeros_like(pair)
    return jnp.concatenate([jnp.where(left, pair, zero), jnp.where(left, zero, pair)], axis=0)


def merge_pair(stacked, left):
    half = stacked.shape[0] // 2
    return jnp.where(left, stacked[:half], stacked[half:])


KERNELS = {
    "pack": (1, 8),
    "turn_rows": (1, 8),
    "norm_input": (0.01, 12),
    "attention_forward": (0.01, 28),
    "left_operands": (8, 16),
    "proj_forward": (0.01, 16),
    "expand_first": (0.01, 24),
    "expand_second": (25, 20),
    "shrink_weight_grad": (5, 16),
    "hidden_back": (14, 20),
    "middle_back": (45, 28),
    "expand_weight_grad": (14, 16),
    "heads_back": (20, 16),
    "attention_weight_grad": (20, 16),
    "last_weight_grad": (10, 12),
    "input_sums": (10, 20),
    "shrink_forward": (8, 16),
    "input_back": (8, 12),
    "combine": (0.5, 12),
    "cut_half": (0.5, 12),
    "join_halves": (0.5, 12),
    "finish_down": (1, 12),
    "finish_up": (1, 12),
    "finish_attention": (1, 12),
}
SCALE = 1.0


class Far:
    def __init__(self, array):
        self.array = array

    def operand(self):
        return pltpu.with_memory_space_constraint(self.array, pltpu.HBM)

    def result(self):
        return pltpu.HBM(self.array.shape, self.array.dtype)


TOKEN = jax.ShapeDtypeStruct((8, 128), f32)


def call(kernel, name, out_shape, scratch, inputs, after=()):
    given, skip, many = len(inputs), len(after), len(out_shape)
    specs = [HBM if isinstance(a, Far) else SCALAR if a.dtype == jnp.int32 else FULL for a in inputs]
    outs = [HBM if isinstance(o, Far) else FULL for o in out_shape] + [FULL]
    micros, mib = KERNELS[name]

    def run(*refs):
        token = refs[given + skip + many]
        token[...] = jnp.zeros(token.shape, f32)
        kernel(*refs[:given], *refs[given + skip : given + skip + many], *refs[given + skip + many + 1 :])

    return pl.pallas_call(
        run,
        out_shape=[o.result() if isinstance(o, Far) else o for o in out_shape] + [TOKEN],
        in_specs=specs + [FULL if a.shape == TOKEN.shape else ANY for a in after],
        out_specs=outs,
        scratch_shapes=scratch,
        compiler_params=pltpu.CompilerParams(vmem_limit_bytes=mib * MIB),
        cost_estimate=pl.CostEstimate(
            flops=int(micros * SCALE * 1e9), bytes_accessed=0, transcendentals=0
        ),
        name=name,
    )(*[a.operand() if isinstance(a, Far) else a for a in inputs], *after)


def combine(sums, after=()):
    arrays = [a for terms in sums for a in terms]

    def kernel(*refs):
        at = 0
        for terms, out in zip(sums, refs[len(arrays) :]):
            total = refs[at][...].astype(f32)
            for k in range(1, len(terms)):
                total = total + refs[at + k][...].astype(f32)
            out[...] = total.astype(out.dtype)
            at += len(terms)

    shapes = [jax.ShapeDtypeStruct(terms[0].shape, terms[0].dtype) for terms in sums]
    return call(kernel, "combine", shapes, [], arrays, after)


def side_by_side(sums, after=()):
    arrays = [a for some in sums for terms in some for a in terms]

    def kernel(*refs):
        refs = list(refs)
        outs = refs[len(arrays) :]
        for some, out in zip(sums, outs):
            at = 0
            for terms in some:
                values = [refs.pop(0)[...].astype(f32) for _ in terms]
                total = values[0]
                for value in values[1:]:
                    total = total + value
                out[:, at : at + total.shape[1]] = total.astype(out.dtype)
                at += total.shape[1]

    shapes = [
        jax.ShapeDtypeStruct((some[0][0].shape[0], sum(terms[0].shape[1] for terms in some)), bf16) for some in sums
    ]
    return call(kernel, "combine", shapes, [], arrays, after)


def tie(values, after):
    def nothing(*refs):
        pass

    n = len(values)
    return pl.pallas_call(
        nothing,
        out_shape=[jax.ShapeDtypeStruct(v.shape, v.dtype) for v in values],
        in_specs=[ANY] * n + [FULL if a.shape == TOKEN.shape else ANY for a in after],
        out_specs=[ANY] * n,
        input_output_aliases={i: i for i in range(n)},
        compiler_params=pltpu.CompilerParams(vmem_limit_bytes=MIB),
        name="tie",
    )(*values, *after)


def pack(qkv_ref, proj_ref, down_ref, vectors_ref, out_o, down_o, sem):
    cols, width = qkv_ref.shape[1], proj_ref.shape[1]
    pairs = [(qkv_ref, out_o.at[:, pl.ds(0, cols)]), (proj_ref, out_o.at[:, pl.ds(cols, width)])]
    here = start_all(pairs + [(down_ref, down_o)], sem)
    out_o[:, cols + width :] = vectors_ref[...].astype(f32).T.astype(bf16)
    wait_all(here)


def norm_input(x_ref, normed_o):
    normed_o[...] = normalise(x_ref[...].astype(f32))[0]


def turn_rows(source, out_o):
    out_o[...] = source[...].T


def attention_forward(clips, rows, seq, idx, normed, *refs):
    pieces = refs[:BLOCKS]
    attended, n1_o, mixed_o, probs_o, small_o, up_shift_o = refs[BLOCKS : BLOCKS + 6]
    weights_o, proj_o, weights, small_block, mixed, probs_all, sem = refs[BLOCKS + 6 :]
    width = normed.shape[1]
    pair = 2 * (width // HEADS)
    rows_in_order(idx, pieces, weights, [(0, 0, 3 * width)])
    rows_in_order(idx, pieces, small_block, [(4 * width, 0, SMALL)])
    rows_in_order(idx, pieces, proj_o, [(3 * width, 0, width)])
    gone = start_all([(weights, weights_o)], sem, 3)
    small = small_block[...].astype(f32).T
    small_o[...] = small[:16]
    up = [small[8 + k : 9 + k] for k in range(4)]
    part = width // BLOCKS
    for s in range(BLOCKS):
        up_shift_o[s] = jnp.concatenate([u[:, part * s : part * (s + 1)] for u in up], axis=1)
    n1 = (normed[...] * small[0:1] + small[1:2]).astype(bf16)
    for t in range(3):
        acc = nn(n1, weights[:, width * t : width * (t + 1)])
        if t == 0:
            acc = acc + small[2:3]
        if t == 2:
            acc = acc + small[3:4]
        mixed[:, width * t : width * (t + 1)] = acc.astype(bf16)
    gone += start_all([(mixed, mixed_o)], sem)
    n1_o[...] = n1
    left = lanes_of(width // HEADS)
    valid = lax.broadcasted_iota(jnp.int32, (1, rows), 1) < seq
    scale = (width // HEADS) ** (-0.5)

    def probs_copy(p):
        at = pl.ds(p * clips, clips)
        return pltpu.make_async_copy(probs_all.at[at], probs_o.at[at], sem.at[4 + p])

    def heads(p, carry):
        lane = pl.multiple_of(p * pair, pair)
        for c in range(clips):
            here = pl.ds(c * rows, rows)
            q = mixed[here, pl.ds(lane, pair)]
            k = mixed[here, pl.ds(lane + width, pair)]
            v = mixed[here, pl.ds(lane + 2 * width, pair)]
            scores = nt(stack_pair(q, left), k) * scale
            scores = jnp.where(valid, scores, -1e30)
            peak = jnp.max(scores, axis=-1, keepdims=True)
            raised = jnp.exp(scores - peak)
            total = jnp.sum(raised, axis=-1, keepdims=True)
            probs = (raised * (1.0 / total)).astype(bf16)
            probs_all[p * clips + c] = probs
            attended[here, pl.ds(lane, pair)] = merge_pair(nn(probs, v), left).astype(bf16)
        probs_copy(p).start()
        return carry

    lax.fori_loop(0, HEADS // 2, heads, 0, unroll=2)

    def gone_heads(p, carry):
        probs_copy(p).wait()
        return carry

    lax.fori_loop(0, HEADS // 2, gone_heads, 0)
    wait_all(gone)


def proj_forward(x_ref, attended, small, weights, middle_far, n2_o, middle, sem):
    value = x_ref[...].astype(f32) + (nn(attended[...], weights[...]) + small[4:5])
    middle[...] = value
    gone = start_all([(middle, middle_far)], sem)
    normed, inverse = normalise(value)
    n2_o[...] = (normed * small[5:6] + small[6:7]).astype(bf16)
    wait_all(gone)


def left_operands(idx, n1, attended, n2, send_o, keep_o, turned):
    width = n1.shape[1]
    half, part = width // 2, width // BLOCKS
    for k, source in enumerate((n1, attended, n2)):
        turned[k] = source[...].T
        for p in range(BLOCKS):
            to = k * half + p % HALF * part
            rows = pl.ds(pl.multiple_of(idx[p] * part, 16), part)
            (send_o if p < HALF else keep_o)[to : to + part] = turned[k, rows]


def expand_tiles(start, idx, n2_ref, shift_ref, weights, hidden_o, slope_far, hidden_far, pre, slope, sem):
    width = n2_ref.shape[1]
    step = 256
    gone = []

    def multiply(t, c):
        cols = slice(c * step, (c + 1) * step)
        pre[t, :, cols] = nn(n2_ref[...], weights[t, :, cols])

    for c in range(width // step):
        multiply(0, c)
    for t in range(2):
        shift = jnp.concatenate([shift_ref[idx[2 * (start + t) + k]] for k in range(2)], axis=1)
        for c in range(width // step):
            cols = slice(c * step, (c + 1) * step)
            if t == 0:
                multiply(1, c)
            act, derivative = gelu_both(pre[t, :, cols] + shift[:, cols])
            hidden_o[t, :, cols] = act.astype(bf16)
            slope[t, :, cols] = derivative.astype(bf16)
        gone += start_all([(hidden_o.at[t], hidden_far.at[t]), (slope.at[t], slope_far.at[t])], sem, 2 * t)
    return gone


def expand_first(idx, n2_ref, shift_ref, *refs):
    pieces = refs[:BLOCKS]
    hidden_o, two_o, slope_far, hidden_far, up_far, one, pre, slope, sem = refs[BLOCKS:]
    tile = n2_ref.shape[1] // 2
    for t in range(2):
        columns_by_place(idx, pieces, one.at[t], tile, (2 * t, 2 * t + 1))
    gone = start_all([(one, up_far.at[pl.ds(0, 2)])], sem, 4)
    gone += expand_tiles(0, idx, n2_ref, shift_ref, one, hidden_o, slope_far, hidden_far, pre, slope, sem)
    for t in range(2):
        columns_by_place(idx, pieces, two_o.at[t], tile, (2 * t + 4, 2 * t + 5))
    gone += start_all([(two_o, up_far.at[pl.ds(2, 2)])], sem, 5)
    wait_all(gone)


def expand_second(*refs):
    wait_all(expand_tiles(2, *refs))


def shrink_weight_grad(ogt, ogt_sibling, own, sibling, *outs):
    left = beside(ogt, ogt_sibling)
    for t in range(2):
        grad = nn(left, below(own.at[t], sibling.at[t])).astype(bf16)
        tile = grad.shape[1] // 2
        for k in range(2):
            outs[2 * t + k][...] = grad[:, k * tile : (k + 1) * tile]


def expand_weight_grad(idx, own_left, sibling_left, own, sibling, *outs):
    half = own_left.shape[0] // 3
    part = half // HALF
    at = pl.ds(2 * half, half)
    left = beside(own_left.at[at], sibling_left.at[at])
    for t in range(4):
        grad = nn(left, below(own.at[t], sibling.at[(t + 2) % 4])).astype(bf16)
        tile = grad.shape[1] // 2
        for k in range(2):
            to = pl.multiple_of(idx[2 * t + k] * tile, 128)
            for b in range(HALF):
                outs[b][:, pl.ds(to, tile)] = grad[b * part : (b + 1) * part, k * tile : (k + 1) * tile]


def rows_out(grad, outs, columns):
    part = grad.shape[0] // HALF
    for b in range(HALF):
        outs[b][:, columns] = grad[b * part : (b + 1) * part].astype(bf16)


def attention_weight_grad(own_left, sibling_left, own_low, sibling_low, own_mixed, sibling_mixed, *outs):
    width = own_low.shape[1]
    half = width // 2
    for k, right, columns in (
        (1, below(own_low, sibling_low), slice(0, width)),
        (0, below(own_mixed, sibling_mixed), slice(width, None)),
    ):
        at = pl.ds(k * half, half)
        rows_out(nn(beside(own_left.at[at], sibling_left.at[at]), right), outs, columns)


def last_weight_grad(own_left, sibling_left, own_mixed, sibling_mixed, *outs):
    at = pl.ds(0, own_left.shape[0] // 3)
    left = beside(own_left.at[at], sibling_left.at[at])
    rows_out(nn(left, below(own_mixed, sibling_mixed)), outs, slice(None))


def hidden_back(idx, og_ref, slope_one, slope_two, *refs):
    down_pieces, (grad_pre, sums_o, down_far, slope, sem) = refs[:BLOCKS], refs[BLOCKS:]
    tile = down_pieces[0].shape[0]
    here = [
        start_all([((slope_one if t < 2 else slope_two).at[t % 2], slope.at[t])], sem, BLOCKS + t)
        for t in range(4)
    ]
    pairs = [(piece, down_far.at[i // 2, pl.ds(i % 2 * tile, tile)]) for i, piece in enumerate(down_pieces)]
    gone = start_all(pairs, sem)
    for t in range(grad_pre.shape[0]):
        down = below(down_pieces[2 * t], down_pieces[2 * t + 1])
        grad_hidden = nt(og_ref[...], down)
        wait_all(here[t])
        gp = (grad_hidden * slope[t].astype(f32)).astype(bf16)
        grad_pre[t] = gp
        sums = jnp.sum(gp.astype(f32), axis=0, keepdims=True)
        for k in range(2):
            sums_o[idx[2 * t + k]] = sums[:, k * tile : (k + 1) * tile]
    wait_all(gone)


def middle_back(og_ref, small_ref, weights, middle_ref, up_ref, grad_pre, *refs):
    grad_middle_o, low_o, grad_att_o, vectors_o, up, middle, sem = refs

    def up_copy(t):
        return pltpu.make_async_copy(up_ref.at[t], up.at[t], sem.at[t])

    for t in range(4):
        up_copy(t).start()
    here = start_all([(middle_ref, middle)], sem, 4)
    grad_middle_o[...] = jnp.zeros(grad_middle_o.shape, f32)

    def step(t, carry):
        up_copy(t).wait()
        grad_middle_o[...] += nt(grad_pre[t], up[t])
        return carry

    lax.fori_loop(0, 4, step, 0)
    wait_all(here)
    gn2 = grad_middle_o[...]
    normed, inverse = normalise(middle[...])
    og = og_ref[...].astype(f32)
    value = og + norm_back(gn2 * small_ref[5:6], normed, inverse)
    grad_middle_o[...] = value
    low = value.astype(bf16)
    low_o[...] = low
    grad_att_o[...] = nt(low, weights[...]).astype(bf16)
    vectors_o[0:1] = jnp.sum(low.astype(f32), axis=0, keepdims=True)
    vectors_o[1:2] = jnp.sum(gn2 * normed, axis=0, keepdims=True)
    vectors_o[2:3] = jnp.sum(gn2, axis=0, keepdims=True)
    vectors_o[3:4] = jnp.sum(og, axis=0, keepdims=True)


def heads_back(half, clips, rows, grad_att, mixed_ref, probs_ref, grad_mixed_o, mixed, probs_all, sem):
    width = grad_att.shape[1]
    group = width // 2
    head_dim = width // HEADS
    pair = 2 * head_dim
    count = group // pair
    left = lanes_of(head_dim)
    scale = head_dim ** (-0.5)
    arrived = []
    for p in range(count):
        at = half * group + p * pair
        pairs = [
            (mixed_ref.at[:, pl.ds(k * width + at, pair)], mixed.at[:, pl.ds(k * group + p * pair, pair)])
            for k in range(3)
        ]
        source = pl.ds((half * count + p) * clips, clips)
        pairs.append((probs_ref.at[source], probs_all.at[pl.ds(p * clips, clips)]))
        arrived.append(start_all(pairs, sem, 4 * p))
    for p in range(count):
        wait_all(arrived[p])
        lanes = slice(p * pair, (p + 1) * pair)
        for c in range(clips):
            here = pl.ds(c * rows, rows)
            q, k, v = (mixed[here, t * group + p * pair : t * group + (p + 1) * pair] for t in range(3))
            low_probs = probs_all[p * clips + c]
            probs = low_probs.astype(f32)
            at = half * group + p * pair
            grad = stack_pair(grad_att[here, at : at + pair], left)
            grad_probs = nt(grad, v)
            inner = jnp.sum(probs * grad_probs, axis=-1, keepdims=True)
            grad_scores = (probs * (grad_probs - inner)).astype(bf16)
            gq = merge_pair(nn(grad_scores, k), left) * scale
            gk = tn(grad_scores, stack_pair(q, left)) * scale
            gv = tn(low_probs, grad)
            for t, value in enumerate((gq, gk, gv)):
                grad_mixed_o[here, t * group + p * pair : t * group + (p + 1) * pair] = value.astype(bf16)


def input_sums(first, second, x_ref, vectors_ref, sums_ref, weights_ref, gn1_o, vectors_o, weights, gn1_all, sem):
    width = x_ref.shape[1]
    group = width // 2
    part = width // BLOCKS
    here = []
    for g in range(2):
        pairs = []
        for k in range(3):
            source = weights_ref.at[:, pl.ds(k * width + g * group, group)]
            pairs.append((source, weights.at[g, :, pl.ds(k * group, group)]))
        here.append(start_all(pairs, sem, 1 + 3 * g))
    normed, inverse = normalise(x_ref[...].astype(f32))

    def sum_of(ref, k):
        return jnp.sum(ref[:, k * group : (k + 1) * group].astype(f32), axis=0, keepdims=True)

    vectors_o[2:3] = jnp.concatenate([sum_of(first, 0), sum_of(second, 0)], axis=1)
    vectors_o[3:4] = jnp.concatenate([sum_of(first, 2), sum_of(second, 2)], axis=1)
    vectors_o[4:8] = vectors_ref[0:4]
    for k in range(4):
        vectors_o[8 + k : 9 + k] = jnp.concatenate(
            [sums_ref[s][:, part * k : part * (k + 1)] for s in range(BLOCKS)], axis=1
        )
    vectors_o[12:] = jnp.zeros((4, width), f32)
    gn1 = None
    for g, grad in enumerate((first, second)):
        wait_all(here[g])
        more = nt(grad[...], weights[g])
        gn1 = more if gn1 is None else gn1 + more
    gn1_all[...] = gn1
    gone = start_all([(gn1_all, gn1_o)], sem)
    vectors_o[0:1] = jnp.sum(gn1 * normed, axis=0, keepdims=True)
    vectors_o[1:2] = jnp.sum(gn1, axis=0, keepdims=True)
    wait_all(gone)


def shrink_forward(start, clips, rows, seq, small_ref, hidden_ref, base_ref, down_ref, out_o, hidden, base, down, sem):
    here = []
    for t in range(2):
        here.append(start_all([(down_ref.at[start + t], down.at[t]), (hidden_ref.at[t], hidden.at[t])], sem, 2 * t))
    base_here = start_all([(base_ref, base)], sem, 4)
    total = None
    for t in range(2):
        wait_all(here[t])
        more = nn(hidden[t], down[t])
        total = more if total is None else total + more
    wait_all(base_here)
    total = total + base[...]
    if start == 0:
        out_o[...] = total + small_ref[7:8]
    else:
        for c in range(clips):
            out_o[:, c, :] = total[c * rows : c * rows + seq].astype(bf16)


def input_back(clips, rows, seq, gn1_ref, middle_ref, x_ref, small_ref, out_o):
    normed, inverse = normalise(x_ref[...].astype(f32))
    grad = middle_ref[...] + norm_back(gn1_ref[...] * small_ref[0:1], normed, inverse)
    for c in range(clips):
        out_o[:, c, :] = grad[c * rows : c * rows + seq]


def half_of(ref, axis, place):
    size = ref.shape[axis] // 2
    at = pl.ds(pl.multiple_of(place * size, 128), size)
    return ref.at[at] if axis == 0 else ref.at[:, at]


def cut_half(axis, bit, counts, idx, *refs):
    terms, (send_o, keep_o, whole) = list(refs[:-3]), refs[-3:]
    at = 0
    for count in counts:
        some = [terms.pop(0) for _ in range(count)]
        total = some[0][...].astype(f32)
        for term in some[1:]:
            total = total + term[...].astype(f32)
        size = total.shape[axis]
        (whole.at[at : at + size] if axis == 0 else whole.at[:, at : at + size])[...] = total.astype(bf16)
        at += size
    send_o[...] = half_of(whole, axis, 1 - idx[bit])[...]
    keep_o[...] = half_of(whole, axis, idx[bit])[...]


def join_halves(axis, bit, idx, own, other, out_o):
    half_of(out_o, axis, idx[bit])[...] = own[...].astype(out_o.dtype)
    half_of(out_o, axis, 1 - idx[bit])[...] = other[...].astype(out_o.dtype)


def squares_of(ref, sums_o):
    sums_o[...] = jnp.broadcast_to(jnp.sum(ref[...] * ref[...]), sums_o.shape)


def finish_down(idx, own, other, out_o, sums_o, whole):
    join_halves(0, 2 * BLOCKS, idx, own, other, whole)
    out_o[...] = whole[...].T
    squares_of(whole, sums_o)


def finish_up(idx, own, other, out_o, sums_o):
    join_halves(1, 2 * BLOCKS, idx, own, other, out_o)
    squares_of(out_o, sums_o)


def finish_attention(idx, own, other, qkv_o, proj_o, whole):
    join_halves(1, 2 * BLOCKS, idx, own, other, whole)
    width = proj_o.shape[1]
    group = width // 2
    proj_o[...] = whole[:, :width]
    for k in range(3):
        for g in range(2):
            at = width + (3 * g + k) * group
            to = k * width + g * group
            qkv_o[:, to : to + group] = whole[:, at : at + group]


def square_sums(half, one, two, out_o):
    value = half[...].astype(f32)
    out_o[...] = jnp.sum(value * value) + 0.5 * (one[...] + two[...])


def add_pairs(*refs):
    values, out_o = [r[...] for r in refs[:-1]], refs[-1]
    total = values[0] + values[1]
    out_o[...] = total if len(values) == 2 else total + (values[2] + values[3])


def add_vectors(total, vectors, out_o):
    out_o[...] = total[...] + jnp.sum(vectors[...] * vectors[...])


def cores(values):
    return lax.ppermute(values, "wide", [(i, i ^ 1) for i in range(BLOCKS)])


def near(values):
    return lax.ppermute(values, "wide", [(i, i ^ (4 if i & 1 else 2)) for i in range(BLOCKS)])


def across(values):
    return lax.ppermute(values, "wide", [(i, i ^ 6) for i in range(BLOCKS)])


def cross(values):
    return lax.ppermute(values, "wide", [(i, i ^ (2 if i & 1 else 4)) for i in range(BLOCKS)])


class Scatter:
    def __init__(self, blocks):
        self.far, self.other, self.first, self.own = blocks
        self.came_far = cross(self.far)

    def pass_on(self, after):
        first, token = combine([[self.first, self.came_far]], after)
        (other,) = tie([self.other], [token])
        self.came_first, self.came_other = near(first), cross(other)
        return token

    def total(self):
        return [self.own, self.came_other, self.came_first]


class Halves:
    def __init__(self, idx, axis):
        self.idx, self.axis, self.steps = idx, axis, 0

    def send(self, values, bit):
        self.came = lax.ppermute(values, "narrow", [(i, i ^ bit) for i in range(4)])

    def cut(self, sums, bit, after):
        whole = list(sums[0][0].shape)
        whole[self.axis] = sum(terms[0].shape[self.axis] for terms in sums)
        shape = list(whole)
        shape[self.axis] //= 2
        out = jax.ShapeDtypeStruct(tuple(shape), bf16)
        send, self.keep, token = call(
            functools.partial(cut_half, self.axis, 2 * BLOCKS + bit - 1, [len(terms) for terms in sums]),
            "cut_half",
            [out, out],
            [pltpu.VMEM(tuple(whole), bf16)],
            [self.idx, *(term for terms in sums for term in terms)],
            after,
        )
        self.send(send, bit)
        return token

    def one(self, sums, after):
        return self.cut(sums, 1, after)

    def two(self, after):
        return self.cut([[self.keep, self.came]], 2, after)

    def three(self, after):
        self.keep, token = combine([[self.keep, self.came]], after)
        self.send(self.keep, 2)
        return token

    def four(self, after):
        shape = list(self.keep.shape)
        shape[self.axis] *= 2
        self.keep, token = call(
            functools.partial(join_halves, self.axis, 2 * BLOCKS + 1),
            "join_halves",
            [jax.ShapeDtypeStruct(tuple(shape), bf16)],
            [],
            [self.idx, self.keep, self.came],
            after,
        )
        self.send(self.keep, 1)
        return token


class Gather:
    def __init__(self, own):
        self.own, self.first, self.other = own, near(own), cross(own)

    def direct(self):
        self.far = across(self.own)

    def forward(self, after):
        self.first, self.other = tie([self.first, self.other], after)
        self.far = cross(self.first)

    def parts(self, after=()):
        mine = [self.far, self.other, self.first]
        if after:
            mine = list(tie(mine, after))
        mine.append(self.own)
        return [cores(m) for m in mine] + mine

    def early(self):
        self.ahead = [cores(m) for m in (self.other, self.first, self.own)]

    def late(self, after):
        (far,) = tie([self.far], self.ahead + after)
        return [cores(far)] + self.ahead + [far, self.other, self.first, self.own]

    def parts_early(self):
        early = [cores(m) for m in (self.other, self.first, self.own)]
        (far,) = tie([self.far], early)
        return [cores(far)] + early + [far, self.other, self.first, self.own]


class Everywhere:
    def __init__(self, value):
        self.hops = [("wide", b, BLOCKS) for b in (1, 2, 4)] + [("narrow", b, 4) for b in (1, 2)]
        self.send(value)

    def send(self, value):
        self.value = value
        if self.hops:
            axis, bit, count = self.hops.pop(0)
            self.came = lax.ppermute(value, axis, [(i, i ^ bit) for i in range(count)])

    def terms(self):
        return [self.value, self.came]


def spread(whole):
    return list(jnp.split(whole, BLOCKS, axis=0))


def reduce_plain(whole):
    return lax.psum(lax.psum_scatter(whole, "wide", scatter_dimension=0, tiled=True), "narrow")


def body(
    fast,
    tokens,
    out_grad,
    first_gain,
    first_shift,
    qkv_weight,
    query_bias,
    value_bias,
    proj_weight,
    proj_bias,
    second_gain,
    second_shift,
    expand_weight,
    expand_bias,
    shrink_weight,
    shrink_bias,
):
    clips, seq, width = tokens.shape
    rows = -(-seq // 16) * 16
    flat = clips * rows
    part = width // BLOCKS
    hidden = 4 * width
    tile = hidden // BLOCKS
    tiles = hidden // width
    group = width // 2
    pairs = HEADS // 2 * clips
    first_cols = width + 3 * group
    second_cols = 3 * group
    own = first_gain.shape[0]
    gather_plain = functools.partial(lax.all_gather, axis_name="wide", axis=0, tiled=True)

    def shape(*dims, dtype=bf16):
        return jax.ShapeDtypeStruct(dims, dtype)

    def vmem(*dims, dtype=bf16):
        return pltpu.VMEM(dims, dtype)

    if fast:
        me = lax.axis_index("wide")
        odd = me % 2
        relative = [
            jnp.where(odd == 1, b, a) for a, b in zip((7, 3, 5, 1, 6, 4, 2, 0), (7, 5, 3, 1, 6, 2, 4, 0))
        ]
        order = jnp.stack(relative) ^ me
        where = jnp.sum(
            jnp.where(order[None, :] == jnp.arange(BLOCKS)[:, None], jnp.arange(BLOCKS)[None, :], 0),
            axis=1,
        )
        line = lax.axis_index("narrow")
        idx = jnp.concatenate([order, where, jnp.stack([line % 2, line // 2])]).astype(jnp.int32)
    else:
        idx = jnp.concatenate([jnp.arange(BLOCKS), jnp.arange(BLOCKS)]).astype(jnp.int32)

    vectors = [
        first_gain,
        first_shift,
        query_bias,
        value_bias,
        proj_bias,
        second_gain,
        second_shift,
        shrink_bias,
    ]
    block = jnp.concatenate([jnp.stack(vectors), expand_bias.reshape(4, own)], axis=0)
    block = jnp.pad(block, ((0, SMALL - block.shape[0]), (0, 0)))
    packed, down_own, token = call(
        pack,
        "pack",
        [shape(own, 4 * width + SMALL), shape(*shrink_weight.shape)],
        [sems(3)],
        [Far(qkv_weight), Far(proj_weight), Far(shrink_weight), block],
    )
    pad = ((0, 0), (0, rows - seq), (0, 0))
    x = jnp.pad(tokens, pad).reshape(flat, width)
    og = jnp.pad(out_grad, pad).reshape(flat, width)
    ogt, token = call(turn_rows, "turn_rows", [shape(width, flat)], [], [og])

    after = []
    if fast:
        attn = Gather(packed)
        up = Gather(expand_weight)
        attn.forward([x, ogt, idx])
        attn_parts = attn.parts_early()
    else:
        up_parts = spread(gather_plain(expand_weight))
        down_parts = spread(gather_plain(shrink_weight))
        whole = gather_plain(packed)
        bias = whole[:, 4 * width + 8 : 4 * width + 12].reshape(width // own, own, 4)
        bias = bias.transpose(0, 2, 1).reshape(BLOCKS, 4, part).transpose(0, 2, 1).reshape(width, 4)
        attn_parts = spread(whole.at[:, 4 * width + 8 : 4 * width + 12].set(bias))

    def sibling(array):
        return cores(array) if fast else jnp.zeros_like(array)

    ogt_sibling = sibling(ogt)
    normed, token = call(norm_input, "norm_input", [shape(flat, width, dtype=f32)], [], [x])
    attended, n1, mixed, probs, small, up_shift, w_qkv, w_proj, token = call(
        functools.partial(attention_forward, clips, rows, seq),
        "attention_forward",
        (
            shape(flat, width),
            shape(flat, width),
            Far(shape(flat, 3 * width)),
            Far(shape(pairs, 2 * rows, rows)),
            shape(16, width, dtype=f32),
            shape(BLOCKS, 1, tile, dtype=f32),
            Far(shape(width, 3 * width)),
            shape(width, width),
        ),
        [vmem(width, 3 * width), vmem(width, SMALL), vmem(flat, 3 * width), vmem(pairs, 2 * rows, rows), sems(4 + HEADS // 2)],
        [idx, normed, *attn_parts],
    )
    if fast:
        up.forward([token])
        up.early()
    middle, n2, token = call(
        proj_forward,
        "proj_forward",
        (Far(shape(flat, width, dtype=f32)), shape(flat, width)),
        [vmem(flat, width, dtype=f32), sems(1)],
        [x, attended, small, w_proj],
    )
    if fast:
        up_parts = up.late([token])
        (down_own,) = tie([down_own], [token])
        down = Gather(down_own)
    turned_send, turned_keep, token = call(
        left_operands,
        "left_operands",
        [shape(3 * width // 2, flat)] * 2,
        [vmem(3, width, flat)],
        [idx, n1, attended, n2],
        [token],
    )
    turned_sibling = sibling(turned_send)

    two_tiles = shape(2, flat, width)
    expand_scratch = [vmem(2, flat, width, dtype=f32), vmem(2, flat, width), sems(6)]
    hidden_one, up_two, slope_one, hidden_one_far, up_far, token = call(
        expand_first,
        "expand_first",
        (two_tiles, shape(2, width, width), Far(two_tiles), Far(two_tiles), Far(shape(tiles, width, width))),
        [vmem(2, width, width)] + expand_scratch,
        [idx, n2, up_shift, *up_parts],
        [token],
    )
    hidden_sibling = sibling(hidden_one)
    if fast:
        down.forward([token])
    hidden_two, slope_two, hidden_two_far, token = call(
        expand_second,
        "expand_second",
        (two_tiles, Far(two_tiles), Far(two_tiles)),
        expand_scratch,
        [idx, n2, up_shift, up_two],
        [token],
    )

    def shrink_grad(own_hidden, sibling_hidden):
        return call(
            shrink_weight_grad,
            "shrink_weight_grad",
            [shape(width, tile)] * HALF,
            [],
            [ogt, ogt_sibling, own_hidden, sibling_hidden],
        )

    *down_blocks, token = shrink_grad(hidden_two, hidden_sibling)
    if fast:
        down_sum = Scatter(down_blocks)
        down_parts = down.parts([token])
    grad_pre, sums, down_far, token = call(
        hidden_back,
        "hidden_back",
        [shape(tiles, flat, width), shape(BLOCKS, 1, tile, dtype=f32), Far(shape(tiles, width, width))],
        [vmem(tiles, flat, width), sems(BLOCKS + 4)],
        [idx, og, Far(slope_one), Far(slope_two), *down_parts],
        [turned_sibling],
    )
    grad_pre_sibling = sibling(grad_pre)
    if fast:
        token = down_sum.pass_on([token])
    grad_middle, low, grad_att, sums_two, token = call(
        middle_back,
        "middle_back",
        (shape(flat, width, dtype=f32), shape(flat, width), shape(flat, width), shape(8, width, dtype=f32)),
        [vmem(tiles, width, width), vmem(flat, width, dtype=f32), sems(5)],
        [og, small, w_proj, Far(middle), Far(up_far), grad_pre],
        [token],
    )
    low_sibling = sibling(low)

    def expand_grad(left, left_sibling, after=()):
        return call(
            expand_weight_grad,
            "expand_weight_grad",
            [shape(part, hidden)] * HALF,
            [],
            [idx, left, left_sibling, grad_pre, grad_pre_sibling],
            after,
        )

    *up_blocks, token = expand_grad(turned_keep, turned_sibling, [token])
    if fast:
        up_sum = Scatter(up_blocks)
        down_fold = Halves(idx, 0)
        token = down_fold.one([down_sum.total()], [token])

    def heads(half, after):
        return call(
            functools.partial(heads_back, half, clips, rows),
            "heads_back",
            [shape(flat, 3 * group)],
            [vmem(flat, 3 * group), vmem(pairs // 2, 2 * rows, rows), sems(12)],
            [grad_att, Far(mixed), Far(probs)],
            after,
        )

    first_mixed, token = heads(0, [token, low_sibling])
    first_sibling = sibling(first_mixed)
    if fast:
        token = up_sum.pass_on([token])
        token = down_fold.two([token])
    second_mixed, token = heads(1, [token])
    second_sibling = sibling(second_mixed)
    if fast:
        token = down_fold.three([token])

    def attention_grad(left, left_sibling, after=()):
        return call(
            attention_weight_grad,
            "attention_weight_grad",
            [shape(part, first_cols)] * HALF,
            [],
            [left, left_sibling, low, low_sibling, first_mixed, first_sibling],
            after,
        )

    *first_blocks, token = attention_grad(turned_keep, turned_sibling, [token])

    def last_grad(left, left_sibling, after=()):
        return call(
            last_weight_grad,
            "last_weight_grad",
            [shape(part, second_cols)] * HALF,
            [],
            [left, left_sibling, second_mixed, second_sibling],
            after,
        )

    *second_blocks, token = last_grad(turned_keep, turned_sibling, [token])
    if fast:
        *attn_blocks, token = side_by_side([[[a], [b]] for a, b in zip(first_blocks, second_blocks)], [token])
        attn_sum = Scatter(attn_blocks)
        up_fold = Halves(idx, 1)
        token = up_fold.one([up_sum.total()], [token])
        token = down_fold.four([token])
    gn1, vectors, token = call(
        input_sums,
        "input_sums",
        (Far(shape(flat, width, dtype=f32)), shape(16, width, dtype=f32)),
        [vmem(2, width, 3 * group), vmem(flat, width, dtype=f32), sems(7)],
        [first_mixed, second_mixed, x, sums_two, sums, Far(w_qkv)],
        [token],
    )
    if fast:
        token = attn_sum.pass_on([token])
        token = up_fold.two([token])
        every = Everywhere(vectors)

    def shrink(start, hidden, base, out, after):
        return call(
            functools.partial(shrink_forward, start, clips, rows, seq),
            "shrink_forward",
            [out],
            [vmem(2, flat, width), vmem(flat, width, dtype=f32), vmem(2, width, width), sems(5)],
            [small, Far(hidden), Far(base), Far(down_far)],
            after,
        )

    partial_out, token = shrink(0, hidden_one_far, middle, shape(flat, width, dtype=f32), [token])
    if fast:
        vectors, token = combine([every.terms()], [token])
        every.send(vectors)
        token = up_fold.three([token])
        fold = Halves(idx, 1)
        token = fold.one([attn_sum.total()], [token])
    block_out, token = shrink(2, hidden_two_far, partial_out, shape(seq, clips, width), [token])
    if fast:
        token = fold.two([token])
        token = up_fold.four([token])
        vectors, token = combine([every.terms()], [token])
        every.send(vectors)
        grad_down, sums_down, token = call(
            finish_down,
            "finish_down",
            [shape(tile, width, dtype=f32), TOKEN],
            [vmem(width, tile, dtype=f32)],
            [idx, down_fold.keep, down_fold.came],
            [token],
        )
    tokens_grad, token = call(
        functools.partial(input_back, clips, rows, seq),
        "input_back",
        [shape(seq, clips, width, dtype=f32)],
        [],
        [gn1, grad_middle, x, small],
        [token],
    )

    if fast:
        token = fold.three([token])
        vectors, token = combine([every.terms()], [token])
        every.send(vectors)
        grad_up, sums_up, token = call(
            finish_up,
            "finish_up",
            [shape(part, hidden, dtype=f32), TOKEN],
            [],
            [idx, up_fold.keep, up_fold.came],
            [token],
        )
        vectors, token = combine([every.terms()], [token])
        every.send(vectors)
        token = fold.four([token])
        squares, token = call(square_sums, "combine", [TOKEN], [], [fold.keep, sums_down, sums_up], [token])
        hops = (("narrow", 4, (1,)), ("wide", BLOCKS, (1,)), ("wide", BLOCKS, (2, 4, 6)))
        for n, (axis, count, bits) in enumerate(hops):
            came = [lax.ppermute(squares, axis, [(i, i ^ b) for i in range(count)]) for b in bits]
            squares, token = call(add_pairs, "combine", [TOKEN], [], [squares, *came], [token])
            if n == 0:
                vectors, token = combine([every.terms()], [token])
        squares, token = call(add_vectors, "combine", [TOKEN], [], [squares, vectors], [token])
        grad_sq_norm = squares[0, 0]
        index = me * own
    else:
        none = jnp.zeros_like(turned_send)
        halves = (
            (shrink_grad(hidden_one, hidden_sibling)[:-1], down_blocks),
            (expand_grad(turned_send, none)[:-1], up_blocks),
            (attention_grad(turned_send, none)[:-1], first_blocks),
            (last_grad(turned_send, none)[:-1], second_blocks),
        )
        whole_down = jnp.concatenate([b.T for half in halves[0] for b in half], axis=0)
        grad_down = reduce_plain(whole_down).astype(f32)
        grad_up, grad_first, grad_second = (
            reduce_plain(jnp.concatenate([b for half in pair for b in half], axis=0)).astype(f32)
            for pair in halves[1:]
        )
        vectors = lax.psum(vectors, ("wide", "narrow"))
        index = lax.axis_index("wide") * own
    up_bias = vectors[8:12].reshape(4, BLOCKS, part).transpose(1, 0, 2).reshape(-1)
    up_bias = lax.dynamic_slice(up_bias, (4 * index,), (4 * own,))
    small_grads = lax.dynamic_slice(vectors[:8], (0, index), (8, own))
    if fast:
        grad_qkv, grad_proj, token = call(
            finish_attention,
            "finish_attention",
            [shape(part, 3 * width, dtype=f32), shape(part, width, dtype=f32)],
            [vmem(part, hidden, dtype=f32)],
            [idx, fold.keep, fold.came],
        )
    else:
        grad_proj = grad_first[:, :width]
        grad_qkv = jnp.concatenate(
            [
                g[:, at + k * group : at + (k + 1) * group]
                for k in range(3)
                for g, at in ((grad_first, width), (grad_second, 0))
            ],
            axis=1,
        )
        local = sum(jnp.sum(g * g) for g in (small_grads, up_bias, grad_down, grad_up, grad_first, grad_second))
        grad_sq_norm = lax.psum(local, "wide")
    return (
        block_out.transpose(1, 0, 2),
        tokens_grad.transpose(1, 0, 2),
        small_grads[0],
        small_grads[1],
        grad_qkv,
        small_grads[2],
        small_grads[3],
        grad_proj,
        small_grads[4],
        small_grads[5],
        small_grads[6],
        grad_up,
        up_bias,
        grad_down,
        small_grads[7],
        grad_sq_norm,
    )


def solution(mesh):
    fast = mesh.shape["wide"] == BLOCKS and mesh.shape["narrow"] == 4
    clips = P(("wide", "narrow"), None, None)
    vector = P("wide")
    matrix = P("wide", None)
    return jax.shard_map(
        functools.partial(body, fast),
        mesh=mesh,
        in_specs=(
            clips,
            clips,
            vector,
            vector,
            matrix,
            vector,
            vector,
            matrix,
            vector,
            vector,
            vector,
            matrix,
            vector,
            matrix,
            vector,
        ),
        out_specs=(
            clips,
            clips,
            vector,
            vector,
            matrix,
            vector,
            vector,
            matrix,
            vector,
            vector,
            vector,
            matrix,
            vector,
            matrix,
            vector,
            P(),
        ),
        check_vma=False,
    )
```

```python
import functools

import jax
import jax.numpy as jnp
from jax import lax
from jax.experimental import pallas as pl
from jax.experimental.pallas import tpu as pltpu
from jax.sharding import PartitionSpec as P

HEADS = 12
EPS = 1e-06
BLOCKS = 8
HALF = BLOCKS // 2
SMALL = 128
MIB = 1024 * 1024

f32 = jnp.float32
bf16 = jnp.bfloat16

ANY = pl.BlockSpec(memory_space=pl.ANY)
HBM = pl.BlockSpec(memory_space=pltpu.HBM)
FULL = pl.BlockSpec(memory_space=pltpu.VMEM)
SCALAR = pl.BlockSpec(memory_space=pltpu.SMEM)


def nn(a, b):
    return lax.dot_general(a, b, (((1,), (0,)), ((), ())), preferred_element_type=f32)


def nt(a, b):
    return lax.dot_general(a, b, (((1,), (1,)), ((), ())), preferred_element_type=f32)


def tn(a, b):
    return lax.dot_general(a, b, (((0,), (0,)), ((), ())), preferred_element_type=f32)


def normalise(values):
    mean_row = jnp.mean(values, axis=-1, keepdims=True)
    centered = values - mean_row
    spread = jnp.mean(centered * centered, axis=-1, keepdims=True)
    inverse = lax.rsqrt(spread + EPS)
    return centered * inverse, inverse


def norm_back(grad, normed, inverse):
    first = jnp.mean(grad, axis=-1, keepdims=True)
    second = jnp.mean(grad * normed, axis=-1, keepdims=True)
    return inverse * (grad - first - normed * second)


def gelu_both(values):
    cdf = 0.5 * (1.0 + lax.erf(values * (0.5**0.5)))
    density = 0.3989422804014327 * jnp.exp(-0.5 * values * values)
    return values * cdf, cdf + values * density


def sems(count):
    return pltpu.SemaphoreType.DMA((count,))


def start_all(pairs, sem, first=0):
    copies = [pltpu.make_async_copy(a, b, sem.at[first + k]) for k, (a, b) in enumerate(pairs)]
    for copy in copies:
        copy.start()
    return copies


def wait_all(copies):
    for copy in copies:
        copy.wait()


def rows_in_order(idx, pieces, target, columns=None):
    for i, piece in enumerate(pieces):
        count = piece.shape[0]
        rows = pl.ds(pl.multiple_of(idx[i] * count, 16), count)
        for source, to, size in columns or [(0, 0, piece.shape[1])]:
            target[rows, to : to + size] = piece[:, source : source + size]


def columns_by_place(idx, pieces, target, tile, places):
    for i, piece in enumerate(pieces):
        count = piece.shape[0]
        rows = pl.ds(pl.multiple_of(idx[i] * count, 16), count)
        for k, place in enumerate(places):
            source = pl.ds(pl.multiple_of(idx[place] * tile, 128), tile)
            target[rows, k * tile : (k + 1) * tile] = piece[:, source]


def rows_by_place(idx, target, value):
    part = value.shape[0] // BLOCKS
    for b in range(BLOCKS):
        to = pl.multiple_of(idx[BLOCKS + b] * part, 16)
        target[pl.ds(to, part)] = value[b * part : (b + 1) * part]


def beside(one, two):
    return jnp.concatenate([one[...], two[...]], axis=1)


def below(one, two):
    return jnp.concatenate([one[...], two[...]], axis=0)


def lanes_of(head_dim):
    return lax.broadcasted_iota(jnp.int32, (1, 2 * head_dim), 1) < head_dim


def stack_pair(pair, left):
    zero = jnp.zeros_like(pair)
    return jnp.concatenate([jnp.where(left, pair, zero), jnp.where(left, zero, pair)], axis=0)


def merge_pair(stacked, left):
    half = stacked.shape[0] // 2
    return jnp.where(left, stacked[:half], stacked[half:])


KERNELS = {
    "pack": (1, 8),
    "turn_rows": (1, 8),
    "norm_input": (0.01, 12),
    "attention_forward": (0.01, 28),
    "left_operands": (8, 16),
    "proj_forward": (0.01, 16),
    "expand_first": (0.01, 24),
    "expand_second": (25, 20),
    "shrink_weight_grad": (5, 16),
    "hidden_back": (14, 20),
    "middle_back": (45, 28),
    "expand_weight_grad": (14, 16),
    "heads_back": (20, 16),
    "attention_weight_grad": (20, 16),
    "last_weight_grad": (10, 12),
    "input_sums": (10, 20),
    "shrink_forward": (8, 16),
    "input_back": (8, 12),
    "combine": (0.5, 12),
    "cut_half": (0.5, 12),
    "join_halves": (0.5, 12),
    "finish_down": (1, 12),
    "finish_up": (1, 12),
    "finish_attention": (1, 12),
}
SCALE = 1.0


class Far:
    def __init__(self, array):
        self.array = array

    def operand(self):
        return pltpu.with_memory_space_constraint(self.array, pltpu.HBM)

    def result(self):
        return pltpu.HBM(self.array.shape, self.array.dtype)


TOKEN = jax.ShapeDtypeStruct((8, 128), f32)


def call(kernel, name, out_shape, scratch, inputs, after=()):
    given, skip, many = len(inputs), len(after), len(out_shape)
    specs = [HBM if isinstance(a, Far) else SCALAR if a.dtype == jnp.int32 else FULL for a in inputs]
    outs = [HBM if isinstance(o, Far) else FULL for o in out_shape] + [FULL]
    micros, mib = KERNELS[name]

    def run(*refs):
        token = refs[given + skip + many]
        token[...] = jnp.zeros(token.shape, f32)
        kernel(*refs[:given], *refs[given + skip : given + skip + many], *refs[given + skip + many + 1 :])

    return pl.pallas_call(
        run,
        out_shape=[o.result() if isinstance(o, Far) else o for o in out_shape] + [TOKEN],
        in_specs=specs + [FULL if a.shape == TOKEN.shape else ANY for a in after],
        out_specs=outs,
        scratch_shapes=scratch,
        compiler_params=pltpu.CompilerParams(vmem_limit_bytes=mib * MIB),
        cost_estimate=pl.CostEstimate(
            flops=int(micros * SCALE * 1e9), bytes_accessed=0, transcendentals=0
        ),
        name=name,
    )(*[a.operand() if isinstance(a, Far) else a for a in inputs], *after)


def combine(sums, after=()):
    arrays = [a for terms in sums for a in terms]

    def kernel(*refs):
        at = 0
        for terms, out in zip(sums, refs[len(arrays) :]):
            total = refs[at][...].astype(f32)
            for k in range(1, len(terms)):
                total = total + refs[at + k][...].astype(f32)
            out[...] = total.astype(out.dtype)
            at += len(terms)

    shapes = [jax.ShapeDtypeStruct(terms[0].shape, terms[0].dtype) for terms in sums]
    return call(kernel, "combine", shapes, [], arrays, after)


def side_by_side(sums, after=()):
    arrays = [a for some in sums for terms in some for a in terms]

    def kernel(*refs):
        refs = list(refs)
        outs = refs[len(arrays) :]
        for some, out in zip(sums, outs):
            at = 0
            for terms in some:
                values = [refs.pop(0)[...].astype(f32) for _ in terms]
                total = values[0]
                for value in values[1:]:
                    total = total + value
                out[:, at : at + total.shape[1]] = total.astype(out.dtype)
                at += total.shape[1]

    shapes = [
        jax.ShapeDtypeStruct((some[0][0].shape[0], sum(terms[0].shape[1] for terms in some)), bf16) for some in sums
    ]
    return call(kernel, "combine", shapes, [], arrays, after)


def tie(values, after):
    def nothing(*refs):
        pass

    n = len(values)
    return pl.pallas_call(
        nothing,
        out_shape=[jax.ShapeDtypeStruct(v.shape, v.dtype) for v in values],
        in_specs=[ANY] * n + [FULL if a.shape == TOKEN.shape else ANY for a in after],
        out_specs=[ANY] * n,
        input_output_aliases={i: i for i in range(n)},
        compiler_params=pltpu.CompilerParams(vmem_limit_bytes=MIB),
        name="tie",
    )(*values, *after)


def pack(qkv_ref, proj_ref, down_ref, vectors_ref, out_o, down_o, sem):
    cols, width = qkv_ref.shape[1], proj_ref.shape[1]
    pairs = [(qkv_ref, out_o.at[:, pl.ds(0, cols)]), (proj_ref, out_o.at[:, pl.ds(cols, width)])]
    here = start_all(pairs + [(down_ref, down_o)], sem)
    out_o[:, cols + width :] = vectors_ref[...].astype(f32).T.astype(bf16)
    wait_all(here)


def norm_input(x_ref, normed_o):
    normed_o[...] = normalise(x_ref[...].astype(f32))[0]


def turn_rows(source, out_o):
    out_o[...] = source[...].T


def attention_forward(clips, rows, seq, idx, normed, *refs):
    pieces = refs[:BLOCKS]
    attended, n1_o, mixed_o, probs_o, small_o, up_shift_o = refs[BLOCKS : BLOCKS + 6]
    weights_o, proj_o, weights, small_block, mixed, probs_all, sem = refs[BLOCKS + 6 :]
    width = normed.shape[1]
    pair = 2 * (width // HEADS)
    rows_in_order(idx, pieces, weights, [(0, 0, 3 * width)])
    rows_in_order(idx, pieces, small_block, [(4 * width, 0, SMALL)])
    rows_in_order(idx, pieces, proj_o, [(3 * width, 0, width)])
    gone = start_all([(weights, weights_o)], sem, 3)
    small = small_block[...].astype(f32).T
    small_o[...] = small[:16]
    up = [small[8 + k : 9 + k] for k in range(4)]
    part = width // BLOCKS
    for s in range(BLOCKS):
        up_shift_o[s] = jnp.concatenate([u[:, part * s : part * (s + 1)] for u in up], axis=1)
    n1 = (normed[...] * small[0:1] + small[1:2]).astype(bf16)
    for t in range(3):
        acc = nn(n1, weights[:, width * t : width * (t + 1)])
        if t == 0:
            acc = acc + small[2:3]
        if t == 2:
            acc = acc + small[3:4]
        mixed[:, width * t : width * (t + 1)] = acc.astype(bf16)
    gone += start_all([(mixed, mixed_o)], sem)
    n1_o[...] = n1
    left = lanes_of(width // HEADS)
    valid = lax.broadcasted_iota(jnp.int32, (1, rows), 1) < seq
    scale = (width // HEADS) ** (-0.5)

    def probs_copy(p):
        at = pl.ds(p * clips, clips)
        return pltpu.make_async_copy(probs_all.at[at], probs_o.at[at], sem.at[4 + p])

    def heads(p, carry):
        lane = pl.multiple_of(p * pair, pair)
        for c in range(clips):
            here = pl.ds(c * rows, rows)
            q = mixed[here, pl.ds(lane, pair)]
            k = mixed[here, pl.ds(lane + width, pair)]
            v = mixed[here, pl.ds(lane + 2 * width, pair)]
            scores = nt(stack_pair(q, left), k) * scale
            scores = jnp.where(valid, scores, -1e30)
            peak = jnp.max(scores, axis=-1, keepdims=True)
            raised = jnp.exp(scores - peak)
            total = jnp.sum(raised, axis=-1, keepdims=True)
            probs = (raised * (1.0 / total)).astype(bf16)
            probs_all[p * clips + c] = probs
            attended[here, pl.ds(lane, pair)] = merge_pair(nn(probs, v), left).astype(bf16)
        probs_copy(p).start()
        return carry

    lax.fori_loop(0, HEADS // 2, heads, 0, unroll=2)

    def gone_heads(p, carry):
        probs_copy(p).wait()
        return carry

    lax.fori_loop(0, HEADS // 2, gone_heads, 0)
    wait_all(gone)


def proj_forward(x_ref, attended, small, weights, middle_far, n2_o, middle, sem):
    value = x_ref[...].astype(f32) + (nn(attended[...], weights[...]) + small[4:5])
    middle[...] = value
    gone = start_all([(middle, middle_far)], sem)
    normed, inverse = normalise(value)
    n2_o[...] = (normed * small[5:6] + small[6:7]).astype(bf16)
    wait_all(gone)


def left_operands(idx, n1, attended, n2, send_o, keep_o, turned):
    width = n1.shape[1]
    half, part = width // 2, width // BLOCKS
    for k, source in enumerate((n1, attended, n2)):
        turned[k] = source[...].T
        for p in range(BLOCKS):
            to = k * half + p % HALF * part
            rows = pl.ds(pl.multiple_of(idx[p] * part, 16), part)
            (send_o if p < HALF else keep_o)[to : to + part] = turned[k, rows]


def expand_tiles(start, idx, n2_ref, shift_ref, weights, hidden_o, slope_far, hidden_far, pre, slope, sem):
    width = n2_ref.shape[1]
    step = 256
    gone = []

    def multiply(t, c):
        cols = slice(c * step, (c + 1) * step)
        pre[t, :, cols] = nn(n2_ref[...], weights[t, :, cols])

    for c in range(width // step):
        multiply(0, c)
    for t in range(2):
        shift = jnp.concatenate([shift_ref[idx[2 * (start + t) + k]] for k in range(2)], axis=1)
        for c in range(width // step):
            cols = slice(c * step, (c + 1) * step)
            if t == 0:
                multiply(1, c)
            act, derivative = gelu_both(pre[t, :, cols] + shift[:, cols])
            hidden_o[t, :, cols] = act.astype(bf16)
            slope[t, :, cols] = derivative.astype(bf16)
        gone += start_all([(hidden_o.at[t], hidden_far.at[t]), (slope.at[t], slope_far.at[t])], sem, 2 * t)
    return gone


def expand_first(idx, n2_ref, shift_ref, *refs):
    pieces = refs[:BLOCKS]
    hidden_o, two_o, slope_far, hidden_far, up_far, one, pre, slope, sem = refs[BLOCKS:]
    tile = n2_ref.shape[1] // 2
    for t in range(2):
        columns_by_place(idx, pieces, one.at[t], tile, (2 * t, 2 * t + 1))
    gone = start_all([(one, up_far.at[pl.ds(0, 2)])], sem, 4)
    gone += expand_tiles(0, idx, n2_ref, shift_ref, one, hidden_o, slope_far, hidden_far, pre, slope, sem)
    for t in range(2):
        columns_by_place(idx, pieces, two_o.at[t], tile, (2 * t + 4, 2 * t + 5))
    gone += start_all([(two_o, up_far.at[pl.ds(2, 2)])], sem, 5)
    wait_all(gone)


def expand_second(*refs):
    wait_all(expand_tiles(2, *refs))


def shrink_weight_grad(ogt, ogt_sibling, own, sibling, *outs):
    left = beside(ogt, ogt_sibling)
    for t in range(2):
        grad = nn(left, below(own.at[t], sibling.at[t])).astype(bf16)
        tile = grad.shape[1] // 2
        for k in range(2):
            outs[2 * t + k][...] = grad[:, k * tile : (k + 1) * tile]


def expand_weight_grad(idx, own_left, sibling_left, own, sibling, *outs):
    half = own_left.shape[0] // 3
    part = half // HALF
    at = pl.ds(2 * half, half)
    left = beside(own_left.at[at], sibling_left.at[at])
    for t in range(4):
        grad = nn(left, below(own.at[t], sibling.at[(t + 2) % 4])).astype(bf16)
        tile = grad.shape[1] // 2
        for k in range(2):
            to = pl.multiple_of(idx[2 * t + k] * tile, 128)
            for b in range(HALF):
                outs[b][:, pl.ds(to, tile)] = grad[b * part : (b + 1) * part, k * tile : (k + 1) * tile]


def rows_out(grad, outs, columns):
    part = grad.shape[0] // HALF
    for b in range(HALF):
        outs[b][:, columns] = grad[b * part : (b + 1) * part].astype(bf16)


def attention_weight_grad(own_left, sibling_left, own_low, sibling_low, own_mixed, sibling_mixed, *outs):
    width = own_low.shape[1]
    half = width // 2
    for k, right, columns in (
        (1, below(own_low, sibling_low), slice(0, width)),
        (0, below(own_mixed, sibling_mixed), slice(width, None)),
    ):
        at = pl.ds(k * half, half)
        rows_out(nn(beside(own_left.at[at], sibling_left.at[at]), right), outs, columns)


def last_weight_grad(own_left, sibling_left, own_mixed, sibling_mixed, *outs):
    at = pl.ds(0, own_left.shape[0] // 3)
    left = beside(own_left.at[at], sibling_left.at[at])
    rows_out(nn(left, below(own_mixed, sibling_mixed)), outs, slice(None))


def hidden_back(idx, og_ref, slope_one, slope_two, *refs):
    down_pieces, (grad_pre, sums_o, down_far, slope, sem) = refs[:BLOCKS], refs[BLOCKS:]
    tile = down_pieces[0].shape[0]
    here = [
        start_all([((slope_one if t < 2 else slope_two).at[t % 2], slope.at[t])], sem, BLOCKS + t)
        for t in range(4)
    ]
    pairs = [(piece, down_far.at[i // 2, pl.ds(i % 2 * tile, tile)]) for i, piece in enumerate(down_pieces)]
    gone = start_all(pairs, sem)
    for t in range(grad_pre.shape[0]):
        down = below(down_pieces[2 * t], down_pieces[2 * t + 1])
        grad_hidden = nt(og_ref[...], down)
        wait_all(here[t])
        gp = (grad_hidden * slope[t].astype(f32)).astype(bf16)
        grad_pre[t] = gp
        sums = jnp.sum(gp.astype(f32), axis=0, keepdims=True)
        for k in range(2):
            sums_o[idx[2 * t + k]] = sums[:, k * tile : (k + 1) * tile]
    wait_all(gone)


def middle_back(og_ref, small_ref, weights, middle_ref, up_ref, grad_pre, *refs):
    grad_middle_o, low_o, grad_att_o, vectors_o, up, middle, sem = refs

    def up_copy(t):
        return pltpu.make_async_copy(up_ref.at[t], up.at[t], sem.at[t])

    for t in range(4):
        up_copy(t).start()
    here = start_all([(middle_ref, middle)], sem, 4)
    grad_middle_o[...] = jnp.zeros(grad_middle_o.shape, f32)

    def step(t, carry):
        up_copy(t).wait()
        grad_middle_o[...] += nt(grad_pre[t], up[t])
        return carry

    lax.fori_loop(0, 4, step, 0)
    wait_all(here)
    gn2 = grad_middle_o[...]
    normed, inverse = normalise(middle[...])
    og = og_ref[...].astype(f32)
    value = og + norm_back(gn2 * small_ref[5:6], normed, inverse)
    grad_middle_o[...] = value
    low = value.astype(bf16)
    low_o[...] = low
    grad_att_o[...] = nt(low, weights[...]).astype(bf16)
    vectors_o[0:1] = jnp.sum(low.astype(f32), axis=0, keepdims=True)
    vectors_o[1:2] = jnp.sum(gn2 * normed, axis=0, keepdims=True)
    vectors_o[2:3] = jnp.sum(gn2, axis=0, keepdims=True)
    vectors_o[3:4] = jnp.sum(og, axis=0, keepdims=True)


def heads_back(half, clips, rows, grad_att, mixed_ref, probs_ref, grad_mixed_o, mixed, probs_all, sem):
    width = grad_att.shape[1]
    group = width // 2
    head_dim = width // HEADS
    pair = 2 * head_dim
    count = group // pair
    left = lanes_of(head_dim)
    scale = head_dim ** (-0.5)
    arrived = []
    for p in range(count):
        at = half * group + p * pair
        pairs = [
            (mixed_ref.at[:, pl.ds(k * width + at, pair)], mixed.at[:, pl.ds(k * group + p * pair, pair)])
            for k in range(3)
        ]
        source = pl.ds((half * count + p) * clips, clips)
        pairs.append((probs_ref.at[source], probs_all.at[pl.ds(p * clips, clips)]))
        arrived.append(start_all(pairs, sem, 4 * p))
    for p in range(count):
        wait_all(arrived[p])
        lanes = slice(p * pair, (p + 1) * pair)
        for c in range(clips):
            here = pl.ds(c * rows, rows)
            q, k, v = (mixed[here, t * group + p * pair : t * group + (p + 1) * pair] for t in range(3))
            low_probs = probs_all[p * clips + c]
            probs = low_probs.astype(f32)
            at = half * group + p * pair
            grad = stack_pair(grad_att[here, at : at + pair], left)
            grad_probs = nt(grad, v)
            inner = jnp.sum(probs * grad_probs, axis=-1, keepdims=True)
            grad_scores = (probs * (grad_probs - inner)).astype(bf16)
            gq = merge_pair(nn(grad_scores, k), left) * scale
            gk = tn(grad_scores, stack_pair(q, left)) * scale
            gv = tn(low_probs, grad)
            for t, value in enumerate((gq, gk, gv)):
                grad_mixed_o[here, t * group + p * pair : t * group + (p + 1) * pair] = value.astype(bf16)


def input_sums(first, second, x_ref, vectors_ref, sums_ref, weights_ref, gn1_o, vectors_o, weights, gn1_all, sem):
    width = x_ref.shape[1]
    group = width // 2
    part = width // BLOCKS
    here = []
    for g in range(2):
        pairs = []
        for k in range(3):
            source = weights_ref.at[:, pl.ds(k * width + g * group, group)]
            pairs.append((source, weights.at[g, :, pl.ds(k * group, group)]))
        here.append(start_all(pairs, sem, 1 + 3 * g))
    normed, inverse = normalise(x_ref[...].astype(f32))

    def sum_of(ref, k):
        return jnp.sum(ref[:, k * group : (k + 1) * group].astype(f32), axis=0, keepdims=True)

    vectors_o[2:3] = jnp.concatenate([sum_of(first, 0), sum_of(second, 0)], axis=1)
    vectors_o[3:4] = jnp.concatenate([sum_of(first, 2), sum_of(second, 2)], axis=1)
    vectors_o[4:8] = vectors_ref[0:4]
    for k in range(4):
        vectors_o[8 + k : 9 + k] = jnp.concatenate(
            [sums_ref[s][:, part * k : part * (k + 1)] for s in range(BLOCKS)], axis=1
        )
    vectors_o[12:] = jnp.zeros((4, width), f32)
    gn1 = None
    for g, grad in enumerate((first, second)):
        wait_all(here[g])
        more = nt(grad[...], weights[g])
        gn1 = more if gn1 is None else gn1 + more
    gn1_all[...] = gn1
    gone = start_all([(gn1_all, gn1_o)], sem)
    vectors_o[0:1] = jnp.sum(gn1 * normed, axis=0, keepdims=True)
    vectors_o[1:2] = jnp.sum(gn1, axis=0, keepdims=True)
    wait_all(gone)


def shrink_forward(start, clips, rows, seq, small_ref, hidden_ref, base_ref, down_ref, out_o, hidden, base, down, sem):
    here = []
    for t in range(2):
        here.append(start_all([(down_ref.at[start + t], down.at[t]), (hidden_ref.at[t], hidden.at[t])], sem, 2 * t))
    base_here = [] if start else start_all([(base_ref, base)], sem, 4)
    total = None
    for t in range(2):
        wait_all(here[t])
        more = nn(hidden[t], down[t])
        total = more if total is None else total + more
    wait_all(base_here)
    total = total + (base_ref if start else base)[...]
    if start == 0:
        out_o[...] = total + small_ref[7:8]
    else:
        for c in range(clips):
            out_o[:, c, :] = total[c * rows : c * rows + seq].astype(bf16)


def input_back(clips, rows, seq, gn1_ref, middle_ref, x_ref, small_ref, out_o):
    normed, inverse = normalise(x_ref[...].astype(f32))
    grad = middle_ref[...] + norm_back(gn1_ref[...] * small_ref[0:1], normed, inverse)
    for c in range(clips):
        out_o[:, c, :] = grad[c * rows : c * rows + seq]


def half_of(ref, axis, place):
    size = ref.shape[axis] // 2
    at = pl.ds(pl.multiple_of(place * size, 128), size)
    return ref.at[at] if axis == 0 else ref.at[:, at]


def cut_half(axis, bit, counts, idx, *refs):
    terms, (send_o, keep_o, whole) = list(refs[:-3]), refs[-3:]
    at = 0
    for count in counts:
        some = [terms.pop(0) for _ in range(count)]
        total = some[0][...].astype(f32)
        for term in some[1:]:
            total = total + term[...].astype(f32)
        size = total.shape[axis]
        (whole.at[at : at + size] if axis == 0 else whole.at[:, at : at + size])[...] = total.astype(bf16)
        at += size
    send_o[...] = half_of(whole, axis, 1 - idx[bit])[...]
    keep_o[...] = half_of(whole, axis, idx[bit])[...]


def join_halves(axis, bit, idx, own, other, out_o):
    half_of(out_o, axis, idx[bit])[...] = own[...].astype(out_o.dtype)
    half_of(out_o, axis, 1 - idx[bit])[...] = other[...].astype(out_o.dtype)


def squares_of(ref, sums_o):
    sums_o[...] = jnp.broadcast_to(jnp.sum(ref[...] * ref[...]), sums_o.shape)


def finish_down(idx, own, other, out_o, sums_o, whole):
    join_halves(0, 2 * BLOCKS, idx, own, other, whole)
    out_o[...] = whole[...].T
    squares_of(whole, sums_o)


def finish_up(idx, own, other, out_o, sums_o):
    join_halves(1, 2 * BLOCKS, idx, own, other, out_o)
    squares_of(out_o, sums_o)


def finish_attention(idx, own, other, qkv_o, proj_o, whole):
    join_halves(1, 2 * BLOCKS, idx, own, other, whole)
    width = proj_o.shape[1]
    group = width // 2
    proj_o[...] = whole[:, :width]
    for k in range(3):
        for g in range(2):
            at = width + (3 * g + k) * group
            to = k * width + g * group
            qkv_o[:, to : to + group] = whole[:, at : at + group]


def square_sums(half, one, two, out_o):
    value = half[...].astype(f32)
    out_o[...] = jnp.sum(value * value) + 0.5 * (one[...] + two[...])


def add_pairs(*refs):
    values, out_o = [r[...] for r in refs[:-1]], refs[-1]
    total = values[0] + values[1]
    out_o[...] = total if len(values) == 2 else total + (values[2] + values[3])


def add_vectors(total, vectors, out_o):
    out_o[...] = total[...] + jnp.sum(vectors[...] * vectors[...])


def cores(values):
    return lax.ppermute(values, "wide", [(i, i ^ 1) for i in range(BLOCKS)])


def near(values):
    return lax.ppermute(values, "wide", [(i, i ^ (4 if i & 1 else 2)) for i in range(BLOCKS)])


def across(values):
    return lax.ppermute(values, "wide", [(i, i ^ 6) for i in range(BLOCKS)])


def cross(values):
    return lax.ppermute(values, "wide", [(i, i ^ (2 if i & 1 else 4)) for i in range(BLOCKS)])


class Scatter:
    def __init__(self, blocks):
        self.far, self.other, self.first, self.own = blocks
        self.came_far = cross(self.far)

    def pass_on(self, after):
        first, token = combine([[self.first, self.came_far]], after)
        (other,) = tie([self.other], [token])
        self.came_first, self.came_other = near(first), cross(other)
        return token

    def total(self):
        return [self.own, self.came_other, self.came_first]


class Halves:
    def __init__(self, idx, axis):
        self.idx, self.axis, self.steps = idx, axis, 0

    def send(self, values, bit):
        self.came = lax.ppermute(values, "narrow", [(i, i ^ bit) for i in range(4)])

    def cut(self, sums, bit, after):
        whole = list(sums[0][0].shape)
        whole[self.axis] = sum(terms[0].shape[self.axis] for terms in sums)
        shape = list(whole)
        shape[self.axis] //= 2
        out = jax.ShapeDtypeStruct(tuple(shape), bf16)
        send, self.keep, token = call(
            functools.partial(cut_half, self.axis, 2 * BLOCKS + bit - 1, [len(terms) for terms in sums]),
            "cut_half",
            [out, out],
            [pltpu.VMEM(tuple(whole), bf16)],
            [self.idx, *(term for terms in sums for term in terms)],
            after,
        )
        self.send(send, bit)
        return token

    def one(self, sums, after):
        return self.cut(sums, 1, after)

    def two(self, after):
        return self.cut([[self.keep, self.came]], 2, after)

    def three(self, after):
        self.keep, token = combine([[self.keep, self.came]], after)
        self.send(self.keep, 2)
        return token

    def four(self, after):
        shape = list(self.keep.shape)
        shape[self.axis] *= 2
        self.keep, token = call(
            functools.partial(join_halves, self.axis, 2 * BLOCKS + 1),
            "join_halves",
            [jax.ShapeDtypeStruct(tuple(shape), bf16)],
            [],
            [self.idx, self.keep, self.came],
            after,
        )
        self.send(self.keep, 1)
        return token


class Gather:
    def __init__(self, own):
        self.own, self.first, self.other = own, near(own), cross(own)

    def direct(self):
        self.far = across(self.own)

    def forward(self, after):
        self.first, self.other = tie([self.first, self.other], after)
        self.far = cross(self.first)

    def parts(self, after=()):
        mine = [self.far, self.other, self.first]
        if after:
            mine = list(tie(mine, after))
        mine.append(self.own)
        return [cores(m) for m in mine] + mine

    def early(self):
        self.ahead = [cores(m) for m in (self.other, self.first, self.own)]

    def late(self, after):
        (far,) = tie([self.far], self.ahead + after)
        return [cores(far)] + self.ahead + [far, self.other, self.first, self.own]

    def parts_early(self):
        early = [cores(m) for m in (self.other, self.first, self.own)]
        (far,) = tie([self.far], early)
        return [cores(far)] + early + [far, self.other, self.first, self.own]


class Everywhere:
    def __init__(self, value):
        self.hops = [("wide", b, BLOCKS) for b in (1, 2, 4)] + [("narrow", b, 4) for b in (1, 2)]
        self.send(value)

    def send(self, value):
        self.value = value
        if self.hops:
            axis, bit, count = self.hops.pop(0)
            self.came = lax.ppermute(value, axis, [(i, i ^ bit) for i in range(count)])

    def terms(self):
        return [self.value, self.came]


def spread(whole):
    return list(jnp.split(whole, BLOCKS, axis=0))


def reduce_plain(whole):
    return lax.psum(lax.psum_scatter(whole, "wide", scatter_dimension=0, tiled=True), "narrow")


def body(
    fast,
    tokens,
    out_grad,
    first_gain,
    first_shift,
    qkv_weight,
    query_bias,
    value_bias,
    proj_weight,
    proj_bias,
    second_gain,
    second_shift,
    expand_weight,
    expand_bias,
    shrink_weight,
    shrink_bias,
):
    clips, seq, width = tokens.shape
    rows = -(-seq // 16) * 16
    flat = clips * rows
    part = width // BLOCKS
    hidden = 4 * width
    tile = hidden // BLOCKS
    tiles = hidden // width
    group = width // 2
    pairs = HEADS // 2 * clips
    first_cols = width + 3 * group
    second_cols = 3 * group
    own = first_gain.shape[0]
    gather_plain = functools.partial(lax.all_gather, axis_name="wide", axis=0, tiled=True)

    def shape(*dims, dtype=bf16):
        return jax.ShapeDtypeStruct(dims, dtype)

    def vmem(*dims, dtype=bf16):
        return pltpu.VMEM(dims, dtype)

    if fast:
        me = lax.axis_index("wide")
        odd = me % 2
        relative = [
            jnp.where(odd == 1, b, a) for a, b in zip((7, 3, 5, 1, 6, 4, 2, 0), (7, 5, 3, 1, 6, 2, 4, 0))
        ]
        order = jnp.stack(relative) ^ me
        where = jnp.sum(
            jnp.where(order[None, :] == jnp.arange(BLOCKS)[:, None], jnp.arange(BLOCKS)[None, :], 0),
            axis=1,
        )
        line = lax.axis_index("narrow")
        idx = jnp.concatenate([order, where, jnp.stack([line % 2, line // 2])]).astype(jnp.int32)
    else:
        idx = jnp.concatenate([jnp.arange(BLOCKS), jnp.arange(BLOCKS)]).astype(jnp.int32)

    vectors = [
        first_gain,
        first_shift,
        query_bias,
        value_bias,
        proj_bias,
        second_gain,
        second_shift,
        shrink_bias,
    ]
    block = jnp.concatenate([jnp.stack(vectors), expand_bias.reshape(4, own)], axis=0)
    block = jnp.pad(block, ((0, SMALL - block.shape[0]), (0, 0)))
    packed, down_own, token = call(
        pack,
        "pack",
        [shape(own, 4 * width + SMALL), shape(*shrink_weight.shape)],
        [sems(3)],
        [Far(qkv_weight), Far(proj_weight), Far(shrink_weight), block],
    )
    pad = ((0, 0), (0, rows - seq), (0, 0))
    x = jnp.pad(tokens, pad).reshape(flat, width)
    og = jnp.pad(out_grad, pad).reshape(flat, width)
    ogt, token = call(turn_rows, "turn_rows", [shape(width, flat)], [], [og])

    after = []
    if fast:
        attn = Gather(packed)
        up = Gather(expand_weight)
        attn.forward([x, ogt, idx])
        attn_parts = attn.parts_early()
    else:
        up_parts = spread(gather_plain(expand_weight))
        down_parts = spread(gather_plain(shrink_weight))
        whole = gather_plain(packed)
        bias = whole[:, 4 * width + 8 : 4 * width + 12].reshape(width // own, own, 4)
        bias = bias.transpose(0, 2, 1).reshape(BLOCKS, 4, part).transpose(0, 2, 1).reshape(width, 4)
        attn_parts = spread(whole.at[:, 4 * width + 8 : 4 * width + 12].set(bias))

    def sibling(array):
        return cores(array) if fast else jnp.zeros_like(array)

    ogt_sibling = sibling(ogt)
    normed, token = call(norm_input, "norm_input", [shape(flat, width, dtype=f32)], [], [x])
    attended, n1, mixed, probs, small, up_shift, w_qkv, w_proj, token = call(
        functools.partial(attention_forward, clips, rows, seq),
        "attention_forward",
        (
            shape(flat, width),
            shape(flat, width),
            Far(shape(flat, 3 * width)),
            Far(shape(pairs, 2 * rows, rows)),
            shape(16, width, dtype=f32),
            shape(BLOCKS, 1, tile, dtype=f32),
            Far(shape(width, 3 * width)),
            shape(width, width),
        ),
        [vmem(width, 3 * width), vmem(width, SMALL), vmem(flat, 3 * width), vmem(pairs, 2 * rows, rows), sems(4 + HEADS // 2)],
        [idx, normed, *attn_parts],
    )
    if fast:
        up.forward([token])
        up.early()
    middle, n2, token = call(
        proj_forward,
        "proj_forward",
        (Far(shape(flat, width, dtype=f32)), shape(flat, width)),
        [vmem(flat, width, dtype=f32), sems(1)],
        [x, attended, small, w_proj],
    )
    if fast:
        up_parts = up.late([token])
        (down_own,) = tie([down_own], [token])
        down = Gather(down_own)
    turned_send, turned_keep, token = call(
        left_operands,
        "left_operands",
        [shape(3 * width // 2, flat)] * 2,
        [vmem(3, width, flat)],
        [idx, n1, attended, n2],
        [token],
    )
    turned_sibling = sibling(turned_send)

    two_tiles = shape(2, flat, width)
    expand_scratch = [vmem(2, flat, width, dtype=f32), vmem(2, flat, width), sems(6)]
    hidden_one, up_two, slope_one, hidden_one_far, up_far, token = call(
        expand_first,
        "expand_first",
        (two_tiles, shape(2, width, width), Far(two_tiles), Far(two_tiles), Far(shape(tiles, width, width))),
        [vmem(2, width, width)] + expand_scratch,
        [idx, n2, up_shift, *up_parts],
        [token],
    )
    hidden_sibling = sibling(hidden_one)
    if fast:
        down.forward([token])
    hidden_two, slope_two, hidden_two_far, token = call(
        expand_second,
        "expand_second",
        (two_tiles, Far(two_tiles), Far(two_tiles)),
        expand_scratch,
        [idx, n2, up_shift, up_two],
        [token],
    )

    def shrink_grad(own_hidden, sibling_hidden):
        return call(
            shrink_weight_grad,
            "shrink_weight_grad",
            [shape(width, tile)] * HALF,
            [],
            [ogt, ogt_sibling, own_hidden, sibling_hidden],
        )

    *down_blocks, token = shrink_grad(hidden_two, hidden_sibling)
    if fast:
        down_sum = Scatter(down_blocks)
        down_parts = down.parts([token])
    grad_pre, sums, down_far, token = call(
        hidden_back,
        "hidden_back",
        [shape(tiles, flat, width), shape(BLOCKS, 1, tile, dtype=f32), Far(shape(tiles, width, width))],
        [vmem(tiles, flat, width), sems(BLOCKS + 4)],
        [idx, og, Far(slope_one), Far(slope_two), *down_parts],
        [turned_sibling],
    )
    grad_pre_sibling = sibling(grad_pre)
    if fast:
        token = down_sum.pass_on([token])
    grad_middle, low, grad_att, sums_two, token = call(
        middle_back,
        "middle_back",
        (shape(flat, width, dtype=f32), shape(flat, width), shape(flat, width), shape(8, width, dtype=f32)),
        [vmem(tiles, width, width), vmem(flat, width, dtype=f32), sems(5)],
        [og, small, w_proj, Far(middle), Far(up_far), grad_pre],
        [token],
    )
    low_sibling = sibling(low)

    def expand_grad(left, left_sibling, after=()):
        return call(
            expand_weight_grad,
            "expand_weight_grad",
            [shape(part, hidden)] * HALF,
            [],
            [idx, left, left_sibling, grad_pre, grad_pre_sibling],
            after,
        )

    *up_blocks, token = expand_grad(turned_keep, turned_sibling, [token])
    if fast:
        up_sum = Scatter(up_blocks)
        down_fold = Halves(idx, 0)
        token = down_fold.one([down_sum.total()], [token])

    def heads(half, after):
        return call(
            functools.partial(heads_back, half, clips, rows),
            "heads_back",
            [shape(flat, 3 * group)],
            [vmem(flat, 3 * group), vmem(pairs // 2, 2 * rows, rows), sems(12)],
            [grad_att, Far(mixed), Far(probs)],
            after,
        )

    first_mixed, token = heads(0, [token, low_sibling])
    first_sibling = sibling(first_mixed)
    if fast:
        token = up_sum.pass_on([token])
        token = down_fold.two([token])
    second_mixed, token = heads(1, [token])
    second_sibling = sibling(second_mixed)
    if fast:
        token = down_fold.three([token])

    def attention_grad(left, left_sibling, after=()):
        return call(
            attention_weight_grad,
            "attention_weight_grad",
            [shape(part, first_cols)] * HALF,
            [],
            [left, left_sibling, low, low_sibling, first_mixed, first_sibling],
            after,
        )

    *first_blocks, token = attention_grad(turned_keep, turned_sibling, [token])

    def last_grad(left, left_sibling, after=()):
        return call(
            last_weight_grad,
            "last_weight_grad",
            [shape(part, second_cols)] * HALF,
            [],
            [left, left_sibling, second_mixed, second_sibling],
            after,
        )

    *second_blocks, token = last_grad(turned_keep, turned_sibling, [token])
    if fast:
        *attn_blocks, token = side_by_side([[[a], [b]] for a, b in zip(first_blocks, second_blocks)], [token])
        attn_sum = Scatter(attn_blocks)
        up_fold = Halves(idx, 1)
        token = up_fold.one([up_sum.total()], [token])
        token = down_fold.four([token])
    gn1, vectors, token = call(
        input_sums,
        "input_sums",
        (Far(shape(flat, width, dtype=f32)), shape(16, width, dtype=f32)),
        [vmem(2, width, 3 * group), vmem(flat, width, dtype=f32), sems(7)],
        [first_mixed, second_mixed, x, sums_two, sums, Far(w_qkv)],
        [token],
    )
    if fast:
        token = attn_sum.pass_on([token])
        token = up_fold.two([token])
        every = Everywhere(vectors)

    def shrink(start, hidden, base, out, after):
        return call(
            functools.partial(shrink_forward, start, clips, rows, seq),
            "shrink_forward",
            [out],
            [vmem(2, flat, width), vmem(flat, width, dtype=f32), vmem(2, width, width), sems(5)],
            [small, Far(hidden), base if start else Far(base), Far(down_far)],
            after,
        )

    partial_out, token = shrink(0, hidden_one_far, middle, shape(flat, width, dtype=f32), [token])
    if fast:
        vectors, token = combine([every.terms()], [token])
        every.send(vectors)
        token = up_fold.three([token])
        fold = Halves(idx, 1)
        token = fold.one([attn_sum.total()], [token])
    block_out, token = shrink(2, hidden_two_far, partial_out, shape(seq, clips, width), [token])
    if fast:
        token = fold.two([token])
        token = up_fold.four([token])
        vectors, token = combine([every.terms()], [token])
        every.send(vectors)
        grad_down, sums_down, token = call(
            finish_down,
            "finish_down",
            [shape(tile, width, dtype=f32), TOKEN],
            [vmem(width, tile, dtype=f32)],
            [idx, down_fold.keep, down_fold.came],
            [token],
        )
    tokens_grad, token = call(
        functools.partial(input_back, clips, rows, seq),
        "input_back",
        [shape(seq, clips, width, dtype=f32)],
        [],
        [gn1, grad_middle, x, small],
        [token],
    )

    if fast:
        token = fold.three([token])
        vectors, token = combine([every.terms()], [token])
        every.send(vectors)
        grad_up, sums_up, token = call(
            finish_up,
            "finish_up",
            [shape(part, hidden, dtype=f32), TOKEN],
            [],
            [idx, up_fold.keep, up_fold.came],
            [token],
        )
        vectors, token = combine([every.terms()], [token])
        every.send(vectors)
        token = fold.four([token])
        squares, token = call(square_sums, "combine", [TOKEN], [], [fold.keep, sums_down, sums_up], [token])
        hops = (("narrow", 4, (1,)), ("wide", BLOCKS, (1,)), ("wide", BLOCKS, (2, 4, 6)))
        for n, (axis, count, bits) in enumerate(hops):
            came = [lax.ppermute(squares, axis, [(i, i ^ b) for i in range(count)]) for b in bits]
            squares, token = call(add_pairs, "combine", [TOKEN], [], [squares, *came], [token])
            if n == 0:
                vectors, token = combine([every.terms()], [token])
        squares, token = call(add_vectors, "combine", [TOKEN], [], [squares, vectors], [token])
        grad_sq_norm = squares[0, 0]
        index = me * own
    else:
        none = jnp.zeros_like(turned_send)
        halves = (
            (shrink_grad(hidden_one, hidden_sibling)[:-1], down_blocks),
            (expand_grad(turned_send, none)[:-1], up_blocks),
            (attention_grad(turned_send, none)[:-1], first_blocks),
            (last_grad(turned_send, none)[:-1], second_blocks),
        )
        whole_down = jnp.concatenate([b.T for half in halves[0] for b in half], axis=0)
        grad_down = reduce_plain(whole_down).astype(f32)
        grad_up, grad_first, grad_second = (
            reduce_plain(jnp.concatenate([b for half in pair for b in half], axis=0)).astype(f32)
            for pair in halves[1:]
        )
        vectors = lax.psum(vectors, ("wide", "narrow"))
        index = lax.axis_index("wide") * own
    up_bias = vectors[8:12].reshape(4, BLOCKS, part).transpose(1, 0, 2).reshape(-1)
    up_bias = lax.dynamic_slice(up_bias, (4 * index,), (4 * own,))
    small_grads = lax.dynamic_slice(vectors[:8], (0, index), (8, own))
    if fast:
        grad_qkv, grad_proj, token = call(
            finish_attention,
            "finish_attention",
            [shape(part, 3 * width, dtype=f32), shape(part, width, dtype=f32)],
            [vmem(part, hidden, dtype=f32)],
            [idx, fold.keep, fold.came],
        )
    else:
        grad_proj = grad_first[:, :width]
        grad_qkv = jnp.concatenate(
            [
                g[:, at + k * group : at + (k + 1) * group]
                for k in range(3)
                for g, at in ((grad_first, width), (grad_second, 0))
            ],
            axis=1,
        )
        local = sum(jnp.sum(g * g) for g in (small_grads, up_bias, grad_down, grad_up, grad_first, grad_second))
        grad_sq_norm = lax.psum(local, "wide")
    return (
        block_out.transpose(1, 0, 2),
        tokens_grad.transpose(1, 0, 2),
        small_grads[0],
        small_grads[1],
        grad_qkv,
        small_grads[2],
        small_grads[3],
        grad_proj,
        small_grads[4],
        small_grads[5],
        small_grads[6],
        grad_up,
        up_bias,
        grad_down,
        small_grads[7],
        grad_sq_norm,
    )


def solution(mesh):
    fast = mesh.shape["wide"] == BLOCKS and mesh.shape["narrow"] == 4
    clips = P(("wide", "narrow"), None, None)
    vector = P("wide")
    matrix = P("wide", None)
    return jax.shard_map(
        functools.partial(body, fast),
        mesh=mesh,
        in_specs=(
            clips,
            clips,
            vector,
            vector,
            matrix,
            vector,
            vector,
            matrix,
            vector,
            vector,
            vector,
            matrix,
            vector,
            matrix,
            vector,
        ),
        out_specs=(
            clips,
            clips,
            vector,
            vector,
            matrix,
            vector,
            vector,
            matrix,
            vector,
            vector,
            vector,
            matrix,
            vector,
            matrix,
            vector,
            P(),
        ),
        check_vma=False,
    )
```
